128 devices in a mesh: row: 8 (over z_lo, x), seq: 16 (over y, z_hi, core).
Axes of the slice: x: 4, y: 4, z: 4 (z_hi: 2, z_lo: 2; z = z_hi * 2 + z_lo), core: 2. Of those that a mesh axis runs over, the one named last changes fastest.
Arguments:
- mixer_input: bfloat16 [32768, 4352], P(('row', 'seq')), parts along dimension 0, may hold values from -6 to 6
- gate_input: bfloat16 [32768, 4096], P(('row', 'seq')), parts along dimension 0, may hold values from -6 to 6
- conv_forward: float32 [4, 4352], replicated, may hold values from -3 to 3
- conv_reverse: float32 [4, 4352], replicated, may hold values from -3 to 3
- step_size: float32 [64, 32768], P(None, ('row', 'seq')), parts along dimension 1, may hold values from 0 to 1, as said below
- decay_rate: float32 [512], P('row'), parts along dimension 0, may hold values from 1 to 8, as said below
- skip_scale: float32 [64], replicated, may hold values from 0.5 to 1.5
- norm_gain: float32 [4096], replicated, may hold values from 0.5 to 1.5
Outputs:
- mixer_output: bfloat16 [32768, 4096], P(('row', 'seq')), parts along dimension 0
The draws below stay inside these ranges and needn't reach their ends.
There are 8 independent parts, one for each index of `row`. The reference program is written for one: setup_inputs(seed, part) draws one part's arguments, and reference() takes and returns one part's arrays. A program takes and returns all parts, laid end to end along the dimension named above; an argument that names none is the same for every part. Nothing has to cross between parts.
Inputs may be any that keep to these rules, and one draw needn't show every extreme that they name: `step_size`: positive step sizes. `decay_rate`: positive coefficients.
All inputs are finite; a program needn't handle non-finite values.
Results may differ from the reference program's by a relative error of at most 0.007.
Values may be sent and summed in bfloat16 or wider, within the bound.
No kernel may reach another device: no remote copies, remote signals or barrier semaphores. Data moves between devices by JAX's collectives and lax.ppermute only.
A program may use at most 192 MiB of HBM per device.

```python
import math
import jax
import jax.numpy as jnp
from jax import lax

HEADS = 64
HEAD_DIM = 64
STATE = 128
WIDTH = 4
GROUP = 256
TOK_DEV = 256
INNER = 4096
E = 4352
SEQUENCE_TOKENS = 4096


def decay_plan(key, fast_share):
    head_key, pick_key = jax.random.split(key, 2)
    coefficient = jnp.exp(jax.random.uniform(head_key, (HEADS,), jnp.float32, 0.0, math.log(8.0)))
    fast = jax.random.uniform(pick_key, (HEADS,), jnp.float32) < fast_share
    target = jnp.where(fast, 1.0 / 40.0, 0.7 / SEQUENCE_TOKENS)
    return (coefficient, target)


def draw_decay_rate(key, part):
    coefficient, target = decay_plan(key, 0.5)
    return coefficient.astype(jnp.float32)


def draw_step_size(key, part):
    coefficient, target = decay_plan(key, 0.5)
    key = jax.random.fold_in(key, 7)
    block_random_key, coarse_random_key, spike_random_key = jax.random.split(key, 3)
    block_factor = jnp.exp(jax.random.uniform(block_random_key, (HEADS, SEQUENCE_TOKENS // TOK_DEV), jnp.float32, math.log(0.5), math.log(2.0)))
    factor = jnp.repeat(block_factor, TOK_DEV, axis=1)
    rough = jax.random.uniform(coarse_random_key, (HEADS, SEQUENCE_TOKENS), jnp.float32, 0.5, 1.5)
    spike_locations = jax.random.randint(spike_random_key, (3,), 0, SEQUENCE_TOKENS)
    spike_train = jnp.any(jnp.arange(SEQUENCE_TOKENS)[:, None] == spike_locations[None, :], axis=1)
    additional_term = jnp.where(spike_train, 0.25, 0.0)
    steps = (target[:, None] * factor * rough + additional_term[None, :]) / coefficient[:, None]
    return steps.astype(jnp.float32)


def steps_of(rng, extent, cuts, low, high):
    gain, own = 1.0, jax.random.fold_in(rng, 6)
    for axis_at, blocks in cuts:
        heights = jnp.exp(jax.random.uniform(jax.random.fold_in(own, axis_at), (blocks,), jnp.float32, low / len(cuts), high / len(cuts)))
        gain = gain * jnp.repeat(heights, extent[axis_at] // blocks).reshape([-1 if axis == axis_at else 1 for axis in range(len(extent))])
    return gain


def bell_draw(stream_key, extent, spread, most, cuts=(), held_as=jnp.bfloat16):
    entries = spread * jax.random.normal(stream_key, extent, jnp.float32)
    if cuts:
        entries = entries * steps_of(stream_key, extent, cuts, -0.22, 0.18)
    return jnp.clip(entries, -most, most).astype(held_as)


def setup_inputs(seed: int = 0, part: int = 0) -> dict:
    key_list = jax.random.split(jax.random.key(seed), 9)
    own_keys = jax.random.split(jax.random.fold_in(key_list[8], part), 9)
    mixer_input = bell_draw(own_keys[0], (SEQUENCE_TOKENS, E), 1.0, 6.0, ((0, 16),))
    gate_input = bell_draw(own_keys[1], (SEQUENCE_TOKENS, INNER), 1.0, 6.0, ((0, 16),))
    conv_forward = bell_draw(key_list[2], (WIDTH, E), WIDTH ** -0.5, 3.0, (), jnp.float32)
    conv_reverse = bell_draw(key_list[3], (WIDTH, E), WIDTH ** -0.5, 3.0, (), jnp.float32)
    step_size = draw_step_size(jax.random.fold_in(jax.random.fold_in(key_list[8], part), 71), part)
    decay_rate = draw_decay_rate(jax.random.fold_in(jax.random.fold_in(key_list[8], part), 71), part)
    skip_scale = jnp.clip(jax.random.uniform(key_list[6], (HEADS,), jnp.float32, 0.5, 1.5), 0.5, 1.5)
    norm_gain = jnp.clip(1.0 + 0.1 * jax.random.normal(key_list[7], (INNER,), jnp.float32), 0.5, 1.5)
    return dict(mixer_input=mixer_input, gate_input=gate_input, conv_forward=conv_forward, conv_reverse=conv_reverse, step_size=step_size, decay_rate=decay_rate, skip_scale=skip_scale, norm_gain=norm_gain)


def conv_pair(padded, conv_forward, conv_reverse, length):
    reach = conv_forward.shape[0] - 1
    ahead = jnp.zeros((length, padded.shape[1]), jnp.float32)
    behind = jnp.zeros((length, padded.shape[1]), jnp.float32)
    for kernel_tap in range(reach + 1):
        ahead = ahead + conv_forward[kernel_tap] * padded[kernel_tap:kernel_tap + length].astype(jnp.float32)
        start = 2 * reach - kernel_tap
        behind = behind + conv_reverse[kernel_tap] * padded[start:start + length].astype(jnp.float32)
    return (jax.nn.silu(ahead).astype(jnp.bfloat16), jax.nn.silu(behind).astype(jnp.bfloat16))

def split_pieces(convolved):
    length = convolved.shape[0]
    inner = HEADS * HEAD_DIM
    values = convolved[:, :inner].reshape(length, HEADS, HEAD_DIM)
    keys = convolved[:, inner:inner + STATE]
    queries = convolved[:, inner + STATE:]
    return (values, keys, queries)

def block_terms(block_values, block_keys, block_queries, block_steps, decay_rate):
    log_steps = -decay_rate[:, None] * block_steps
    cumulative = jnp.cumsum(log_steps, axis=1)
    width = block_steps.shape[1]
    position = jnp.arange(width)
    causal = position[:, None] >= position[None, :]
    segment = jnp.where(causal[None], cumulative[:, :, None] - cumulative[:, None, :], -1e+30)
    intersection = jnp.dot(block_queries, block_keys.T, preferred_element_type=jnp.float32)
    scores = (intersection[None] * jnp.exp(segment) * block_steps[:, None, :]).astype(jnp.bfloat16)
    within = jnp.einsum('hts,shp->thp', scores.astype(jnp.float32), block_values.astype(jnp.float32))
    factors = block_steps * jnp.exp(cumulative[:, -1:] - cumulative)
    weighted = (block_values.astype(jnp.float32) * factors.T[:, :, None]).astype(jnp.bfloat16)
    state = jnp.einsum('tn,thp->hpn', block_keys.astype(jnp.float32), weighted.astype(jnp.float32))
    return (within, state, cumulative)

def directed(values, keys, queries, steps, decay_rate):
    length = values.shape[0]
    block_count = length // GROUP
    value_blocks = values.reshape(block_count, GROUP, HEADS, HEAD_DIM)
    key_blocks = keys.reshape(block_count, GROUP, STATE)
    query_blocks = queries.reshape(block_count, GROUP, STATE)
    step_blocks = steps.reshape(HEADS, block_count, GROUP).transpose(1, 0, 2)

    def advance(carry, item):
        within, state, cumulative = block_terms(item[0], item[1], item[2], item[3], decay_rate)
        carried_term = jnp.einsum('tn,hpn->thp', item[2].astype(jnp.float32), carry, precision=lax.Precision.HIGHEST)
        result = within + jnp.exp(cumulative).T[:, :, None] * carried_term
        carry = jnp.exp(cumulative[:, -1])[:, None, None] * carry + state
        return (carry, result)
    start_state = jnp.zeros((HEADS, HEAD_DIM, STATE), jnp.float32)
    _, results = lax.scan(advance, start_state, (value_blocks, key_blocks, query_blocks, step_blocks))
    return results.reshape(length, HEADS, HEAD_DIM)

def reference(mixer_input, gate_input, conv_forward, conv_reverse, step_size, decay_rate, skip_scale, norm_gain):
    length = mixer_input.shape[0]
    reach = WIDTH - 1
    padded = jnp.pad(mixer_input, ((reach, reach), (0, 0)))
    ahead, behind = conv_pair(padded, conv_forward, conv_reverse, length)
    values_ahead, keys_ahead, queries_ahead = split_pieces(ahead)
    values_behind, keys_behind, queries_behind = split_pieces(behind)
    forward = directed(values_ahead, keys_ahead, queries_ahead, step_size, decay_rate)
    reverse = directed(values_behind[::-1], keys_behind[::-1], queries_behind[::-1], step_size[:, ::-1], decay_rate)[::-1]
    mixed = forward + reverse + skip_scale[None, :, None] * values_ahead.astype(jnp.float32)
    gated = mixed.reshape(length, HEADS * HEAD_DIM) * jax.nn.silu(gate_input.astype(jnp.float32))
    scale = lax.rsqrt(lax.optimization_barrier(jnp.mean(gated * gated, axis=-1, keepdims=True)) + 1e-05)
    return (gated * scale * norm_gain).astype(jnp.bfloat16)
```

```python
import functools

import jax
import jax.numpy as jnp
from jax import lax
from jax.experimental import pallas as pl
from jax.experimental.pallas import tpu as pltpu
from jax.sharding import PartitionSpec as P

HEADS = 64
HEAD_DIM = 64
STATE = 128
TOK = 256
SUB = 128
INNER = 4096
E = 4352
QUART = INNER // 4
CW = 512
HC = CW // HEAD_DIM
HALO = 16
MSG = 2 * STATE + 16
YMSG = STATE + 16
PIECES = 2
LOG2E = 1.4426950408889634
F32 = jnp.float32
BF16 = jnp.bfloat16
WF, WR, GF, GR, WV, GT = range(6)
MIB = 2**20


def dot(a, b, **kw):
    return jnp.dot(a, b, preferred_element_type=F32, **kw)


def shape(dtype, *dims):
    return jax.ShapeDtypeStruct(dims, dtype)


VMEM = pl.BlockSpec(memory_space=pltpu.VMEM)
HBM = pl.BlockSpec(memory_space=pltpu.HBM)


def vmem(dtype, *dims):
    return pltpu.VMEM(dims, dtype)


def call(kernel, name, outs, operands, params=(), scratch=(), limit=12, flops=10**8, moved=10**6, aliases=None):
    operands = [pltpu.with_memory_space_constraint(v, pltpu.VMEM) for v in operands]
    params = [pltpu.with_memory_space_constraint(v, pltpu.HBM) for v in params]
    return pl.pallas_call(
        kernel,
        name=name,
        in_specs=[VMEM] * len(operands) + [HBM] * len(params),
        out_specs=[HBM if isinstance(o, jax.ShapeDtypeStruct) else VMEM for o in outs],
        out_shape=outs,
        scratch_shapes=list(scratch),
        input_output_aliases=aliases or {},
        compiler_params=pltpu.CompilerParams(vmem_limit_bytes=limit * MIB),
        cost_estimate=pl.CostEstimate(flops=flops, bytes_accessed=moved, transcendentals=0),
    )(*operands, *params)


def place():
    at = lax.axis_index("seq")
    return at & 1, (at >> 1) & 1, at >> 2


def columns(start, width):
    return pl.ds(pl.multiple_of(start, 128), width)


def split2(x):
    hi = x.astype(BF16)
    lo = (x - hi.astype(F32)).astype(BF16)
    return hi, lo


def spread_matrix(start, width=CW):
    k = lax.broadcasted_iota(jnp.int32, (2 * HEADS, width), 0)
    col = lax.broadcasted_iota(jnp.int32, (2 * HEADS, width), 1)
    low = (k & (HEADS - 1)) * HEAD_DIM - start
    return jnp.where((col >= low) & (col < low + HEAD_DIM), 1.0, 0.0).astype(BF16)


def read_decay(rows):
    rows = rows.astype(F32)
    return rows[0:1] + rows[1:2]


def decay_rows(d):
    hi, lo = split2(d)
    none = jnp.zeros((14, d.shape[1]), F32)
    return jnp.concatenate([hi.astype(F32), lo.astype(F32), none], axis=0).astype(BF16)


def make_tables(step_t, decay, skip, table_ref, mcol_ref, mrow_ref, drow_ref):
    step = jnp.transpose(step_t)
    a = -decay * step
    row = lax.broadcasted_iota(jnp.int32, (TOK, TOK), 0)
    col = lax.broadcasted_iota(jnp.int32, (TOK, TOK), 1)
    tri = jnp.where((row >= col) & ((row >= SUB) == (col >= SUB)), 1.0, 0.0)
    cum = dot(tri, a, precision=lax.Precision.HIGHEST)
    excl = cum - a
    e0 = cum[SUB - 1 : SUB]
    e1 = cum[TOK - 1 : TOK]
    ends = jnp.concatenate([jnp.broadcast_to(e0, (SUB, HEADS)), jnp.broadcast_to(e1, (SUB, HEADS))], axis=0)
    zero = jnp.zeros_like(cum)

    def put(at, value):
        hi, lo = split2(value)
        table_ref[at] = jnp.concatenate([hi, lo], axis=1)

    put(WF, step * jnp.exp(jnp.minimum(ends - cum, zero)))
    put(WR, step * jnp.exp(excl))
    put(GF, jnp.exp(cum))
    put(GR, jnp.exp(jnp.minimum(ends - excl, zero)))
    put(WV, step * jnp.exp(-0.5 * a))
    put(GT, jnp.exp(0.5 * a))
    m = (cum - 0.5 * a) * LOG2E
    mcol_ref[...] = jnp.concatenate([m, zero], axis=1)
    mrow_ref[...] = jnp.transpose(m)
    h0, l0 = split2(jnp.exp(e0))
    h1, l1 = split2(jnp.exp(e1))
    hd, ld = split2(jnp.exp(e0 + e1))
    hs, ls = split2(skip)
    no = jnp.zeros_like(h0)
    wide = [
        jnp.concatenate([hd, no], axis=1).astype(F32),
        jnp.concatenate([no, ld], axis=1).astype(F32),
        jnp.zeros((6, 2 * HEADS), F32),
        jnp.concatenate([h0, l0], axis=1).astype(F32),
        jnp.concatenate([h1, l1], axis=1).astype(F32),
        jnp.concatenate([hs, ls], axis=1).astype(F32),
        jnp.zeros((5, 2 * HEADS), F32),
    ]
    drow_ref[...] = jnp.concatenate(wide, axis=0).astype(BF16)


def conv(x, cf, cr):
    rows = x.shape[0]
    back = pltpu.roll(x, 1, 0)
    fore = pltpu.roll(x, rows - 1, 0)
    h = cf[3:4] * x + cf[2:3] * back + pltpu.roll(cf[1:2] * x + cf[0:1] * back, 2, 0)
    g = cr[3:4] * x + cr[2:3] * fore + pltpu.roll(cr[1:2] * x + cr[0:1] * fore, rows - 2, 0)
    return h, g


def silu_of_half(h):
    return (h + h * jnp.tanh(h)).astype(BF16)


def copy_all(pairs, sems):
    copies = [pltpu.make_async_copy(src, dst, sems.at[k]) for k, (src, dst) in enumerate(pairs)]
    for copy in copies:
        copy.start()
    return copies


def quarter(k):
    c, z, y = place()
    return (c if k >= 2 else 1 - c) * 2 + (z if k & 1 else 1 - z)


def front_kernel(
    x_hbm, step_hbm, decay_hbm, skip_hbm, cf_hbm, cr_hbm,
    table_ref, mcol_ref, mrow_ref, drow_ref, x_ref, taps_ref, kq_ref, u0_ref, u2_ref,
    step_ref, decay_ref, skip_ref, cf_ref, cr_ref, sems,
):
    copies = copy_all(
        [
            (step_hbm, step_ref),
            (decay_hbm, decay_ref),
            (skip_hbm, skip_ref),
            (cf_hbm, cf_ref),
            (cr_hbm, cr_ref),
            (x_hbm, x_ref),
        ],
        sems,
    )
    for copy in copies[:3]:
        copy.wait()
    make_tables(step_ref[...], decay_ref[...], skip_ref[...], table_ref, mcol_ref, mrow_ref, drow_ref)
    for copy in copies[3:]:
        copy.wait()
    taps_ref[0:4] = cf_ref[...] * 0.5
    taps_ref[4:8] = cr_ref[...] * 0.5
    for ref, start in ((kq_ref, INNER), (u0_ref, quarter(0) * QUART), (u2_ref, quarter(2) * QUART)):

        def body(i, _):
            at = columns(start + i * 128, 128)
            cols = columns(i * 128, 128)
            h, g = conv(x_ref[:, at].astype(F32), taps_ref[0:4, at], taps_ref[4:8, at])
            ref[0, :, cols] = silu_of_half(h)
            ref[1, :, cols] = silu_of_half(g)
            return _

        lax.fori_loop(0, ref.shape[2] // 128, body, 0)


def make_front(x, step_size, decay_rate, skip_scale, cf, cr):
    return call(
        front_kernel,
        "front",
        [
            vmem(BF16, 6, TOK, 2 * HEADS),
            vmem(F32, TOK, 2 * HEADS),
            vmem(F32, HEADS, TOK),
            vmem(BF16, 16, 2 * HEADS),
            vmem(BF16, TOK, E),
            vmem(F32, 8, E),
            vmem(BF16, 2, TOK, 2 * STATE),
            vmem(BF16, 2, TOK, QUART),
            vmem(BF16, 2, TOK, QUART),
        ],
        (),
        (x, step_size, decay_rate.reshape(1, HEADS), skip_scale.reshape(1, HEADS), cf, cr),
        [
            pltpu.VMEM((HEADS, TOK), F32),
            pltpu.VMEM((1, HEADS), F32),
            pltpu.VMEM((1, HEADS), F32),
            pltpu.VMEM((4, E), F32),
            pltpu.VMEM((4, E), F32),
            pltpu.SemaphoreType.DMA((6,)),
        ],
    )


def edges(x_ref, core_ref, chip_ref, at):
    c, z, y = place()
    core, chip = core_ref[:, at].astype(F32), chip_ref[:, at].astype(F32)
    return jnp.where(c == 0, chip, core), jnp.where(c == 0, core, chip)


def repair(u_ref, x_ref, taps_ref, core_ref, chip_ref, start):
    def body(i, _):
        at = columns(start + i * 256, 256)
        cols = columns(i * 256, 256)
        prev, nxt = edges(x_ref, core_ref, chip_ref, at)
        cf, cr = taps_ref[0:4, at], taps_ref[4:8, at]
        h, _g = conv(jnp.concatenate([prev, x_ref[0:HALO, at].astype(F32)], axis=0), cf, cr)
        u_ref[0, 0:HALO, cols] = silu_of_half(h[HALO:])
        _h, g = conv(jnp.concatenate([x_ref[TOK - HALO : TOK, at].astype(F32), nxt], axis=0), cf, cr)
        u_ref[1, TOK - HALO : TOK, cols] = silu_of_half(g[:HALO])
        return _

    lax.fori_loop(0, u_ref.shape[2] // 256, body, 0)


def local_states(u_ref, kt_ref, table_ref, drow_ref, sub_ref, msg_ref, which, piece):
    spread = spread_matrix(quarter(which) * QUART + piece * CW)
    drow = dot(drow_ref[...], spread)
    d0, d1 = drow[8:9], drow[9:10]
    cols = slice(piece * CW, (piece + 1) * CW)

    def weighted(d, row, r):
        w = dot(table_ref[row, r : r + SUB], spread)
        return (u_ref[d, r : r + SUB, cols].astype(F32) * w).astype(BF16)

    f0 = dot(kt_ref[0, :, 0:SUB], weighted(0, WF, 0))
    f1 = dot(kt_ref[0, :, SUB:TOK], weighted(0, WF, SUB))
    r0 = dot(kt_ref[1, :, 0:SUB], weighted(1, WR, 0))
    r1 = dot(kt_ref[1, :, SUB:TOK], weighted(1, WR, SUB))
    fwd, rev = d1 * f0 + f1, r0 + d0 * r1
    sub_ref[0, :, cols] = f0.astype(BF16)
    sub_ref[1, :, cols] = r1.astype(BF16)
    msg_ref[0:STATE, cols] = fwd.astype(BF16)
    msg_ref[STATE : 2 * STATE, cols] = rev.astype(BF16)
    msg_ref[2 * STATE : MSG, cols] = drow.astype(BF16)
    return fwd, rev, drow


def joined(fwd, rev, drow, far_ref, chip_ref, piece):
    c, z, y = place()
    core0 = c == 0
    cols = slice(piece * CW, (piece + 1) * CW)
    dm = drow[0:1] + drow[1:2]
    do = read_decay(far_ref[2 * STATE : MSG, cols])
    one = jnp.ones_like(dm)
    am, ao = jnp.where(core0, do, one), jnp.where(core0, one, dm)
    chip_ref[0:STATE] = (am * fwd + ao * far_ref[0:STATE, cols].astype(F32)).astype(BF16)
    am, ao = jnp.where(core0, one, do), jnp.where(core0, dm, one)
    chip_ref[STATE : 2 * STATE] = (am * rev + ao * far_ref[STATE : 2 * STATE, cols].astype(F32)).astype(BF16)
    chip_ref[2 * STATE : MSG] = decay_rows(dm * do)


def first_kernel(
    kq_in, u_in, x_ref, taps_ref, core_ref, chip_ref, table_ref, drow_ref, kq_ref, u_ref, kt_ref, sub_ref, msg_ref
):
    repair(kq_ref, x_ref, taps_ref, core_ref, chip_ref, INNER)
    for d in range(2):
        kt_ref[d] = jnp.transpose(kq_ref[d, :, 0:STATE].astype(F32)).astype(BF16)
    repair(u_ref, x_ref, taps_ref, core_ref, chip_ref, quarter(0) * QUART)
    for piece in range(PIECES):
        local_states(u_ref, kt_ref, table_ref, drow_ref, sub_ref, msg_ref, 0, piece)


def partner_kernel(
    u_in, x_ref, taps_ref, core_ref, chip_ref, table_ref, drow_ref, kt_ref, far_ref, u_ref, sub_ref, msg_ref, *chip_refs
):
    repair(u_ref, x_ref, taps_ref, core_ref, chip_ref, quarter(2) * QUART)
    for piece in range(PIECES):
        state = local_states(u_ref, kt_ref, table_ref, drow_ref, sub_ref, msg_ref, 2, piece)
        joined(*state, far_ref, chip_refs[piece], piece)


def rest_kernel(
    x_ref, taps_ref, core_ref, chip_ref, table_ref, drow_ref, kt_ref, u1_ref, u3_ref, sub_ref, msg_ref
):
    for which, ref in ((1, u1_ref), (3, u3_ref)):

        def body(i, _):
            at = columns(quarter(which) * QUART + i * 128, 128)
            cols = columns(i * 128, 128)
            prev, nxt = edges(x_ref, core_ref, chip_ref, at)
            x = jnp.concatenate([prev[HALO - 8 :], x_ref[:, at].astype(F32), nxt[:8]], axis=0)
            h, g = conv(x, taps_ref[0:4, at], taps_ref[4:8, at])
            ref[0, :, cols] = silu_of_half(h[8 : TOK + 8])
            ref[1, :, cols] = silu_of_half(g[8 : TOK + 8])
            return _

        lax.fori_loop(0, QUART // 128, body, 0)
    for piece in range(PIECES):
        local_states(u1_ref, kt_ref, table_ref, drow_ref, sub_ref, msg_ref, 1, piece)


def own_kernel(u_ref, table_ref, drow_ref, kt_ref, far_ref, sub_ref, msg_ref, *chip_refs):
    for piece in range(PIECES):
        state = local_states(u_ref, kt_ref, table_ref, drow_ref, sub_ref, msg_ref, 3, piece)
        joined(*state, far_ref, chip_refs[piece], piece)


U = vmem(BF16, 2, TOK, QUART)
SUBSTATE = vmem(BF16, 2, STATE, QUART)
MESSAGE = vmem(BF16, MSG, QUART)
CHIP = [vmem(BF16, MSG, CW)] * PIECES


def group_kernel(keep_ref, got_ref, *outs):
    c, z, y = place()
    z0 = z == 0
    dm, do = read_decay(keep_ref[2 * STATE : MSG]), read_decay(got_ref[2 * STATE : MSG])
    one = jnp.ones_like(dm)
    am, ao = jnp.where(z0, do, one), jnp.where(z0, one, dm)
    fwd = (am * keep_ref[0:STATE].astype(F32) + ao * got_ref[0:STATE].astype(F32)).astype(BF16)
    am, ao = jnp.where(z0, one, do), jnp.where(z0, dm, one)
    rows = slice(STATE, 2 * STATE)
    rev = (am * keep_ref[rows].astype(F32) + ao * got_ref[rows].astype(F32)).astype(BF16)
    decay = decay_rows(dm * do)
    for k in range(1, 4):
        outs[k - 1][0:STATE] = jnp.where(y + k < 4, fwd, rev)
        outs[k - 1][STATE:YMSG] = decay


def make_group(keep, got):
    return call(group_kernel, "group", [vmem(BF16, YMSG, keep.shape[1])] * 3, (keep, got))


def entries_kernel(keep_ref, got_ref, r1_ref, r2_ref, r3_ref, mine_ref, back_ref):
    c, z, y = place()
    z0 = z == 0
    r = [ref[0:STATE].astype(F32) for ref in (r1_ref, r2_ref, r3_ref)]
    d = [read_decay(ref[STATE:YMSG]) for ref in (r1_ref, r2_ref, r3_ref)]
    zero = jnp.zeros_like(r[0])
    ef = jnp.where(y >= 3, r[2], zero)
    ef = jnp.where(y >= 2, r[1] + d[1] * ef, zero)
    ef = jnp.where(y >= 1, r[0] + d[0] * ef, zero)
    er = jnp.where(y <= 0, r[0], zero)
    er = jnp.where(y <= 1, r[1] + d[1] * er, zero)
    er = jnp.where(y <= 2, r[2] + d[2] * er, zero)
    dm, do = read_decay(keep_ref[2 * STATE : MSG]), read_decay(got_ref[2 * STATE : MSG])
    df = jnp.where(z0, dm, do)
    tf = jnp.where(z0, keep_ref[0:STATE].astype(F32), got_ref[0:STATE].astype(F32))
    second_f = df * ef + tf
    dr = jnp.where(z0, do, dm)
    rows = slice(STATE, 2 * STATE)
    tr = jnp.where(z0, got_ref[rows].astype(F32), keep_ref[rows].astype(F32))
    first_r = dr * er + tr
    mine_ref[0] = jnp.where(z0, ef, second_f).astype(BF16)
    mine_ref[1] = jnp.where(z0, first_r, er).astype(BF16)
    back_ref[0] = jnp.where(z0, second_f, ef).astype(BF16)
    back_ref[1] = jnp.where(z0, er, first_r).astype(BF16)


def make_entries(keep, got, arrived):
    return call(entries_kernel, "entries", [vmem(BF16, 2, STATE, keep.shape[1])] * 2, (keep, got, *arrived))


def within_kernel(pair, ua_ref, ub_ref, kq_ref, table_ref, mcol_ref, mrow_ref, drow_ref, gate_hbm, gain_hbm, *refs):
    if pair == 0:
        outa_ref, outb_ref, gate_ref, gain_ref, qk_ref, sems = refs
        copies = copy_all([(gate_hbm, gate_ref), (gain_hbm, gain_ref)], sems)
    else:
        outa_ref, outb_ref, qk_ref = refs
    row = lax.broadcasted_iota(jnp.int32, (SUB, SUB), 0)
    col = lax.broadcasted_iota(jnp.int32, (SUB, SUB), 1)
    low = lax.broadcasted_iota(jnp.int32, (SUB, 2 * HEAD_DIM), 1) < HEAD_DIM
    for b in range(2):
        rows = slice(b * SUB, (b + 1) * SUB)
        for d in range(2):
            keys = kq_ref[d, rows, 0:STATE]
            queries = kq_ref[d, rows, STATE : 2 * STATE]
            prod = lax.dot_general(queries, keys, (((1,), (1,)), ((), ())), preferred_element_type=F32)
            qk_ref[d, b] = jnp.where((row >= col) if d == 0 else (row <= col), prod, 0.0)

    for u_ref, out_ref, which in ((ua_ref, outa_ref, pair), (ub_ref, outb_ref, pair + 2)):

        def body(i, _):
            chunk = quarter(which) * (QUART // CW) + i
            spread = spread_matrix(chunk * CW)
            skip = dot(drow_ref[...], spread)[10:11]
            mcol = pltpu.roll(mcol_ref[...], 2 * HEADS - HC * chunk, 1)
            mrow = mrow_ref[pl.ds(pl.multiple_of(chunk * HC, HC), HC), :]
            for b in range(2):
                rows = slice(b * SUB, (b + 1) * SUB)
                wv = dot(table_ref[WV, rows], spread)
                gt = dot(table_ref[GT, rows], spread)
                for two in range(HC // 2):
                    cols = slice(two * 128, (two + 1) * 128)
                    at = columns(i * CW + two * 128, 128)
                    up = u_ref[0, rows, at].astype(F32)
                    xf = (up * wv[:, cols]).astype(BF16)
                    xb = (u_ref[1, rows, at].astype(F32) * wv[:, cols]).astype(BF16)
                    none = jnp.zeros_like(xf)
                    left, right = [], []
                    for h in range(2):
                        k = two * 2 + h
                        diff = mcol[rows, k : k + 1] - mrow[k : k + 1, rows]
                        decay = jnp.exp2(-jnp.abs(diff))
                        left += [(decay * qk_ref[0, b]).astype(BF16), (decay * qk_ref[1, b]).astype(BF16)]
                        keep = low if h == 0 else ~low
                        right += [jnp.where(keep, xf, none), jnp.where(keep, xb, none)]
                    res = dot(jnp.concatenate(left, axis=1), jnp.concatenate(right, axis=0))
                    out_ref[rows, at] = (res * gt[:, cols] + up * skip[:, cols]).astype(BF16)
            return _

        lax.fori_loop(0, QUART // CW, body, 0)
    if pair == 0:
        for copy in copies:
            copy.wait()


def make_within(pair, ua, ub, kq, table, mcol, mrow, drow, gate, gain):
    outs = [vmem(BF16, TOK, QUART)] * 2
    scratch = [pltpu.VMEM((2, 2, SUB, SUB), F32)]
    if pair == 0:
        outs += [vmem(BF16, TOK, INNER), vmem(F32, 1, INNER)]
        scratch += [pltpu.SemaphoreType.DMA((2,))]
    return call(
        functools.partial(within_kernel, pair),
        "within_a" if pair == 0 else "within_b",
        outs,
        (ua, ub, kq, table, mcol, mrow, drow),
        (gate, gain),
        scratch,
    )


def finish_part(which, piece, entry_ref, far_ref, sub_ref, within_ref, shared, gated_ref, start, square):
    kq_ref, table_ref, drow_ref, gate_ref = shared
    c, z, y = place()
    core0 = c == 0
    at = columns(quarter(which) * QUART + piece * CW, CW)
    cols = slice(piece * CW, (piece + 1) * CW)
    spread = spread_matrix(quarter(which) * QUART + piece * CW)
    drow = dot(drow_ref[...], spread)
    d0, d1 = drow[8:9], drow[9:10]
    moved = read_decay(far_ref[2 * STATE : MSG, cols])
    state = far_ref[pl.ds(pl.multiple_of((1 - c) * STATE, STATE), STATE), cols].astype(F32)
    one = jnp.ones_like(moved)
    none = jnp.zeros_like(state)
    ef = jnp.where(core0, one, moved) * entry_ref[0].astype(F32) + jnp.where(core0, none, state)
    er = jnp.where(core0, moved, one) * entry_ref[1].astype(F32) + jnp.where(core0, state, none)
    inside = [
        (ef.astype(BF16), (er * d1 + sub_ref[1, :, cols].astype(F32)).astype(BF16)),
        ((ef * d0 + sub_ref[0, :, cols].astype(F32)).astype(BF16), er.astype(BF16)),
    ]
    for b in range(2):
        rows = slice(b * SUB, (b + 1) * SUB)
        cf = dot(kq_ref[0, rows, STATE : 2 * STATE], inside[b][0])
        cr = dot(kq_ref[1, rows, STATE : 2 * STATE], inside[b][1])
        gf = dot(table_ref[GF, rows], spread)
        gr = dot(table_ref[GR, rows], spread)
        mixed = within_ref[rows, cols].astype(F32) + gf * cf + gr * cr
        half = gate_ref[rows, at].astype(F32) * 0.5
        gated = mixed * (half + half * jnp.tanh(half))
        gated_ref[rows, start : start + CW] = gated
        sq = gated * gated
        for k in range(0, CW, 128):
            part = sq[:, k : k + 128]
            square[b] = part if square[b] is None else square[b] + part


def finish_kernel(whiches, piece, last, before, *refs):
    refs = list(refs)
    parts = [[refs.pop(0) for _ in range(4)] for _ in whiches]
    shared = [refs.pop(0) for _ in range(4)]
    square = [None, None]
    if last:
        gain_ref = refs.pop(0)
        earlier = [(refs.pop(0), list(done)) for done in before]
        squares = [refs.pop(0) for _ in before]
        out_hbm, gated_ref, out_ref, sems = refs
    else:
        gated_ref, square_ref = refs
    for k, (which, part) in enumerate(zip(whiches, parts)):
        finish_part(which, piece, *part, shared, gated_ref, k * CW, square)
    if not last:
        square_ref[0:SUB] = square[0]
        square_ref[SUB:TOK] = square[1]
        return
    pieces = [(gated_ref, 0, whiches[0], piece)]
    for ref, done in earlier:
        pieces += [(ref, k * CW, which, p) for k, (which, p) in enumerate(done)]
    step = 64
    copies = []
    for b in range(2):
        total = square[b]
        for ref in squares:
            total = total + ref[b * SUB : (b + 1) * SUB]
        mean = jnp.sum(total, axis=1, keepdims=True) * (1.0 / INNER)
        scale = lax.rsqrt(mean + 1e-05)
        for r in range(0, SUB, step):
            rows = slice(b * SUB + r, b * SUB + r + step)
            for ref, start, which, p in pieces:
                at = columns(quarter(which) * QUART + p * CW, CW)
                out_ref[rows, at] = (
                    ref[rows, start : start + CW] * scale[r : r + step] * gain_ref[:, at]
                ).astype(BF16)
            copies.append(pltpu.make_async_copy(out_ref.at[rows], out_hbm.at[rows], sems.at[len(copies)]))
            copies[-1].start()
    for copy in copies:
        copy.wait()


def make_finish(whiches, piece, parts, shared, gain=None, before=()):
    last = gain is not None
    operands = [v for part in parts for v in part] + list(shared)
    scratch = []
    if last:
        operands += [gain] + [done[1][0] for done in before] + [done[1][1] for done in before]
        outs = [shape(BF16, TOK, INNER)]
        scratch = [pltpu.VMEM((TOK, CW), F32), pltpu.VMEM((TOK, INNER), BF16), pltpu.SemaphoreType.DMA((4,))]
    else:
        outs = [vmem(F32, TOK, CW * len(whiches)), vmem(F32, TOK, 128)]
    kernel = functools.partial(finish_kernel, whiches, piece, last, [done[0] for done in before])
    name = "finish_" + "".join(map(str, whiches)) + "ab"[piece]
    return call(kernel, name, outs, operands, (), scratch)


def per_device(mixer_input, gate_input, conv_forward, conv_reverse, step_size, decay_rate, skip_scale, norm_gain):
    n = lax.axis_size("seq")
    barrier = lax.optimization_barrier
    c = lax.axis_index("seq") & 1

    def send(v, perm):
        return lax.ppermute(v, "seq", perm)

    core = [(i, i ^ 1) for i in range(n)]
    zswap = [(i, i ^ 2) for i in range(n)]
    chips = [(i, i + 1) for i in range(1, n - 1, 2)] + [(i + 1, i) for i in range(1, n - 1, 2)]

    head, tail = mixer_input[:HALO], mixer_input[TOK - HALO :]
    halo_core = send(jnp.where(c == 0, tail, head), core)
    halo_chip = send(jnp.where(c == 0, head, tail), chips)
    table, mcol, mrow, drow, x, taps, kq, u0, u2 = make_front(
        mixer_input, step_size, decay_rate, skip_scale, conv_forward, conv_reverse
    )
    halo = (x, taps, halo_core, halo_chip)
    kq, u0, kt, sub0, msg0 = call(
        first_kernel,
        "states_0",
        [vmem(BF16, 2, TOK, 2 * STATE), U, vmem(BF16, 2, STATE, TOK), SUBSTATE, MESSAGE],
        (kq, u0, *halo, table, drow),
        aliases={0: 0, 1: 1},
    )
    far2 = send(msg0, core)
    u2, sub2, msg2, *zsend = call(
        partner_kernel,
        "states_2",
        [U, SUBSTATE, MESSAGE, *CHIP],
        (u2, *halo, table, drow, kt, far2),
        aliases={0: 0},
    )
    got = [send(m, zswap) for m in zsend]
    x, zsend = barrier((x, zsend))
    halo = (x, taps, halo_core, halo_chip)
    u1, u3, sub1, msg1 = call(rest_kernel, "states_1", [U, U, SUBSTATE, MESSAGE], (*halo, table, drow, kt))
    far3 = send(msg1, core)
    sub3, msg3, *keep = call(own_kernel, "states_3", [SUBSTATE, MESSAGE, *CHIP], (u3, table, drow, kt, far3))
    far0 = send(msg2, core)
    far1 = send(msg3, core)

    arrived, mine, back = [], [], []
    for p in range(PIECES):
        msgs = make_group(keep[p], got[p])
        arrived.append([send(m, [(i, (i + 4 * k) % n) for i in range(n)]) for k, m in enumerate(msgs, 1)])
    gate, gain = gate_input, norm_gain.reshape(1, INNER)
    tables = (kq, table, mcol, mrow, drow)
    u0, u2, msgs = barrier((u0, u2, msgs))
    w0, w2, gate, gain = make_within(0, u0, u2, *tables, gate, gain)
    arrived[0], w0, w2 = barrier((arrived[0], w0, w2))
    for p in range(PIECES):
        m, b = make_entries(keep[p], got[p], arrived[p])
        mine.append(m)
        back.append(b)
    entry2 = [send(b, zswap) for b in back]
    entry1 = [send(m, core) for m in mine]
    u1, u3, back = barrier((u1, u3, back))
    w1, w3 = make_within(1, u1, u3, *tables, gate_input, norm_gain.reshape(1, INNER))
    shared = (kq, table, drow, gate)
    done = []
    for p in range(PIECES):
        parts = [(mine[p], far3, sub3, w3), (entry1[p], far1, sub1, w1)]
        done.append(([(3, p), (1, p)], make_finish((3, 1), p, parts, shared)))
    entry2[0], *rest = barrier((entry2[0], *[v for d in done for v in d[1]]))
    done = [(d[0], rest[2 * k : 2 * k + 2]) for k, d in enumerate(done)]
    entry0 = [send(e, core) for e in entry2]
    parts = [(entry2[0], far2, sub2, w2), (entry0[0], far0, sub0, w0)]
    done.append(([(2, 0), (0, 0)], make_finish((2, 0), 0, parts, shared)))
    done.append(([(2, 1)], make_finish((2,), 1, [(entry2[1], far2, sub2, w2)], shared)))
    (out,) = make_finish((0,), 1, [(entry0[1], far0, sub0, w0)], shared, gain, done)
    return out


def solution(mesh):
    in_specs = (
        P(("row", "seq"), None),
        P(("row", "seq"), None),
        P(),
        P(),
        P(None, ("row", "seq")),
        P("row"),
        P(),
        P(),
    )
    out_specs = P(("row", "seq"), None)
    return jax.shard_map(per_device, mesh=mesh, in_specs=in_specs, out_specs=out_specs, check_vma=False)
```

```python
import functools

import jax
import jax.numpy as jnp
from jax import lax
from jax.experimental import pallas as pl
from jax.experimental.pallas import tpu as pltpu
from jax.sharding import PartitionSpec as P

HEADS = 64
HEAD_DIM = 64
STATE = 128
TOK = 256
SUB = 128
INNER = 4096
E = 4352
QUART = INNER // 4
CW = 512
HC = CW // HEAD_DIM
HALO = 16
MSG = 2 * STATE + 16
YMSG = STATE + 16
PIECES = 2
LOG2E = 1.4426950408889634
F32 = jnp.float32
BF16 = jnp.bfloat16
WF, WR, GF, GR, WV, GT = range(6)
MIB = 2**20


def dot(a, b, **kw):
    return jnp.dot(a, b, preferred_element_type=F32, **kw)


def shape(dtype, *dims):
    return jax.ShapeDtypeStruct(dims, dtype)


VMEM = pl.BlockSpec(memory_space=pltpu.VMEM)
HBM = pl.BlockSpec(memory_space=pltpu.HBM)


def vmem(dtype, *dims):
    return pltpu.VMEM(dims, dtype)


def call(kernel, name, outs, operands, params=(), scratch=(), limit=12, us=1.0, aliases=None):
    operands = [pltpu.with_memory_space_constraint(v, pltpu.VMEM) for v in operands]
    params = [pltpu.with_memory_space_constraint(v, pltpu.HBM) for v in params]
    return pl.pallas_call(
        kernel,
        name=name,
        in_specs=[VMEM] * len(operands) + [HBM] * len(params),
        out_specs=[HBM if isinstance(o, jax.ShapeDtypeStruct) else VMEM for o in outs],
        out_shape=outs,
        scratch_shapes=list(scratch),
        input_output_aliases=aliases or {},
        compiler_params=pltpu.CompilerParams(vmem_limit_bytes=limit * MIB),
        cost_estimate=pl.CostEstimate(flops=int(us * 1e8), bytes_accessed=int(us * 3e5), transcendentals=0),
    )(*operands, *params)


def place():
    at = lax.axis_index("seq")
    return at & 1, (at >> 1) & 1, at >> 2


def columns(start, width):
    return pl.ds(pl.multiple_of(start, 128), width)


def split2(x):
    hi = x.astype(BF16)
    lo = (x - hi.astype(F32)).astype(BF16)
    return hi, lo


def spread_matrix(start, width=CW):
    k = lax.broadcasted_iota(jnp.int32, (2 * HEADS, width), 0)
    col = lax.broadcasted_iota(jnp.int32, (2 * HEADS, width), 1)
    low = (k & (HEADS - 1)) * HEAD_DIM - start
    return jnp.where((col >= low) & (col < low + HEAD_DIM), 1.0, 0.0).astype(BF16)


def read_decay(rows):
    rows = rows.astype(F32)
    return rows[0:1] + rows[1:2]


def decay_rows(d):
    hi, lo = split2(d)
    none = jnp.zeros((14, d.shape[1]), F32)
    return jnp.concatenate([hi.astype(F32), lo.astype(F32), none], axis=0).astype(BF16)


def make_tables(step_t, decay, skip, table_ref, mcol_ref, mrow_ref, drow_ref):
    step = jnp.transpose(step_t)
    a = -decay * step
    row = lax.broadcasted_iota(jnp.int32, (TOK, TOK), 0)
    col = lax.broadcasted_iota(jnp.int32, (TOK, TOK), 1)
    tri = jnp.where((row >= col) & ((row >= SUB) == (col >= SUB)), 1.0, 0.0)
    cum = dot(tri, a, precision=lax.Precision.HIGHEST)
    excl = cum - a
    e0 = cum[SUB - 1 : SUB]
    e1 = cum[TOK - 1 : TOK]
    ends = jnp.concatenate([jnp.broadcast_to(e0, (SUB, HEADS)), jnp.broadcast_to(e1, (SUB, HEADS))], axis=0)
    zero = jnp.zeros_like(cum)

    def put(at, value):
        hi, lo = split2(value)
        table_ref[at] = jnp.concatenate([hi, lo], axis=1)

    put(WF, step * jnp.exp(jnp.minimum(ends - cum, zero)))
    put(WR, step * jnp.exp(excl))
    put(GF, jnp.exp(cum))
    put(GR, jnp.exp(jnp.minimum(ends - excl, zero)))
    put(WV, step * jnp.exp(-0.5 * a))
    put(GT, jnp.exp(0.5 * a))
    m = (cum - 0.5 * a) * LOG2E
    mcol_ref[...] = jnp.concatenate([m, zero], axis=1)
    mrow_ref[...] = jnp.transpose(m)
    h0, l0 = split2(jnp.exp(e0))
    h1, l1 = split2(jnp.exp(e1))
    hd, ld = split2(jnp.exp(e0 + e1))
    hs, ls = split2(skip)
    no = jnp.zeros_like(h0)
    wide = [
        jnp.concatenate([hd, no], axis=1).astype(F32),
        jnp.concatenate([no, ld], axis=1).astype(F32),
        jnp.zeros((6, 2 * HEADS), F32),
        jnp.concatenate([h0, l0], axis=1).astype(F32),
        jnp.concatenate([h1, l1], axis=1).astype(F32),
        jnp.concatenate([hs, ls], axis=1).astype(F32),
        jnp.zeros((5, 2 * HEADS), F32),
    ]
    drow_ref[...] = jnp.concatenate(wide, axis=0).astype(BF16)


def conv(x, cf, cr):
    rows = x.shape[0]
    back = pltpu.roll(x, 1, 0)
    fore = pltpu.roll(x, rows - 1, 0)
    h = cf[3:4] * x + cf[2:3] * back + pltpu.roll(cf[1:2] * x + cf[0:1] * back, 2, 0)
    g = cr[3:4] * x + cr[2:3] * fore + pltpu.roll(cr[1:2] * x + cr[0:1] * fore, rows - 2, 0)
    return h, g


def silu_of_half(h):
    return (h + h * jnp.tanh(h)).astype(BF16)


def copy_all(pairs, sems):
    copies = [pltpu.make_async_copy(src, dst, sems.at[k]) for k, (src, dst) in enumerate(pairs)]
    for copy in copies:
        copy.start()
    return copies


def quarter(k):
    c, z, y = place()
    return (c if k >= 2 else 1 - c) * 2 + (z if k & 1 else 1 - z)


def conv_inside(x_ref, taps_ref, u_ref, start):
    def body(i, _):
        at = columns(start + i * 128, 128)
        cols = columns(i * 128, 128)
        h, g = conv(x_ref[:, at].astype(F32), taps_ref[0:4, at], taps_ref[4:8, at])
        u_ref[0, :, cols] = silu_of_half(h)
        u_ref[1, :, cols] = silu_of_half(g)
        return _

    lax.fori_loop(0, u_ref.shape[2] // 128, body, 0)


def front_kernel(
    after_ref, x_hbm, step_hbm, decay_hbm, skip_hbm, cf_hbm, cr_hbm,
    x_ref, table_ref, mcol_ref, mrow_ref, drow_ref, taps_ref, kq_ref, u0_ref,
    step_ref, decay_ref, skip_ref, cf_ref, cr_ref, sems,
):
    copies = copy_all(
        [
            (step_hbm, step_ref),
            (decay_hbm, decay_ref),
            (skip_hbm, skip_ref),
            (x_hbm, x_ref),
            (cf_hbm, cf_ref),
            (cr_hbm, cr_ref),
        ],
        sems,
    )
    for copy in copies[:3]:
        copy.wait()
    make_tables(step_ref[...], decay_ref[...], skip_ref[...], table_ref, mcol_ref, mrow_ref, drow_ref)
    for copy in copies[3:]:
        copy.wait()
    taps_ref[0:4] = cf_ref[...] * 0.5
    taps_ref[4:8] = cr_ref[...] * 0.5
    conv_inside(x_ref, taps_ref, kq_ref, INNER)
    conv_inside(x_ref, taps_ref, u0_ref, quarter(0) * QUART)


def edge_kernel(x_hbm, to_core_ref, to_chip_ref, sems):
    c, z, y = place()
    first, end = x_hbm.at[0:HALO], x_hbm.at[TOK - HALO : TOK]

    @pl.when(c == 0)
    def _():
        for copy in copy_all([(end, to_core_ref), (first, to_chip_ref)], sems):
            copy.wait()

    @pl.when(c == 1)
    def _():
        for copy in copy_all([(first, to_core_ref), (end, to_chip_ref)], sems):
            copy.wait()


def make_front(after, x, step_size, decay_rate, skip_scale, cf, cr):
    return call(
        front_kernel,
        "front",
        [
            vmem(BF16, TOK, E),
            vmem(BF16, 6, TOK, 2 * HEADS),
            vmem(F32, TOK, 2 * HEADS),
            vmem(F32, HEADS, TOK),
            vmem(BF16, 16, 2 * HEADS),
            vmem(F32, 8, E),
            vmem(BF16, 2, TOK, 2 * STATE),
            vmem(BF16, 2, TOK, QUART),
        ],
        (after,),
        (x, step_size, decay_rate.reshape(1, HEADS), skip_scale.reshape(1, HEADS), cf, cr),
        [
            pltpu.VMEM((HEADS, TOK), F32),
            pltpu.VMEM((1, HEADS), F32),
            pltpu.VMEM((1, HEADS), F32),
            pltpu.VMEM((4, E), F32),
            pltpu.VMEM((4, E), F32),
            pltpu.SemaphoreType.DMA((6,)),
        ],
    )


def conv_kernel(x_ref, taps_ref, u1_ref):
    conv_inside(x_ref, taps_ref, u1_ref, quarter(1) * QUART)


def edges(x_ref, core_ref, chip_ref, at):
    c, z, y = place()
    core, chip = core_ref[:, at].astype(F32), chip_ref[:, at].astype(F32)
    return jnp.where(c == 0, chip, core), jnp.where(c == 0, core, chip)


def repair(u_ref, x_ref, taps_ref, core_ref, chip_ref, start):
    def body(i, _):
        at = columns(start + i * 256, 256)
        cols = columns(i * 256, 256)
        prev, nxt = edges(x_ref, core_ref, chip_ref, at)
        cf, cr = taps_ref[0:4, at], taps_ref[4:8, at]
        h, _g = conv(jnp.concatenate([prev, x_ref[0:HALO, at].astype(F32)], axis=0), cf, cr)
        u_ref[0, 0:HALO, cols] = silu_of_half(h[HALO:])
        _h, g = conv(jnp.concatenate([x_ref[TOK - HALO : TOK, at].astype(F32), nxt], axis=0), cf, cr)
        u_ref[1, TOK - HALO : TOK, cols] = silu_of_half(g[:HALO])
        return _

    lax.fori_loop(0, u_ref.shape[2] // 256, body, 0)


BASE = {(which, piece): (which % 2) * QUART + piece * CW for which in range(4) for piece in range(PIECES)}


def local_states(u_ref, kt_ref, table_ref, drow_ref, sub_ref, msg_ref, which, piece, base):
    spread = spread_matrix(quarter(which) * QUART + piece * CW)
    drow = dot(drow_ref[...], spread)
    d0, d1 = drow[8:9], drow[9:10]
    cols = slice(piece * CW, (piece + 1) * CW)

    def weighted(d, row, r):
        w = dot(table_ref[row, r : r + SUB], spread)
        return (u_ref[d, r : r + SUB, cols].astype(F32) * w).astype(BF16)

    f0 = dot(kt_ref[0, :, 0:SUB], weighted(0, WF, 0))
    f1 = dot(kt_ref[0, :, SUB:TOK], weighted(0, WF, SUB))
    r0 = dot(kt_ref[1, :, 0:SUB], weighted(1, WR, 0))
    r1 = dot(kt_ref[1, :, SUB:TOK], weighted(1, WR, SUB))
    fwd, rev = d1 * f0 + f1, r0 + d0 * r1
    cols = slice(base, base + CW)
    sub_ref[0, :, cols] = f0.astype(BF16)
    sub_ref[1, :, cols] = r1.astype(BF16)
    msg_ref[0:STATE, cols] = fwd.astype(BF16)
    msg_ref[STATE : 2 * STATE, cols] = rev.astype(BF16)
    msg_ref[2 * STATE : MSG, cols] = drow.astype(BF16)
    return fwd, rev, drow


def joined(fwd, rev, drow, far_ref, chip_ref, base):
    c, z, y = place()
    core0 = c == 0
    cols = slice(base, base + CW)
    dm = drow[0:1] + drow[1:2]
    do = read_decay(far_ref[2 * STATE : MSG, cols])
    one = jnp.ones_like(dm)
    am, ao = jnp.where(core0, do, one), jnp.where(core0, one, dm)
    chip_ref[0:STATE] = (am * fwd + ao * far_ref[0:STATE, cols].astype(F32)).astype(BF16)
    am, ao = jnp.where(core0, one, do), jnp.where(core0, dm, one)
    chip_ref[STATE : 2 * STATE] = (am * rev + ao * far_ref[STATE : 2 * STATE, cols].astype(F32)).astype(BF16)
    chip_ref[2 * STATE : MSG] = decay_rows(dm * do)


def far_kernel(
    kq_in, u0_in, u1_in, x_ref, taps_ref, core_ref, chip_ref, table_ref, drow_ref,
    kq_ref, u0_ref, u1_ref, kt_ref, sub_ref, msg_ref,
):
    repair(kq_ref, x_ref, taps_ref, core_ref, chip_ref, INNER)
    for d in range(2):
        kt_ref[d] = jnp.transpose(kq_ref[d, :, 0:STATE].astype(F32)).astype(BF16)
    for which, u_ref in ((0, u0_ref), (1, u1_ref)):
        repair(u_ref, x_ref, taps_ref, core_ref, chip_ref, quarter(which) * QUART)
        for piece in range(PIECES):
            local_states(u_ref, kt_ref, table_ref, drow_ref, sub_ref, msg_ref, which, piece, BASE[which, piece])


def partner_kernel(u_ref, table_ref, drow_ref, kt_ref, far_ref, sub_ref, msg_ref, zsend_ref):
    state = local_states(u_ref, kt_ref, table_ref, drow_ref, sub_ref, msg_ref, 2, 0, 0)
    joined(*state, far_ref, zsend_ref, BASE[2, 0])


def conv_own_kernel(which, x_ref, taps_ref, core_ref, chip_ref, after_ref, u_ref):
    def body(i, _):
        at = columns(quarter(which) * QUART + i * 128, 128)
        cols = columns(i * 128, 128)
        prev, nxt = edges(x_ref, core_ref, chip_ref, at)
        x = jnp.concatenate([prev[HALO - 8 :], x_ref[:, at].astype(F32), nxt[:8]], axis=0)
        h, g = conv(x, taps_ref[0:4, at], taps_ref[4:8, at])
        u_ref[0, :, cols] = silu_of_half(h[8 : TOK + 8])
        u_ref[1, :, cols] = silu_of_half(g[8 : TOK + 8])
        return _

    lax.fori_loop(0, QUART // 128, body, 0)


def own_kernel(
    u2_ref, u3_ref, table_ref, drow_ref, kt_ref, far_ref, sub_in, msg_in,
    sub_ref, msg_ref, zsend_ref, keep0_ref, keep1_ref,
):
    sub_ref[:, :, 0:CW] = sub_in[...]
    msg_ref[:, 0:CW] = msg_in[...]
    todo = [(u2_ref, 2, 1, zsend_ref), (u3_ref, 3, 0, keep0_ref), (u3_ref, 3, 1, keep1_ref)]
    for u_ref, which, piece, chip_ref in todo:
        base = BASE[which, piece]
        state = local_states(u_ref, kt_ref, table_ref, drow_ref, sub_ref, msg_ref, which, piece, base)
        joined(*state, far_ref, chip_ref, base)


U = vmem(BF16, 2, TOK, QUART)
KEYS = vmem(BF16, 2, TOK, 2 * STATE)
CHIP = vmem(BF16, MSG, CW)


def states_out(pieces):
    return [vmem(BF16, 2, STATE, pieces * CW), vmem(BF16, MSG, pieces * CW)]


def group(keep_ref, got_ref, outs):
    c, z, y = place()
    z0 = z == 0
    dm, do = read_decay(keep_ref[2 * STATE : MSG]), read_decay(got_ref[2 * STATE : MSG])
    one = jnp.ones_like(dm)
    am, ao = jnp.where(z0, do, one), jnp.where(z0, one, dm)
    fwd = (am * keep_ref[0:STATE].astype(F32) + ao * got_ref[0:STATE].astype(F32)).astype(BF16)
    am, ao = jnp.where(z0, one, do), jnp.where(z0, dm, one)
    rows = slice(STATE, 2 * STATE)
    rev = (am * keep_ref[rows].astype(F32) + ao * got_ref[rows].astype(F32)).astype(BF16)
    decay = decay_rows(dm * do)
    for k in range(1, 4):
        outs[k - 1][0:STATE] = jnp.where(y + k < 4, fwd, rev)
        outs[k - 1][STATE:YMSG] = decay


def entries(keep_ref, got_ref, r1_ref, r2_ref, r3_ref, mine_ref, back_ref):
    c, z, y = place()
    z0 = z == 0
    r = [ref[0:STATE].astype(F32) for ref in (r1_ref, r2_ref, r3_ref)]
    d = [read_decay(ref[STATE:YMSG]) for ref in (r1_ref, r2_ref, r3_ref)]
    zero = jnp.zeros_like(r[0])
    ef = jnp.where(y >= 3, r[2], zero)
    ef = jnp.where(y >= 2, r[1] + d[1] * ef, zero)
    ef = jnp.where(y >= 1, r[0] + d[0] * ef, zero)
    er = jnp.where(y <= 0, r[0], zero)
    er = jnp.where(y <= 1, r[1] + d[1] * er, zero)
    er = jnp.where(y <= 2, r[2] + d[2] * er, zero)
    dm, do = read_decay(keep_ref[2 * STATE : MSG]), read_decay(got_ref[2 * STATE : MSG])
    df = jnp.where(z0, dm, do)
    tf = jnp.where(z0, keep_ref[0:STATE].astype(F32), got_ref[0:STATE].astype(F32))
    second_f = df * ef + tf
    dr = jnp.where(z0, do, dm)
    rows = slice(STATE, 2 * STATE)
    tr = jnp.where(z0, got_ref[rows].astype(F32), keep_ref[rows].astype(F32))
    first_r = dr * er + tr
    mine_ref[0] = jnp.where(z0, ef, second_f).astype(BF16)
    mine_ref[1] = jnp.where(z0, first_r, er).astype(BF16)
    back_ref[0] = jnp.where(z0, second_f, ef).astype(BF16)
    back_ref[1] = jnp.where(z0, er, first_r).astype(BF16)


def second_phase_kernel(keep_ref, got_ref, zsend_ref, after_ref, zsend_out, *outs):
    group(keep_ref, got_ref, outs)
    zsend_out[...] = zsend_ref[...]


def third_phase_kernel(
    keep0_ref, got0_ref, r1_ref, r2_ref, r3_ref, keep1_ref, got1_ref, after_ref, mine_ref, back_ref, *outs
):
    entries(keep0_ref, got0_ref, r1_ref, r2_ref, r3_ref, mine_ref, back_ref)
    group(keep1_ref, got1_ref, outs)


def fourth_phase_kernel(
    keep_ref, got_ref, r1_ref, r2_ref, r3_ref, mine0_ref, back0_ref, after_ref, mine_ref, back_ref, near_ref
):
    entries(keep_ref, got_ref, r1_ref, r2_ref, r3_ref, mine_ref, back_ref)
    near_ref[0] = mine0_ref[...]
    near_ref[1] = mine_ref[...]
    near_ref[2] = back0_ref[...]


def fifth_phase_kernel(back_ref, after0_ref, after1_ref, after2_ref, out_ref):
    out_ref[...] = back_ref[...]


def within_kernel(which, u_ref, kq_ref, table_ref, mcol_ref, mrow_ref, drow_ref, after_ref, *refs):
    copies = []
    if which == 0:
        gate_hbm, gain_hbm, out_ref, gate_ref, gain_ref, qk_ref, sems = refs
        copies = copy_all([(gate_hbm, gate_ref), (gain_hbm, gain_ref)], sems)
    else:
        out_ref, qk_ref = refs
    row = lax.broadcasted_iota(jnp.int32, (SUB, SUB), 0)
    col = lax.broadcasted_iota(jnp.int32, (SUB, SUB), 1)
    low = lax.broadcasted_iota(jnp.int32, (SUB, 2 * HEAD_DIM), 1) < HEAD_DIM
    for b in range(2):
        rows = slice(b * SUB, (b + 1) * SUB)
        for d in range(2):
            keys = kq_ref[d, rows, 0:STATE]
            queries = kq_ref[d, rows, STATE : 2 * STATE]
            prod = lax.dot_general(queries, keys, (((1,), (1,)), ((), ())), preferred_element_type=F32)
            qk_ref[d, b] = jnp.where((row >= col) if d == 0 else (row <= col), prod, 0.0)

    def body(i, _):
        chunk = quarter(which) * (QUART // CW) + i
        spread = spread_matrix(chunk * CW)
        skip = dot(drow_ref[...], spread)[10:11]
        mcol = pltpu.roll(mcol_ref[...], 2 * HEADS - HC * chunk, 1)
        mrow = mrow_ref[pl.ds(pl.multiple_of(chunk * HC, HC), HC), :]
        for b in range(2):
            rows = slice(b * SUB, (b + 1) * SUB)
            wv = dot(table_ref[WV, rows], spread)
            gt = dot(table_ref[GT, rows], spread)
            for two in range(HC // 2):
                cols = slice(two * 128, (two + 1) * 128)
                at = columns(i * CW + two * 128, 128)
                up = u_ref[0, rows, at].astype(F32)
                xf = (up * wv[:, cols]).astype(BF16)
                xb = (u_ref[1, rows, at].astype(F32) * wv[:, cols]).astype(BF16)
                none = jnp.zeros_like(xf)
                left, right = [], []
                for h in range(2):
                    k = two * 2 + h
                    diff = mcol[rows, k : k + 1] - mrow[k : k + 1, rows]
                    decay = jnp.exp2(-jnp.abs(diff))
                    left += [(decay * qk_ref[0, b]).astype(BF16), (decay * qk_ref[1, b]).astype(BF16)]
                    keep = low if h == 0 else ~low
                    right += [jnp.where(keep, xf, none), jnp.where(keep, xb, none)]
                res = dot(jnp.concatenate(left, axis=1), jnp.concatenate(right, axis=0))
                out_ref[rows, at] = (res * gt[:, cols] + up * skip[:, cols]).astype(BF16)
        return _

    lax.fori_loop(0, QUART // CW, body, 0)
    for copy in copies:
        copy.wait()


def make_within(which, u, kq, table, mcol, mrow, drow, after, params=()):
    outs = [vmem(BF16, TOK, QUART)]
    scratch = [pltpu.VMEM((2, 2, SUB, SUB), F32)]
    if params:
        outs += [vmem(BF16, TOK, INNER), vmem(F32, 1, INNER)]
        scratch += [pltpu.SemaphoreType.DMA((2,))]
    operands = (u, kq, table, mcol, mrow, drow, after)
    return call(functools.partial(within_kernel, which), f"within_{which}", outs, operands, params, scratch)


def finish_part(which, piece, entry, far_ref, sub_ref, within_ref, shared, gated_ref, start, square):
    kq_ref, table_ref, drow_ref, gate_ref = shared
    c, z, y = place()
    core0 = c == 0
    at = columns(quarter(which) * QUART + piece * CW, CW)
    cols = slice(piece * CW, (piece + 1) * CW)
    spread = spread_matrix(quarter(which) * QUART + piece * CW)
    drow = dot(drow_ref[...], spread)
    d0, d1 = drow[8:9], drow[9:10]
    there = slice(BASE[which, piece], BASE[which, piece] + CW)
    moved = read_decay(far_ref[2 * STATE : MSG, there])
    state = far_ref[pl.ds(pl.multiple_of((1 - c) * STATE, STATE), STATE), there].astype(F32)
    one = jnp.ones_like(moved)
    none = jnp.zeros_like(state)
    ef = jnp.where(core0, one, moved) * entry[0].astype(F32) + jnp.where(core0, none, state)
    er = jnp.where(core0, moved, one) * entry[1].astype(F32) + jnp.where(core0, state, none)
    inside = [
        (ef.astype(BF16), (er * d1 + sub_ref[1, :, there].astype(F32)).astype(BF16)),
        ((ef * d0 + sub_ref[0, :, there].astype(F32)).astype(BF16), er.astype(BF16)),
    ]
    for b in range(2):
        rows = slice(b * SUB, (b + 1) * SUB)
        cf = dot(kq_ref[0, rows, STATE : 2 * STATE], inside[b][0])
        cr = dot(kq_ref[1, rows, STATE : 2 * STATE], inside[b][1])
        gf = dot(table_ref[GF, rows], spread)
        gr = dot(table_ref[GR, rows], spread)
        mixed = within_ref[rows, cols].astype(F32) + gf * cf + gr * cr
        half = gate_ref[rows, at].astype(F32) * 0.5
        gated = mixed * (half + half * jnp.tanh(half))
        gated_ref[rows, start : start + CW] = gated
        sq = gated * gated
        for k in range(0, CW, 128):
            part = sq[:, k : k + 128]
            square[b] = part if square[b] is None else square[b] + part


NEAR = {(1, 0): 0, (1, 1): 1, (0, 0): 2}


def finish_kernel(whiches, piece, last, before, *refs):
    refs = list(refs)
    parts = [[refs.pop(0) for _ in range(4)] for _ in whiches]
    shared = [refs.pop(0) for _ in range(4)]
    square = [None, None]
    if last:
        gain_ref = refs.pop(0)
        earlier = [(refs.pop(0), list(done)) for done in before]
        squares = [refs.pop(0) for _ in before]
        out_hbm, gated_ref, out_ref, sems = refs
    else:
        gated_ref, square_ref = refs
    for k, (which, part) in enumerate(zip(whiches, parts)):
        entry_ref, *part = part
        entry = entry_ref if len(entry_ref.shape) == 3 else entry_ref.at[NEAR[which, piece]]
        finish_part(which, piece, entry, *part, shared, gated_ref, k * CW, square)
    if not last:
        square_ref[0:SUB] = square[0]
        square_ref[SUB:TOK] = square[1]
        return
    pieces = [(gated_ref, 0, whiches[0], piece)]
    for ref, done in earlier:
        pieces += [(ref, k * CW, which, p) for k, (which, p) in enumerate(done)]
    step = 64
    copies = []
    for b in range(2):
        total = square[b]
        for ref in squares:
            total = total + ref[b * SUB : (b + 1) * SUB]
        mean = jnp.sum(total, axis=1, keepdims=True) * (1.0 / INNER)
        scale = lax.rsqrt(mean + 1e-05)
        for r in range(0, SUB, step):
            rows = slice(b * SUB + r, b * SUB + r + step)
            for ref, start, which, p in pieces:
                at = columns(quarter(which) * QUART + p * CW, CW)
                out_ref[rows, at] = (
                    ref[rows, start : start + CW] * scale[r : r + step] * gain_ref[:, at]
                ).astype(BF16)
            copies.append(pltpu.make_async_copy(out_ref.at[rows], out_hbm.at[rows], sems.at[len(copies)]))
            copies[-1].start()
    for copy in copies:
        copy.wait()


def make_finish(whiches, piece, parts, shared, gain=None, before=()):
    last = gain is not None
    operands = [v for part in parts for v in part] + list(shared)
    scratch = []
    if last:
        operands += [gain] + [done[1][0] for done in before] + [done[1][1] for done in before]
        outs = [shape(BF16, TOK, INNER)]
        scratch = [pltpu.VMEM((TOK, CW), F32), pltpu.VMEM((TOK, INNER), BF16), pltpu.SemaphoreType.DMA((4,))]
    else:
        outs = [vmem(F32, TOK, CW * len(whiches)), vmem(F32, TOK, 128)]
    kernel = functools.partial(finish_kernel, whiches, piece, last, [done[0] for done in before])
    name = "finish_" + "".join(map(str, whiches)) + "ab"[piece]
    return call(kernel, name, outs, operands, (), scratch)


def per_device(mixer_input, gate_input, conv_forward, conv_reverse, step_size, decay_rate, skip_scale, norm_gain):
    n = lax.axis_size("seq")

    def send(v, perm):
        return lax.ppermute(v, "seq", perm)

    core = [(i, i ^ 1) for i in range(n)]
    zswap = [(i, i ^ 2) for i in range(n)]
    chips = [(i, i + 1) for i in range(1, n - 1, 2)] + [(i + 1, i) for i in range(1, n - 1, 2)]

    def along_y(msgs):
        return [send(m, [(i, (i + 4 * k) % n) for i in range(n)]) for k, m in enumerate(msgs, 1)]

    edge = vmem(BF16, HALO, E)
    to_core, to_chip = call(
        edge_kernel, "edges", [edge, edge], (), (mixer_input,), [pltpu.SemaphoreType.DMA((2,))]
    )
    x, table, mcol, mrow, drow, taps, kq, u0 = make_front(
        to_core, mixer_input, step_size, decay_rate, skip_scale, conv_forward, conv_reverse
    )
    halo = (x, taps, send(to_core, core), send(to_chip, chips))
    (u1,) = call(conv_kernel, "conv", [U], (x, taps))
    kq, u0, u1, kt, sub_far, msg = call(
        far_kernel,
        "states_far",
        [KEYS, U, U, vmem(BF16, 2, STATE, TOK), *states_out(4)],
        (kq, u0, u1, *halo, table, drow),
        aliases={0: 0, 1: 1, 2: 2},
    )
    far = send(msg, core)
    (u2,) = call(functools.partial(conv_own_kernel, 2), "conv_2", [U], (*halo, msg))
    sub_own, msg, zsend0 = call(
        partner_kernel, "states_partner", [*states_out(1), CHIP], (u2, table, drow, kt, far)
    )
    got0 = send(zsend0, zswap)
    (u3,) = call(functools.partial(conv_own_kernel, 3), "conv_3", [U], (*halo, zsend0))
    sub_own, msg, zsend1, keep0, keep1 = call(
        own_kernel,
        "states_own",
        [*states_out(4), CHIP, CHIP, CHIP],
        (u2, u3, table, drow, kt, far, sub_own, msg),
    )
    near = send(msg, core)
    tables = (kq, table, mcol, mrow, drow)
    w0, gate, gain = make_within(0, u0, *tables, zsend0, (gate_input, norm_gain.reshape(1, INNER)))
    shared = (kq, table, drow, gate)

    yout = [vmem(BF16, YMSG, CW)] * 3
    entry = vmem(BF16, 2, STATE, CW)
    zsend1, *msgs = call(second_phase_kernel, "second_phase", [CHIP, *yout], (keep0, got0, zsend1, w0))
    got1 = send(zsend1, zswap)
    arrived = along_y(msgs)
    (w2,) = make_within(2, u2, *tables, msgs[0])

    mine0, back0, *msgs = call(
        third_phase_kernel, "third_phase", [entry, entry, *yout], (keep0, got0, *arrived, keep1, got1, w2)
    )
    back0 = send(back0, zswap)
    arrived = along_y(msgs)
    (w3,) = make_within(3, u3, *tables, msgs[0])

    mine1, back1, entries = call(
        fourth_phase_kernel,
        "fourth_phase",
        [entry, entry, vmem(BF16, 3, 2, STATE, CW)],
        (keep1, got1, *arrived, mine0, back0, w3),
    )
    back1 = send(back1, zswap)
    entries = send(entries, core)
    (w1,) = make_within(1, u1, *tables, mine1)
    inside = (w0, w1, w2, w3)
    done = []

    def finish(p, *todo, **kw):
        whiches = tuple(q for q, e in todo)
        parts = [(e, far if q >= 2 else near, sub_own if q >= 2 else sub_far, inside[q]) for q, e in todo]
        out = make_finish(whiches, p, parts, shared, **kw)
        done.append(([(q, p) for q in whiches], out))
        return out

    finish(0, (2, back0), (0, entries))
    finish(0, (3, mine0), (1, entries))
    finish(1, (3, mine1), (1, entries))
    (back1,) = call(fifth_phase_kernel, "fifth_phase", [entry], (back1, *[d[1][1] for d in done]))
    entry0 = send(back1, core)
    finish(1, (2, back1))
    (out,) = finish(1, (0, entry0), gain=gain, before=tuple(done))
    return out


def solution(mesh):
    in_specs = (
        P(("row", "seq"), None),
        P(("row", "seq"), None),
        P(),
        P(),
        P(None, ("row", "seq")),
        P("row"),
        P(),
        P(),
    )
    out_specs = P(("row", "seq"), None)
    return jax.shard_map(per_device, mesh=mesh, in_specs=in_specs, out_specs=out_specs, check_vma=False)
```

```python
import functools

import jax
import jax.numpy as jnp
from jax import lax
from jax.experimental import pallas as pl
from jax.experimental.pallas import tpu as pltpu
from jax.sharding import PartitionSpec as P

HEADS = 64
HEAD_DIM = 64
STATE = 128
TOK = 256
SUB = 128
INNER = 4096
E = 4352
HALF = INNER // 2
QUART = INNER // 4
WIDE = HALF + 2 * STATE
STEPS = 256
CW = 512
HC = CW // HEAD_DIM
HALO = 16
MSG = 2 * STATE + 16
YMSG = STATE + 16
LOG2E = 1.4426950408889634
F32 = jnp.float32
BF16 = jnp.bfloat16
WF, WR, GF, GR, WV, GT = range(6)
MIB = 2**20


def dot(a, b, **kw):
    return jnp.dot(a, b, preferred_element_type=F32, **kw)


def shape(dtype, *dims):
    return jax.ShapeDtypeStruct(dims, dtype)


VMEM = pl.BlockSpec(memory_space=pltpu.VMEM)
HBM = pl.BlockSpec(memory_space=pltpu.HBM)


def vmem(dtype, *dims):
    return pltpu.VMEM(dims, dtype)


def call(kernel, name, outs, operands, params=(), scratch=(), limit=12, us=1.0, aliases=None):
    operands = [pltpu.with_memory_space_constraint(v, pltpu.VMEM) for v in operands]
    params = [pltpu.with_memory_space_constraint(v, pltpu.HBM) for v in params]
    return pl.pallas_call(
        kernel,
        name=name,
        in_specs=[VMEM] * len(operands) + [HBM] * len(params),
        out_specs=[HBM if isinstance(o, jax.ShapeDtypeStruct) else VMEM for o in outs],
        out_shape=outs,
        scratch_shapes=list(scratch),
        input_output_aliases=aliases or {},
        compiler_params=pltpu.CompilerParams(vmem_limit_bytes=limit * MIB),
        cost_estimate=pl.CostEstimate(flops=int(us * 1e8), bytes_accessed=int(us * 3e5), transcendentals=0),
    )(*operands, *params)


def place():
    at = lax.axis_index("seq")
    return at & 1, (at >> 1) & 1, at >> 2


def columns(start, width):
    return pl.ds(pl.multiple_of(start, 128), width)


def split2(x):
    hi = x.astype(BF16)
    lo = (x - hi.astype(F32)).astype(BF16)
    return hi, lo


def spread_matrix(start, width=CW):
    k = lax.broadcasted_iota(jnp.int32, (2 * HEADS, width), 0)
    col = lax.broadcasted_iota(jnp.int32, (2 * HEADS, width), 1)
    low = (k & (HEADS - 1)) * HEAD_DIM - start
    return jnp.where((col >= low) & (col < low + HEAD_DIM), 1.0, 0.0).astype(BF16)


def read_decay(rows):
    rows = rows.astype(F32)
    return rows[0:1] + rows[1:2]


def decay_rows(d):
    hi, lo = split2(d)
    none = jnp.zeros((14, d.shape[1]), F32)
    return jnp.concatenate([hi.astype(F32), lo.astype(F32), none], axis=0).astype(BF16)


def make_tables(step, decay, skip, table_ref, mcol_ref, mrow_ref, drow_ref):
    a = -decay * step
    row = lax.broadcasted_iota(jnp.int32, (TOK, TOK), 0)
    col = lax.broadcasted_iota(jnp.int32, (TOK, TOK), 1)
    tri = jnp.where((row >= col) & ((row >= SUB) == (col >= SUB)), 1.0, 0.0)
    cum = dot(tri, a, precision=lax.Precision.HIGHEST)
    excl = cum - a
    e0 = cum[SUB - 1 : SUB]
    e1 = cum[TOK - 1 : TOK]
    ends = jnp.concatenate([jnp.broadcast_to(e0, (SUB, HEADS)), jnp.broadcast_to(e1, (SUB, HEADS))], axis=0)
    zero = jnp.zeros_like(cum)

    def put(at, value):
        hi, lo = split2(value)
        table_ref[at] = jnp.concatenate([hi, lo], axis=1)

    put(WF, step * jnp.exp(jnp.minimum(ends - cum, zero)))
    put(WR, step * jnp.exp(excl))
    put(GF, jnp.exp(cum))
    put(GR, jnp.exp(jnp.minimum(ends - excl, zero)))
    put(WV, step * jnp.exp(-0.5 * a))
    put(GT, jnp.exp(0.5 * a))
    m = (cum - 0.5 * a) * LOG2E
    mcol_ref[...] = jnp.concatenate([m, zero], axis=1)
    mrow_ref[...] = jnp.transpose(m)
    h0, l0 = split2(jnp.exp(e0))
    h1, l1 = split2(jnp.exp(e1))
    hd, ld = split2(jnp.exp(e0 + e1))
    hs, ls = split2(skip)
    no = jnp.zeros_like(h0)
    wide = [
        jnp.concatenate([hd, no], axis=1).astype(F32),
        jnp.concatenate([no, ld], axis=1).astype(F32),
        jnp.zeros((6, 2 * HEADS), F32),
        jnp.concatenate([h0, l0], axis=1).astype(F32),
        jnp.concatenate([h1, l1], axis=1).astype(F32),
        jnp.concatenate([hs, ls], axis=1).astype(F32),
        jnp.zeros((5, 2 * HEADS), F32),
    ]
    drow_ref[...] = jnp.concatenate(wide, axis=0).astype(BF16)


def conv(x, cf, cr):
    rows = x.shape[0]
    back = pltpu.roll(x, 1, 0)
    fore = pltpu.roll(x, rows - 1, 0)
    h = cf[3:4] * x + cf[2:3] * back + pltpu.roll(cf[1:2] * x + cf[0:1] * back, 2, 0)
    g = cr[3:4] * x + cr[2:3] * fore + pltpu.roll(cr[1:2] * x + cr[0:1] * fore, rows - 2, 0)
    return h, g


def silu_of_half(h):
    return (h + h * jnp.tanh(h)).astype(BF16)


def copy_all(pairs, sems):
    copies = [pltpu.make_async_copy(src, dst, sems.at[k]) for k, (src, dst) in enumerate(pairs)]
    for copy in copies:
        copy.start()
    return copies


def start_of(k, p):
    c, z, y = place()
    return (z if k == 3 else 1 - z) * QUART + p * CW


def edge_kernel(x_hbm, step_hbm, to_core_ref, to_chip_ref, step_ref, sems):
    c, z, y = place()
    far = columns((1 - c) * HALF, HALF)
    ends = pl.ds(pl.multiple_of(c * (TOK - HALO), HALO), HALO)
    copies = copy_all(
        [
            (step_hbm, step_ref),
            (x_hbm.at[ends], to_chip_ref),
            (x_hbm.at[:, far], to_core_ref.at[:, 0:HALF]),
            (x_hbm.at[:, INNER:E], to_core_ref.at[:, HALF:WIDE]),
        ],
        sems,
    )
    copies[0].wait()
    step = jnp.transpose(step_ref[...])
    p0 = step.astype(BF16).astype(F32)
    p1 = (step - p0).astype(BF16).astype(F32)
    p2 = step - p0 - p1
    to_core_ref[:, WIDE : WIDE + STEPS] = jnp.concatenate([p0, p1, p2, jnp.zeros_like(p0)], axis=1).astype(BF16)
    for copy in copies[1:]:
        copy.wait()


def halo_kernel(halo_ref, after_ref, mine_ref, to_core_ref):
    c, z, y = place()
    for ref, half in ((mine_ref, c), (to_core_ref, 1 - c)):
        ref[:, 0:HALF] = halo_ref[:, columns(half * HALF, HALF)]
        ref[:, HALF:WIDE] = halo_ref[:, INNER:E]


def conv_piece(x_ref, taps_ref, u_ref, start, halo=None):
    def body(i, _):
        at = columns(start + i * 128, 128)
        cols = columns(i * 128, 128)
        cf, cr = taps_ref[0:4, at], taps_ref[4:8, at]
        x0, x1 = x_ref[0, :, at].astype(F32), x_ref[1, :, at].astype(F32)
        before, after = halo(at) if halo else (x0[0:8], x1[TOK - 8 :])
        for b, rows in enumerate(((before, x0, x1[0:8]), (x0[TOK - 8 :], x1, after))):
            h, g = conv(jnp.concatenate(rows, axis=0), cf, cr)
            u_ref[b, 0, :, cols] = silu_of_half(h[8 : TOK + 8])
            u_ref[b, 1, :, cols] = silu_of_half(g[8 : TOK + 8])
        return _

    lax.fori_loop(0, u_ref.shape[3] // 128, body, 0)


def halo_of(chip_ref, core_ref):
    def rows(at):
        c, z, y = place()
        chip, core = chip_ref[:, at].astype(F32), core_ref[:, at].astype(F32)
        before, after = jnp.where(c == 0, chip, core), jnp.where(c == 0, core, chip)
        return before[HALO - 8 :], after[:8]

    return rows


def repair(x_ref, taps_ref, u_ref, start, halo):
    def body(i, _):
        at = columns(start + i * 256, 256)
        cols = columns(i * 256, 256)
        cf, cr = taps_ref[0:4, at], taps_ref[4:8, at]
        before, after = halo(at)
        h, _g = conv(jnp.concatenate([before, x_ref[0, 0:HALO, at].astype(F32)], axis=0), cf, cr)
        u_ref[0, 0, 0:HALO, cols] = silu_of_half(h[8:])
        _h, g = conv(jnp.concatenate([x_ref[1, TOK - HALO : TOK, at].astype(F32), after], axis=0), cf, cr)
        u_ref[1, 1, TOK - HALO : TOK, cols] = silu_of_half(g[:HALO])
        return _

    lax.fori_loop(0, u_ref.shape[3] // 256, body, 0)


def front_kernel(
    other_ref, x_hbm, step_hbm, decay_hbm, skip_hbm, cf_hbm, cr_hbm, gate_hbm,
    x_ref, table_ref, mcol_ref, mrow_ref, drow_ref, taps_ref, kq_ref, u_ref, gate_ref, gate_to_core_ref,
    step_ref, decay_ref, skip_ref, cf_ref, cr_ref, sems,
):
    c, z, y = place()
    half = columns(c * HALF, HALF)
    copies = copy_all(
        [
            (step_hbm, step_ref),
            (decay_hbm, decay_ref),
            (skip_hbm, skip_ref),
            (x_hbm.at[:, half], x_ref.at[c, :, 0:HALF]),
            (x_hbm.at[:, INNER:E], x_ref.at[c, :, HALF:WIDE]),
            (cf_hbm.at[:, half], cf_ref.at[:, 0:HALF]),
            (cf_hbm.at[:, INNER:E], cf_ref.at[:, HALF:WIDE]),
            (cr_hbm.at[:, half], cr_ref.at[:, 0:HALF]),
            (cr_hbm.at[:, INNER:E], cr_ref.at[:, HALF:WIDE]),
            (other_ref.at[:, 0:WIDE], x_ref.at[1 - c]),
            (gate_hbm.at[:, half], gate_ref),
            (gate_hbm.at[:, columns((1 - c) * HALF, HALF)], gate_to_core_ref),
        ],
        sems,
    )
    for copy in copies[:3]:
        copy.wait()
    def half_of(values):
        return jnp.where(c == 0, values[:, 0 : HEADS // 2], values[:, HEADS // 2 : HEADS])

    parts = other_ref[:, WIDE : WIDE + STEPS].astype(F32)
    other = half_of(parts[:, 0:HEADS] + parts[:, HEADS : 2 * HEADS] + parts[:, 2 * HEADS : 3 * HEADS])
    mine = half_of(jnp.transpose(step_ref[...]))
    step = jnp.concatenate([jnp.where(c == 0, mine, other), jnp.where(c == 0, other, mine)], axis=1)
    decay, skip = half_of(decay_ref[...]), half_of(skip_ref[...])
    decay, skip = jnp.concatenate([decay, decay], axis=1), jnp.concatenate([skip, skip], axis=1)
    make_tables(step, decay, skip, table_ref, mcol_ref, mrow_ref, drow_ref)
    for copy in copies[3:10]:
        copy.wait()
    taps_ref[0:4] = cf_ref[...] * 0.5
    taps_ref[4:8] = cr_ref[...] * 0.5
    conv_piece(x_ref, taps_ref, kq_ref, HALF)
    conv_piece(x_ref, taps_ref, u_ref, start_of(2, 0))
    for copy in copies[10:]:
        copy.wait()


def piece_states(u_ref, kt_ref, table_ref, drow_ref, start, saved_ref, chip_ref):
    blocks = []
    for b in range(2):
        spread = spread_matrix(b * HALF + start)
        drow = dot(drow_ref[...], spread)
        d0, d1 = drow[8:9], drow[9:10]

        def weighted(d, row, r):
            w = dot(table_ref[row, r : r + SUB], spread)
            return (u_ref[b, d, r : r + SUB].astype(F32) * w).astype(BF16)

        f0 = dot(kt_ref[b, 0, :, 0:SUB], weighted(0, WF, 0))
        f1 = dot(kt_ref[b, 0, :, SUB:TOK], weighted(0, WF, SUB))
        r0 = dot(kt_ref[b, 1, :, 0:SUB], weighted(1, WR, 0))
        r1 = dot(kt_ref[b, 1, :, SUB:TOK], weighted(1, WR, SUB))
        saved_ref[2 * b] = f0.astype(BF16)
        saved_ref[2 * b + 1] = r1.astype(BF16)
        blocks.append((d1 * f0 + f1, r0 + d0 * r1, drow[0:1] + drow[1:2]))
    (f0, r0, d0), (f1, r1, d1) = blocks
    saved_ref[4] = f0.astype(BF16)
    saved_ref[5] = r1.astype(BF16)
    chip_ref[0:STATE] = (d1 * f0 + f1).astype(BF16)
    chip_ref[STATE : 2 * STATE] = (r0 + d0 * r1).astype(BF16)
    chip_ref[2 * STATE : MSG] = decay_rows(d0 * d1)


def first_states_kernel(
    kq_in, u_in, x_ref, taps_ref, chip_halo_ref, core_halo_ref, table_ref, drow_ref,
    kq_ref, u_ref, kt_ref, saved_ref, chip_ref,
):
    halo = halo_of(chip_halo_ref, core_halo_ref)
    repair(x_ref, taps_ref, kq_ref, HALF, halo)
    for b in range(2):
        for d in range(2):
            kt_ref[b, d] = jnp.transpose(kq_ref[b, d, :, 0:STATE].astype(F32)).astype(BF16)
    start = start_of(2, 0)
    repair(x_ref, taps_ref, u_ref, start, halo)
    piece_states(u_ref, kt_ref, table_ref, drow_ref, start, saved_ref, chip_ref)


def rest_kernel(todo, x_ref, taps_ref, chip_halo_ref, core_halo_ref, table_ref, drow_ref, kt_ref, after_ref, *outs):
    for n, piece in enumerate(todo):
        u_ref, saved_ref, chip_ref = outs[3 * n : 3 * n + 3]
        conv_piece(x_ref, taps_ref, u_ref, start_of(*piece), halo_of(chip_halo_ref, core_halo_ref))
        piece_states(u_ref, kt_ref, table_ref, drow_ref, start_of(*piece), saved_ref, chip_ref)


KEYS = vmem(BF16, 2, 2, TOK, 2 * STATE)
U = vmem(BF16, 2, 2, TOK, CW)
SAVED = vmem(BF16, 6, STATE, CW)
CHIP = vmem(BF16, MSG, CW)


def group(keep_ref, got_ref, outs):
    c, z, y = place()
    z0 = z == 0
    dm, do = read_decay(keep_ref[2 * STATE : MSG]), read_decay(got_ref[2 * STATE : MSG])
    one = jnp.ones_like(dm)
    am, ao = jnp.where(z0, do, one), jnp.where(z0, one, dm)
    fwd = (am * keep_ref[0:STATE].astype(F32) + ao * got_ref[0:STATE].astype(F32)).astype(BF16)
    am, ao = jnp.where(z0, one, do), jnp.where(z0, dm, one)
    rows = slice(STATE, 2 * STATE)
    rev = (am * keep_ref[rows].astype(F32) + ao * got_ref[rows].astype(F32)).astype(BF16)
    decay = decay_rows(dm * do)
    for k in range(1, 4):
        outs[k - 1][0:STATE] = jnp.where(y + k < 4, fwd, rev)
        outs[k - 1][STATE:YMSG] = decay


def entries(keep_ref, got_ref, r1_ref, r2_ref, r3_ref, mine_ref, back_ref):
    c, z, y = place()
    z0 = z == 0
    r = [ref[0:STATE].astype(F32) for ref in (r1_ref, r2_ref, r3_ref)]
    d = [read_decay(ref[STATE:YMSG]) for ref in (r1_ref, r2_ref, r3_ref)]
    zero = jnp.zeros_like(r[0])
    ef = jnp.where(y >= 3, r[2], zero)
    ef = jnp.where(y >= 2, r[1] + d[1] * ef, zero)
    ef = jnp.where(y >= 1, r[0] + d[0] * ef, zero)
    er = jnp.where(y <= 0, r[0], zero)
    er = jnp.where(y <= 1, r[1] + d[1] * er, zero)
    er = jnp.where(y <= 2, r[2] + d[2] * er, zero)
    dm, do = read_decay(keep_ref[2 * STATE : MSG]), read_decay(got_ref[2 * STATE : MSG])
    df = jnp.where(z0, dm, do)
    tf = jnp.where(z0, keep_ref[0:STATE].astype(F32), got_ref[0:STATE].astype(F32))
    second_f = df * ef + tf
    dr = jnp.where(z0, do, dm)
    rows = slice(STATE, 2 * STATE)
    tr = jnp.where(z0, got_ref[rows].astype(F32), keep_ref[rows].astype(F32))
    first_r = dr * er + tr
    mine_ref[0] = jnp.where(z0, ef, second_f).astype(BF16)
    mine_ref[1] = jnp.where(z0, first_r, er).astype(BF16)
    back_ref[0] = jnp.where(z0, second_f, ef).astype(BF16)
    back_ref[1] = jnp.where(z0, er, first_r).astype(BF16)


def second_phase_kernel(keep_ref, got_ref, zsend_ref, after_ref, zsend_out, *outs):
    group(keep_ref, got_ref, outs)
    zsend_out[...] = zsend_ref[...]


def third_phase_kernel(
    keep0_ref, got0_ref, r1_ref, r2_ref, r3_ref, keep1_ref, got1_ref, after_ref, mine_ref, back_ref, *outs
):
    entries(keep0_ref, got0_ref, r1_ref, r2_ref, r3_ref, mine_ref, back_ref)
    group(keep1_ref, got1_ref, outs)


def fourth_phase_kernel(
    keep_ref, got_ref, r1_ref, r2_ref, r3_ref, after0_ref, after1_ref, mine_ref, back_ref
):
    entries(keep_ref, got_ref, r1_ref, r2_ref, r3_ref, mine_ref, back_ref)


def within_kernel(k, p, u_ref, kq_ref, table_ref, mcol_ref, mrow_ref, drow_ref, after_ref, out_ref, qk_ref):
    row = lax.broadcasted_iota(jnp.int32, (SUB, SUB), 0)
    col = lax.broadcasted_iota(jnp.int32, (SUB, SUB), 1)
    low = lax.broadcasted_iota(jnp.int32, (SUB, 2 * HEAD_DIM), 1) < HEAD_DIM

    def block(b, _):
        for s in range(2):
            rows = slice(s * SUB, (s + 1) * SUB)
            for d in range(2):
                keys = kq_ref[b, d, rows, 0:STATE]
                queries = kq_ref[b, d, rows, STATE : 2 * STATE]
                prod = lax.dot_general(queries, keys, (((1,), (1,)), ((), ())), preferred_element_type=F32)
                qk_ref[d, s] = jnp.where((row >= col) if d == 0 else (row <= col), prod, 0.0)
        start = b * HALF + start_of(k, p)
        first = start // HEAD_DIM
        spread = spread_matrix(start)
        skip = dot(drow_ref[...], spread)[10:11]
        mcol = pltpu.roll(mcol_ref[...], 2 * HEADS - first, 1)
        mrow = mrow_ref[pl.ds(pl.multiple_of(first, HC), HC), :]
        for s in range(2):
            rows = slice(s * SUB, (s + 1) * SUB)
            wv = dot(table_ref[WV, rows], spread)
            gt = dot(table_ref[GT, rows], spread)
            for two in range(HC // 2):
                cols = slice(two * 128, (two + 1) * 128)
                up = u_ref[b, 0, rows, cols].astype(F32)
                xf = (up * wv[:, cols]).astype(BF16)
                xb = (u_ref[b, 1, rows, cols].astype(F32) * wv[:, cols]).astype(BF16)
                none = jnp.zeros_like(xf)
                left, right = [], []
                for h in range(2):
                    at = two * 2 + h
                    diff = mcol[rows, at : at + 1] - mrow[at : at + 1, rows]
                    decay = jnp.exp2(-jnp.abs(diff))
                    left += [(decay * qk_ref[0, s]).astype(BF16), (decay * qk_ref[1, s]).astype(BF16)]
                    keep = low if h == 0 else ~low
                    right += [jnp.where(keep, xf, none), jnp.where(keep, xb, none)]
                res = dot(jnp.concatenate(left, axis=1), jnp.concatenate(right, axis=0))
                out_ref[b, rows, cols] = (res * gt[:, cols] + up * skip[:, cols]).astype(BF16)
        return _

    lax.fori_loop(0, 2, block, 0)


def make_within(k, p, u, kq, table, mcol, mrow, drow, after):
    scratch = [pltpu.VMEM((2, 2, SUB, SUB), F32)]
    operands = (u, kq, table, mcol, mrow, drow, after)
    kernel = functools.partial(within_kernel, k, p)
    return call(kernel, f"within_{k}{p}", [vmem(BF16, 2, TOK, CW)], operands, (), scratch)[0]


def finish_part(k, p, other, entry_ref, saved_ref, within_ref, gate_ref, kq_ref, table_ref, drow_ref, put, square):
    c, z, y = place()
    b = 1 - c if other else c
    start = start_of(k, p)
    at = columns(start, CW)
    spread = spread_matrix(b * HALF + start)
    drow = dot(drow_ref[...], spread)
    d0, d1 = drow[8:9], drow[9:10]
    far = dot(drow_ref[...], spread_matrix((1 - b) * HALF + start))
    far = far[0:1] + far[1:2]
    one = jnp.ones_like(far)
    none = jnp.zeros((STATE, CW), F32)
    first = b == 0
    ef = jnp.where(first, one, far) * entry_ref[0].astype(F32) + jnp.where(first, none, saved_ref[4].astype(F32))
    er = jnp.where(first, far, one) * entry_ref[1].astype(F32) + jnp.where(first, saved_ref[5].astype(F32), none)
    inside = [
        (ef.astype(BF16), (er * d1 + saved_ref[2 * b + 1].astype(F32)).astype(BF16)),
        ((ef * d0 + saved_ref[2 * b].astype(F32)).astype(BF16), er.astype(BF16)),
    ]
    for s in range(2):
        rows = slice(s * SUB, (s + 1) * SUB)
        cf = dot(kq_ref[b, 0, rows, STATE : 2 * STATE], inside[s][0])
        cr = dot(kq_ref[b, 1, rows, STATE : 2 * STATE], inside[s][1])
        gf = dot(table_ref[GF, rows], spread)
        gr = dot(table_ref[GR, rows], spread)
        mixed = within_ref[b, rows].astype(F32) + gf * cf + gr * cr
        half = gate_ref[rows, at].astype(F32) * 0.5
        gated = mixed * (half + half * jnp.tanh(half))
        put(rows, gated)
        sq = gated * gated
        for j in range(0, CW, 128):
            part = sq[:, j : j + 128]
            square[s] = part if square[s] is None else square[s] + part


def finish_piece(k, p, entry_ref, saved_ref, within_ref, gate_refs, shared, own_ref, msg_refs, squares):
    def put_own(rows, gated):
        own_ref[rows] = gated

    def put_other(rows, gated):
        msg_refs[rows.start // SUB][:, 0:CW] = gated.astype(BF16)

    for other, put in ((1, put_other), (0, put_own)):
        finish_part(k, p, other, entry_ref, saved_ref, within_ref, gate_refs[other], *shared, put, squares[other])


NEAR = ((3, 0), (3, 1), (2, 0))
BACK = (2, 1)


def finish_near_kernel(k, p, entry_ref, saved_ref, within_ref, gate_ref, gate_other_ref, *refs):
    shared, (square_in, own_ref, *msg_refs, square_ref) = refs[:3], refs[3:]
    squares = [[None, None], [None, None]]
    finish_piece(k, p, entry_ref, saved_ref, within_ref, (gate_ref, gate_other_ref), shared, own_ref, msg_refs, squares)
    for other in range(2):
        for s in range(2):
            rows = slice(s * SUB, (s + 1) * SUB)
            if (k, p) == NEAR[0]:
                square_ref[other, rows] = squares[other][s]
            else:
                square_ref[other, rows] = square_in[other, rows] + squares[other][s]


def finish_other_kernel(entry_ref, saved_ref, within_ref, gate_ref, *refs):
    shared, square_in, msg_refs = refs[:3], refs[3], refs[-2:]
    square = [square_in[1, s * SUB : (s + 1) * SUB] for s in range(2)]

    def put(rows, gated):
        msg_refs[rows.start // SUB][:, 0:CW] = gated.astype(BF16)

    finish_part(*BACK, 1, entry_ref, saved_ref, within_ref, gate_ref, *shared, put, square)
    lane = lax.broadcasted_iota(jnp.int32, (SUB, 128), 1)
    for s in range(2):
        total = jnp.sum(square[s], axis=1, keepdims=True)
        hi = total.astype(BF16).astype(F32)
        sums = jnp.where(lane == 0, hi, jnp.where(lane == 1, total - hi, 0.0))
        msg_refs[s][:, CW : CW + 128] = sums.astype(BF16)


def finish_own_kernel(entry_ref, saved_ref, within_ref, gate_ref, *refs):
    shared, (square_in, after_ref, gain_hbm, own_ref, square_ref, gain_ref, sem) = refs[:3], refs[3:]
    copy = pltpu.make_async_copy(gain_hbm, gain_ref, sem)
    copy.start()
    square = [square_in[0, s * SUB : (s + 1) * SUB] for s in range(2)]

    def put(rows, gated):
        own_ref[rows] = gated

    finish_part(*BACK, 0, entry_ref, saved_ref, within_ref, gate_ref, *shared, put, square)
    for s in range(2):
        square_ref[s * SUB : (s + 1) * SUB] = square[s]
    copy.wait()


def norm_kernel(*refs):
    own_refs, other_refs, (square_ref, gain_ref, out_hbm, out_ref, sems) = refs[:4], refs[4:12], refs[12:]
    c, z, y = place()
    pieces = []
    for n, piece in enumerate((*NEAR, BACK)):
        pieces.append(((own_refs[n], own_refs[n].at[SUB:TOK]), c * HALF + start_of(*piece)))
        pieces.append((other_refs[2 * n : 2 * n + 2], (1 - c) * HALF + start_of(*piece)))
    step = 32
    copies = []
    for r in range(0, TOK, step):
        rows, inside = slice(r, r + step), slice(r % SUB, r % SUB + step)
        total = square_ref[rows] + other_refs[6 + r // SUB][inside, CW : CW + 128].astype(F32)
        scale = lax.rsqrt(jnp.sum(total, axis=1, keepdims=True) * (1.0 / INNER) + 1e-05)
        for refs, start in pieces:
            at = columns(start, CW)
            out_ref[rows, at] = (refs[r // SUB][inside, 0:CW].astype(F32) * scale * gain_ref[:, at]).astype(BF16)
        copies.append(pltpu.make_async_copy(out_ref.at[rows], out_hbm.at[rows], sems.at[len(copies)]))
        copies[-1].start()
    for copy in copies:
        copy.wait()


def per_device(mixer_input, gate_input, conv_forward, conv_reverse, step_size, decay_rate, skip_scale, norm_gain):
    n = lax.axis_size("seq")

    def send(v, perm):
        return lax.ppermute(v, "seq", perm)

    core = [(i, i ^ 1) for i in range(n)]
    zswap = [(i, i ^ 2) for i in range(n)]
    chips = [(i, i + 1) for i in range(1, n - 1, 2)] + [(i + 1, i) for i in range(1, n - 1, 2)]

    def along_y(msgs):
        return [send(m, [(i, (i + 4 * k) % n) for i in range(n)]) for k, m in enumerate(msgs, 1)]

    to_core, to_chip = call(
        edge_kernel,
        "edges",
        [vmem(BF16, TOK, WIDE + STEPS), vmem(BF16, HALO, E)],
        (),
        (mixer_input, step_size),
        [pltpu.VMEM((HEADS, TOK), F32), pltpu.SemaphoreType.DMA((4,))],
    )
    x, table, mcol, mrow, drow, taps, kq, u2a, gate, gate_to_core = call(
        front_kernel,
        "front",
        [
            vmem(BF16, 2, TOK, WIDE),
            vmem(BF16, 6, TOK, 2 * HEADS),
            vmem(F32, TOK, 2 * HEADS),
            vmem(F32, HEADS, TOK),
            vmem(BF16, 16, 2 * HEADS),
            vmem(F32, 8, WIDE),
            KEYS,
            U,
            vmem(BF16, TOK, HALF),
            vmem(BF16, TOK, HALF),
        ],
        (send(to_core, core),),
        (
            mixer_input,
            step_size,
            decay_rate.reshape(1, HEADS),
            skip_scale.reshape(1, HEADS),
            conv_forward,
            conv_reverse,
            gate_input,
        ),
        [
            pltpu.VMEM((HEADS, TOK), F32),
            pltpu.VMEM((1, HEADS), F32),
            pltpu.VMEM((1, HEADS), F32),
            pltpu.VMEM((4, WIDE), F32),
            pltpu.VMEM((4, WIDE), F32),
            pltpu.SemaphoreType.DMA((12,)),
        ],
    )
    chip_halo, to_core = call(
        halo_kernel, "halo", [vmem(BF16, HALO, WIDE)] * 2, (send(to_chip, chips), kq)
    )
    halo = (x, taps, chip_halo, send(to_core, core))
    kq, u2a, kt, saved2a, zsend0 = call(
        first_states_kernel,
        "states_first",
        [KEYS, U, vmem(BF16, 2, 2, STATE, TOK), SAVED, CHIP],
        (kq, u2a, *halo, table, drow),
        aliases={0: 0, 1: 1},
    )
    got0 = send(zsend0, zswap)

    def make_rest(name, todo, after):
        kernel = functools.partial(rest_kernel, todo)
        return call(kernel, name, [U, SAVED, CHIP] * len(todo), (*halo, table, drow, kt, after))

    u2b, saved2b, zsend1, u3a, saved3a, keep0 = make_rest("states_a", ((2, 1), (3, 0)), zsend0)
    tables = (kq, table, mcol, mrow, drow)

    w2a = make_within(2, 0, u2a, *tables, zsend0)
    yout = [vmem(BF16, YMSG, CW)] * 3
    entry = vmem(BF16, 2, STATE, CW)
    zsend1, *msgs = call(second_phase_kernel, "second_phase", [CHIP, *yout], (keep0, got0, zsend1, w2a))
    got1 = send(zsend1, zswap)
    arrived = along_y(msgs)
    u3b, saved3b, keep1 = make_rest("states_b", ((3, 1),), msgs[0])
    w2b = make_within(2, 1, u2b, *tables, msgs[0])

    mine0, back0, *msgs = call(
        third_phase_kernel, "third_phase", [entry, entry, *yout], (keep0, got0, *arrived, keep1, got1, w2b)
    )
    back0 = send(back0, zswap)
    arrived = along_y(msgs)
    w3a = make_within(3, 0, u3a, *tables, msgs[0])
    w3b = make_within(3, 1, u3b, *tables, w3a)

    mine1, back1 = call(fourth_phase_kernel, "fourth_phase", [entry, entry], (keep1, got1, *arrived, w3b, back0))
    back1 = send(back1, zswap)
    gates = (gate, send(gate_to_core, core))
    shared = (kq, table, drow)
    square = kt
    own, other = [], []
    for (k, p), *part in zip(NEAR, (mine0, mine1, back0), (saved3a, saved3b, saved2a), (w3a, w3b, w2a)):
        gated, *msg, square = call(
            functools.partial(finish_near_kernel, k, p),
            f"finish_{k}{p}",
            [vmem(F32, TOK, CW), vmem(BF16, SUB, CW), vmem(BF16, SUB, CW), vmem(F32, 2, TOK, 128)],
            (*part, *gates, *shared, square),
        )
        own.append(gated)
        other += [send(m, core) for m in msg]
    msg = call(
        finish_other_kernel,
        "finish_other",
        [vmem(BF16, SUB, CW + 128)] * 2,
        (back1, saved2b, w2b, gates[1], *shared, square, *other[:4]),
    )
    other += [send(m, core) for m in msg]
    gated, square, gain = call(
        finish_own_kernel,
        "finish_own",
        [vmem(F32, TOK, CW), vmem(F32, TOK, 128), vmem(F32, 1, INNER)],
        (back1, saved2b, w2b, gates[0], *shared, square, msg[0]),
        (norm_gain.reshape(1, INNER),),
        [pltpu.SemaphoreType.DMA(())],
    )
    own.append(gated)
    (out,) = call(
        norm_kernel,
        "norm",
        [shape(BF16, TOK, INNER)],
        (*own, *other, square, gain),
        (),
        [pltpu.VMEM((TOK, INNER), BF16), pltpu.SemaphoreType.DMA((8,))],
    )
    return out


def solution(mesh):
    in_specs = (
        P(("row", "seq"), None),
        P(("row", "seq"), None),
        P(),
        P(),
        P(None, ("row", "seq")),
        P("row"),
        P(),
        P(),
    )
    out_specs = P(("row", "seq"), None)
    return jax.shard_map(per_device, mesh=mesh, in_specs=in_specs, out_specs=out_specs, check_vma=False)
```

```python
import functools

import jax
import jax.numpy as jnp
from jax import lax
from jax.experimental import pallas as pl
from jax.experimental.pallas import tpu as pltpu
from jax.sharding import PartitionSpec as P

HEADS = 64
HEAD_DIM = 64
STATE = 128
TOK = 256
SUB = 128
INNER = 4096
E = 4352
HALF = INNER // 2
QUART = INNER // 4
WIDE = HALF + 2 * STATE
STEPS = 256
CW = 512
HC = CW // HEAD_DIM
HALO = 16
MSG = 2 * STATE + 16
YMSG = STATE + 16
LOG2E = 1.4426950408889634
F32 = jnp.float32
BF16 = jnp.bfloat16
WF, WR, GF, GR, WV, GT = range(6)
MIB = 2**20


def dot(a, b, **kw):
    return jnp.dot(a, b, preferred_element_type=F32, **kw)


def shape(dtype, *dims):
    return jax.ShapeDtypeStruct(dims, dtype)


VMEM = pl.BlockSpec(memory_space=pltpu.VMEM)
HBM = pl.BlockSpec(memory_space=pltpu.HBM)


def vmem(dtype, *dims):
    return pltpu.VMEM(dims, dtype)


def call(kernel, name, outs, operands, params=(), scratch=(), limit=12, us=1.0, aliases=None):
    operands = [pltpu.with_memory_space_constraint(v, pltpu.VMEM) for v in operands]
    params = [pltpu.with_memory_space_constraint(v, pltpu.HBM) for v in params]
    return pl.pallas_call(
        kernel,
        name=name,
        in_specs=[VMEM] * len(operands) + [HBM] * len(params),
        out_specs=[HBM if isinstance(o, jax.ShapeDtypeStruct) else VMEM for o in outs],
        out_shape=outs,
        scratch_shapes=list(scratch),
        input_output_aliases=aliases or {},
        compiler_params=pltpu.CompilerParams(vmem_limit_bytes=limit * MIB),
        cost_estimate=pl.CostEstimate(flops=int(us * 1e8), bytes_accessed=int(us * 3e5), transcendentals=0),
    )(*operands, *params)


def place():
    at = lax.axis_index("seq")
    return at & 1, (at >> 1) & 1, at >> 2


def columns(start, width):
    return pl.ds(pl.multiple_of(start, 128), width)


def split2(x):
    hi = x.astype(BF16)
    lo = (x - hi.astype(F32)).astype(BF16)
    return hi, lo


def spread_matrix(start, width=CW):
    k = lax.broadcasted_iota(jnp.int32, (2 * HEADS, width), 0)
    col = lax.broadcasted_iota(jnp.int32, (2 * HEADS, width), 1)
    low = (k & (HEADS - 1)) * HEAD_DIM - start
    return jnp.where((col >= low) & (col < low + HEAD_DIM), 1.0, 0.0).astype(BF16)


def expand(table_ref, first, spread):
    both = dot(table_ref[first : first + 2].reshape(2 * TOK, 2 * HEADS), spread)
    return both[0:TOK], both[TOK:]


def read_decay(rows):
    rows = rows.astype(F32)
    return rows[0:1] + rows[1:2]


def decay_rows(d):
    hi, lo = split2(d)
    none = jnp.zeros((14, d.shape[1]), F32)
    return jnp.concatenate([hi.astype(F32), lo.astype(F32), none], axis=0).astype(BF16)


def make_tables(step, decay, skip, table_ref, mcol_ref, mrow_ref, drow_ref):
    a = -decay * step
    row = lax.broadcasted_iota(jnp.int32, (TOK, TOK), 0)
    col = lax.broadcasted_iota(jnp.int32, (TOK, TOK), 1)
    tri = jnp.where((row >= col) & ((row >= SUB) == (col >= SUB)), 1.0, 0.0)
    cum = dot(tri, a, precision=lax.Precision.HIGHEST)
    excl = cum - a
    e0 = cum[SUB - 1 : SUB]
    e1 = cum[TOK - 1 : TOK]
    ends = jnp.concatenate([jnp.broadcast_to(e0, (SUB, HEADS)), jnp.broadcast_to(e1, (SUB, HEADS))], axis=0)
    zero = jnp.zeros_like(cum)

    def put(at, value):
        hi, lo = split2(value)
        table_ref[at] = jnp.concatenate([hi, lo], axis=1)

    put(WF, step * jnp.exp(jnp.minimum(ends - cum, zero)))
    put(WR, step * jnp.exp(excl))
    put(GF, jnp.exp(cum))
    put(GR, jnp.exp(jnp.minimum(ends - excl, zero)))
    put(WV, step * jnp.exp(-0.5 * a))
    put(GT, jnp.exp(0.5 * a))
    m = (cum - 0.5 * a) * LOG2E
    mcol_ref[...] = jnp.concatenate([m, zero], axis=1)
    mrow_ref[...] = jnp.transpose(m)
    h0, l0 = split2(jnp.exp(e0))
    h1, l1 = split2(jnp.exp(e1))
    hd, ld = split2(jnp.exp(e0 + e1))
    hs, ls = split2(skip)
    no = jnp.zeros_like(h0)
    wide = [
        jnp.concatenate([hd, no], axis=1).astype(F32),
        jnp.concatenate([no, ld], axis=1).astype(F32),
        jnp.zeros((6, 2 * HEADS), F32),
        jnp.concatenate([h0, l0], axis=1).astype(F32),
        jnp.concatenate([h1, l1], axis=1).astype(F32),
        jnp.concatenate([hs, ls], axis=1).astype(F32),
        jnp.zeros((5, 2 * HEADS), F32),
    ]
    drow_ref[...] = jnp.concatenate(wide, axis=0).astype(BF16)


def conv(x, cf, cr):
    rows = x.shape[0]
    back = pltpu.roll(x, 1, 0)
    fore = pltpu.roll(x, rows - 1, 0)
    h = cf[3:4] * x + cf[2:3] * back + pltpu.roll(cf[1:2] * x + cf[0:1] * back, 2, 0)
    g = cr[3:4] * x + cr[2:3] * fore + pltpu.roll(cr[1:2] * x + cr[0:1] * fore, rows - 2, 0)
    return h, g


def silu_of_half(h):
    return (h + h * jnp.tanh(h)).astype(BF16)


def copy_all(pairs, sems):
    copies = [pltpu.make_async_copy(src, dst, sems.at[k]) for k, (src, dst) in enumerate(pairs)]
    for copy in copies:
        copy.start()
    return copies


def start_of(k, p):
    c, z, y = place()
    return (z if k == 3 else 1 - z) * QUART + p * CW


def edge_kernel(x_hbm, step_hbm, to_core_ref, to_chip_ref, step_ref, sems):
    c, z, y = place()
    far = columns((1 - c) * HALF, HALF)
    ends = pl.ds(pl.multiple_of(c * (TOK - HALO), HALO), HALO)
    copies = copy_all(
        [
            (step_hbm, step_ref),
            (x_hbm.at[ends], to_chip_ref),
            (x_hbm.at[:, far], to_core_ref.at[:, 0:HALF]),
            (x_hbm.at[:, INNER:E], to_core_ref.at[:, HALF:WIDE]),
        ],
        sems,
    )
    copies[0].wait()
    step = jnp.transpose(step_ref[...])
    p0 = step.astype(BF16).astype(F32)
    p1 = (step - p0).astype(BF16).astype(F32)
    p2 = step - p0 - p1
    to_core_ref[:, WIDE : WIDE + STEPS] = jnp.concatenate([p0, p1, p2, jnp.zeros_like(p0)], axis=1).astype(BF16)
    for copy in copies[1:]:
        copy.wait()


def halo_kernel(halo_ref, after_ref, mine_ref, to_core_ref):
    c, z, y = place()
    for ref, half in ((mine_ref, c), (to_core_ref, 1 - c)):
        ref[:, 0:HALF] = halo_ref[:, columns(half * HALF, HALF)]
        ref[:, HALF:WIDE] = halo_ref[:, INNER:E]


def conv_piece(x_ref, taps_ref, u_ref, start, halo=None):
    def body(i, _):
        at = columns(start + i * 128, 128)
        cols = columns(i * 128, 128)
        cf, cr = taps_ref[0:4, at], taps_ref[4:8, at]
        x0, x1 = x_ref[0, :, at].astype(F32), x_ref[1, :, at].astype(F32)
        before, after = halo(at) if halo else (x0[0:8], x1[TOK - 8 :])
        for b, rows in enumerate(((before, x0, x1[0:8]), (x0[TOK - 8 :], x1, after))):
            h, g = conv(jnp.concatenate(rows, axis=0), cf, cr)
            u_ref[b, 0, :, cols] = silu_of_half(h[8 : TOK + 8])
            u_ref[b, 1, :, cols] = silu_of_half(g[8 : TOK + 8])
        return _

    lax.fori_loop(0, u_ref.shape[3] // 128, body, 0)


def halo_of(chip_ref, core_ref):
    def rows(at):
        c, z, y = place()
        chip, core = chip_ref[:, at].astype(F32), core_ref[:, at].astype(F32)
        before, after = jnp.where(c == 0, chip, core), jnp.where(c == 0, core, chip)
        return before[HALO - 8 :], after[:8]

    return rows


def repair(x_ref, taps_ref, u_ref, start, halo):
    def body(i, _):
        at = columns(start + i * 256, 256)
        cols = columns(i * 256, 256)
        cf, cr = taps_ref[0:4, at], taps_ref[4:8, at]
        before, after = halo(at)
        h, _g = conv(jnp.concatenate([before, x_ref[0, 0:HALO, at].astype(F32)], axis=0), cf, cr)
        u_ref[0, 0, 0:HALO, cols] = silu_of_half(h[8:])
        _h, g = conv(jnp.concatenate([x_ref[1, TOK - HALO : TOK, at].astype(F32), after], axis=0), cf, cr)
        u_ref[1, 1, TOK - HALO : TOK, cols] = silu_of_half(g[:HALO])
        return _

    lax.fori_loop(0, u_ref.shape[3] // 256, body, 0)


def front_kernel(
    other_ref, x_hbm, step_hbm, decay_hbm, skip_hbm, cf_hbm, cr_hbm,
    x_ref, table_ref, mcol_ref, mrow_ref, drow_ref, taps_ref, kq_ref, u_ref,
    step_ref, decay_ref, skip_ref, cf_ref, cr_ref, sems,
):
    c, z, y = place()
    half = columns(c * HALF, HALF)
    copies = copy_all(
        [
            (step_hbm, step_ref),
            (decay_hbm, decay_ref),
            (skip_hbm, skip_ref),
            (x_hbm.at[:, half], x_ref.at[c, :, 0:HALF]),
            (x_hbm.at[:, INNER:E], x_ref.at[c, :, HALF:WIDE]),
            (cf_hbm.at[:, half], cf_ref.at[:, 0:HALF]),
            (cf_hbm.at[:, INNER:E], cf_ref.at[:, HALF:WIDE]),
            (cr_hbm.at[:, half], cr_ref.at[:, 0:HALF]),
            (cr_hbm.at[:, INNER:E], cr_ref.at[:, HALF:WIDE]),
            (other_ref.at[:, 0:WIDE], x_ref.at[1 - c]),
        ],
        sems,
    )
    for copy in copies[:3]:
        copy.wait()
    def half_of(values):
        return jnp.where(c == 0, values[:, 0 : HEADS // 2], values[:, HEADS // 2 : HEADS])

    parts = other_ref[:, WIDE : WIDE + STEPS].astype(F32)
    other = half_of(parts[:, 0:HEADS] + parts[:, HEADS : 2 * HEADS] + parts[:, 2 * HEADS : 3 * HEADS])
    mine = half_of(jnp.transpose(step_ref[...]))
    step = jnp.concatenate([jnp.where(c == 0, mine, other), jnp.where(c == 0, other, mine)], axis=1)
    decay, skip = half_of(decay_ref[...]), half_of(skip_ref[...])
    decay, skip = jnp.concatenate([decay, decay], axis=1), jnp.concatenate([skip, skip], axis=1)
    make_tables(step, decay, skip, table_ref, mcol_ref, mrow_ref, drow_ref)
    for copy in copies[3:]:
        copy.wait()
    taps_ref[0:4] = cf_ref[...] * 0.5
    taps_ref[4:8] = cr_ref[...] * 0.5
    conv_piece(x_ref, taps_ref, kq_ref, HALF)
    conv_piece(x_ref, taps_ref, u_ref, start_of(2, 0))


def piece_states(u_ref, kt_ref, table_ref, drow_ref, start, saved_ref, spread_ref, chip_ref):
    blocks = []
    for b in range(2):
        spread = spread_matrix(b * HALF + start)
        spread_ref[b] = spread
        drow = dot(drow_ref[...], spread)
        d0, d1 = drow[8:9], drow[9:10]

        weights = expand(table_ref, WF, spread)

        def weighted(d, r):
            return (u_ref[b, d, r : r + SUB].astype(F32) * weights[d][r : r + SUB]).astype(BF16)

        f0 = dot(kt_ref[b, 0, :, 0:SUB], weighted(0, 0))
        f1 = dot(kt_ref[b, 0, :, SUB:TOK], weighted(0, SUB))
        r0 = dot(kt_ref[b, 1, :, 0:SUB], weighted(1, 0))
        r1 = dot(kt_ref[b, 1, :, SUB:TOK], weighted(1, SUB))
        saved_ref[2 * b] = f0.astype(BF16)
        saved_ref[2 * b + 1] = r1.astype(BF16)
        blocks.append((d1 * f0 + f1, r0 + d0 * r1, drow[0:1] + drow[1:2]))
    (f0, r0, d0), (f1, r1, d1) = blocks
    saved_ref[4] = f0.astype(BF16)
    saved_ref[5] = r1.astype(BF16)
    chip_ref[0:STATE] = (d1 * f0 + f1).astype(BF16)
    chip_ref[STATE : 2 * STATE] = (r0 + d0 * r1).astype(BF16)
    chip_ref[2 * STATE : MSG] = decay_rows(d0 * d1)


def first_states_kernel(
    kq_in, u_in, x_ref, taps_ref, chip_halo_ref, core_halo_ref, table_ref, drow_ref, gate_hbm,
    kq_ref, u_ref, kt_ref, saved_ref, spread_ref, chip_ref, gate_to_core_ref, sem,
):
    c, z, y = place()
    copy = pltpu.make_async_copy(gate_hbm.at[:, columns((1 - c) * HALF, HALF)], gate_to_core_ref, sem)
    copy.start()
    halo = halo_of(chip_halo_ref, core_halo_ref)
    repair(x_ref, taps_ref, kq_ref, HALF, halo)
    for b in range(2):
        for d in range(2):
            kt_ref[b, d] = jnp.transpose(kq_ref[b, d, :, 0:STATE].astype(F32)).astype(BF16)
    start = start_of(2, 0)
    repair(x_ref, taps_ref, u_ref, start, halo)
    piece_states(u_ref, kt_ref, table_ref, drow_ref, start, saved_ref, spread_ref, chip_ref)
    copy.wait()


def rest_kernel(todo, x_ref, taps_ref, chip_halo_ref, core_halo_ref, table_ref, drow_ref, kt_ref, after_ref, *outs):
    c, z, y = place()
    copies = []
    if len(todo) == 2:
        gate_hbm, gain_hbm, *outs, gate_ref, gain_ref, sems = outs
        copies = copy_all([(gate_hbm.at[:, columns(c * HALF, HALF)], gate_ref), (gain_hbm, gain_ref)], sems)
    for n, piece in enumerate(todo):
        u_ref, saved_ref, spread_ref, chip_ref = outs[4 * n : 4 * n + 4]
        conv_piece(x_ref, taps_ref, u_ref, start_of(*piece), halo_of(chip_halo_ref, core_halo_ref))
        piece_states(u_ref, kt_ref, table_ref, drow_ref, start_of(*piece), saved_ref, spread_ref, chip_ref)
    for copy in copies:
        copy.wait()


KEYS = vmem(BF16, 2, 2, TOK, 2 * STATE)
U = vmem(BF16, 2, 2, TOK, CW)
SAVED = vmem(BF16, 6, STATE, CW)
SPREAD = vmem(BF16, 2, 2 * HEADS, CW)
CHIP = vmem(BF16, MSG, CW)


def group(keep_ref, got_ref, outs):
    c, z, y = place()
    z0 = z == 0
    dm, do = read_decay(keep_ref[2 * STATE : MSG]), read_decay(got_ref[2 * STATE : MSG])
    one = jnp.ones_like(dm)
    am, ao = jnp.where(z0, do, one), jnp.where(z0, one, dm)
    fwd = (am * keep_ref[0:STATE].astype(F32) + ao * got_ref[0:STATE].astype(F32)).astype(BF16)
    am, ao = jnp.where(z0, one, do), jnp.where(z0, dm, one)
    rows = slice(STATE, 2 * STATE)
    rev = (am * keep_ref[rows].astype(F32) + ao * got_ref[rows].astype(F32)).astype(BF16)
    decay = decay_rows(dm * do)
    for k in range(1, 4):
        outs[k - 1][0:STATE] = jnp.where(y + k < 4, fwd, rev)
        outs[k - 1][STATE:YMSG] = decay


def entries(keep_ref, got_ref, r1_ref, r2_ref, r3_ref, mine_ref, back_ref):
    c, z, y = place()
    z0 = z == 0
    r = [ref[0:STATE].astype(F32) for ref in (r1_ref, r2_ref, r3_ref)]
    d = [read_decay(ref[STATE:YMSG]) for ref in (r1_ref, r2_ref, r3_ref)]
    zero = jnp.zeros_like(r[0])
    ef = jnp.where(y >= 3, r[2], zero)
    ef = jnp.where(y >= 2, r[1] + d[1] * ef, zero)
    ef = jnp.where(y >= 1, r[0] + d[0] * ef, zero)
    er = jnp.where(y <= 0, r[0], zero)
    er = jnp.where(y <= 1, r[1] + d[1] * er, zero)
    er = jnp.where(y <= 2, r[2] + d[2] * er, zero)
    dm, do = read_decay(keep_ref[2 * STATE : MSG]), read_decay(got_ref[2 * STATE : MSG])
    df = jnp.where(z0, dm, do)
    tf = jnp.where(z0, keep_ref[0:STATE].astype(F32), got_ref[0:STATE].astype(F32))
    second_f = df * ef + tf
    dr = jnp.where(z0, do, dm)
    rows = slice(STATE, 2 * STATE)
    tr = jnp.where(z0, got_ref[rows].astype(F32), keep_ref[rows].astype(F32))
    first_r = dr * er + tr
    mine_ref[0] = jnp.where(z0, ef, second_f).astype(BF16)
    mine_ref[1] = jnp.where(z0, first_r, er).astype(BF16)
    back_ref[0] = jnp.where(z0, second_f, ef).astype(BF16)
    back_ref[1] = jnp.where(z0, er, first_r).astype(BF16)


def group_kernel(keep_ref, got_ref, *refs):
    group(keep_ref, got_ref, refs[-3:])


def entries_kernel(keep_ref, got_ref, r1_ref, r2_ref, r3_ref, *refs):
    entries(keep_ref, got_ref, r1_ref, r2_ref, r3_ref, *refs[-2:])


def within_kernel(k, p, u_ref, spread_ref, kq_ref, table_ref, mcol_ref, mrow_ref, drow_ref, after_ref, *refs):
    make_qk = len(refs) == 2 and refs[1].shape[0] == 2 and len(refs[1].shape) == 5
    qk_ref, out_ref = (refs[1], refs[0]) if make_qk else refs
    row = lax.broadcasted_iota(jnp.int32, (SUB, SUB), 0)
    col = lax.broadcasted_iota(jnp.int32, (SUB, SUB), 1)
    low = lax.broadcasted_iota(jnp.int32, (SUB, 2 * HEAD_DIM), 1) < HEAD_DIM

    def block(b, _):
        if make_qk:
            for s in range(2):
                rows = slice(s * SUB, (s + 1) * SUB)
                for d in range(2):
                    keys = kq_ref[b, d, rows, 0:STATE]
                    queries = kq_ref[b, d, rows, STATE : 2 * STATE]
                    prod = lax.dot_general(queries, keys, (((1,), (1,)), ((), ())), preferred_element_type=F32)
                    qk_ref[b, d, s] = jnp.where((row >= col) if d == 0 else (row <= col), prod, 0.0)
        start = b * HALF + start_of(k, p)
        first = start // HEAD_DIM
        spread = spread_ref[b]
        skip = dot(drow_ref[...], spread)[10:11]
        mcol = pltpu.roll(mcol_ref[...], 2 * HEADS - first, 1)
        mrow = mrow_ref[pl.ds(pl.multiple_of(first, HC), HC), :]
        wv, gt = expand(table_ref, WV, spread)
        for s in range(2):
            rows = slice(s * SUB, (s + 1) * SUB)
            for two in range(HC // 2):
                cols = slice(two * 128, (two + 1) * 128)
                up = u_ref[b, 0, rows, cols].astype(F32)
                xf = (up * wv[rows, cols]).astype(BF16)
                xb = (u_ref[b, 1, rows, cols].astype(F32) * wv[rows, cols]).astype(BF16)
                none = jnp.zeros_like(xf)
                left, right = [], []
                for h in range(2):
                    at = two * 2 + h
                    diff = mcol[rows, at : at + 1] - mrow[at : at + 1, rows]
                    decay = jnp.exp2(-jnp.abs(diff))
                    left += [(decay * qk_ref[b, 0, s]).astype(BF16), (decay * qk_ref[b, 1, s]).astype(BF16)]
                    keep = low if h == 0 else ~low
                    right += [jnp.where(keep, xf, none), jnp.where(keep, xb, none)]
                res = dot(jnp.concatenate(left, axis=1), jnp.concatenate(right, axis=0))
                out_ref[b, rows, cols] = (res * gt[rows, cols] + up * skip[:, cols]).astype(BF16)
        return _

    lax.fori_loop(0, 2, block, 0)


QK = vmem(F32, 2, 2, 2, SUB, SUB)


def make_within(k, p, u, spread, kq, table, mcol, mrow, drow, after, qk=None):
    outs = [vmem(BF16, 2, TOK, CW)]
    operands = (u, spread, kq, table, mcol, mrow, drow, after)
    kernel = functools.partial(within_kernel, k, p)
    if qk is None:
        return call(kernel, f"within_{k}{p}", [*outs, QK], operands)
    return call(kernel, f"within_{k}{p}", outs, (*operands, qk))[0]


def finish_part(k, p, other, entry_ref, saved_ref, spread_ref, within_ref, gate_ref, kq_ref, table_ref, drow_ref, put, square):
    c, z, y = place()
    b = 1 - c if other else c
    start = start_of(k, p)
    at = columns(start, CW)
    spread = spread_ref[b]
    drow = dot(drow_ref[...], spread)
    d0, d1 = drow[8:9], drow[9:10]
    far = dot(drow_ref[...], spread_ref[1 - b])
    far = far[0:1] + far[1:2]
    one = jnp.ones_like(far)
    none = jnp.zeros((STATE, CW), F32)
    first = b == 0
    ef = jnp.where(first, one, far) * entry_ref[0].astype(F32) + jnp.where(first, none, saved_ref[4].astype(F32))
    er = jnp.where(first, far, one) * entry_ref[1].astype(F32) + jnp.where(first, saved_ref[5].astype(F32), none)
    inside = [
        (ef.astype(BF16), (er * d1 + saved_ref[2 * b + 1].astype(F32)).astype(BF16)),
        ((ef * d0 + saved_ref[2 * b].astype(F32)).astype(BF16), er.astype(BF16)),
    ]
    gf, gr = expand(table_ref, GF, spread)
    for s in range(2):
        rows = slice(s * SUB, (s + 1) * SUB)
        cf = dot(kq_ref[b, 0, rows, STATE : 2 * STATE], inside[s][0])
        cr = dot(kq_ref[b, 1, rows, STATE : 2 * STATE], inside[s][1])
        mixed = within_ref[b, rows].astype(F32) + gf[rows] * cf + gr[rows] * cr
        half = gate_ref[rows, at].astype(F32) * 0.5
        gated = mixed * (half + half * jnp.tanh(half))
        put(rows, gated)
        sq = gated * gated
        for j in range(0, CW, 128):
            part = sq[:, j : j + 128]
            square[s] = part if square[s] is None else square[s] + part


def finish_piece(k, p, entry_ref, saved_ref, spread_ref, within_ref, gates, shared, own_ref, msg_refs, squares):
    def put_own(rows, gated):
        own_ref[rows] = gated

    def put_other(rows, gated):
        msg_refs[rows.start // SUB][:, 0:CW] = gated.astype(BF16)

    for other, put in ((1, put_other), (0, put_own)):
        finish_part(k, p, other, entry_ref, saved_ref, spread_ref, within_ref, gates[other], *shared, put, squares[other])


NEAR = ((3, 0), (3, 1), (2, 0))
BACK = (2, 1)


def finish_near_kernel(k, p, entry_ref, saved_ref, spread_ref, within_ref, gate_ref, gate_other_ref, *refs):
    shared, (square_in, own_ref, *msg_refs, square_ref) = refs[:3], refs[3:]
    squares = [[None, None], [None, None]]
    gates = (gate_ref, gate_other_ref)
    finish_piece(k, p, entry_ref, saved_ref, spread_ref, within_ref, gates, shared, own_ref, msg_refs, squares)
    for other in range(2):
        for s in range(2):
            rows = slice(s * SUB, (s + 1) * SUB)
            if (k, p) == NEAR[0]:
                square_ref[other, rows] = squares[other][s]
            else:
                square_ref[other, rows] = square_in[other, rows] + squares[other][s]


def finish_other_kernel(entry_ref, saved_ref, spread_ref, within_ref, gate_ref, *refs):
    shared, square_in, msg_refs = refs[:3], refs[3], refs[-2:]
    square = [square_in[1, s * SUB : (s + 1) * SUB] for s in range(2)]

    def put(rows, gated):
        msg_refs[rows.start // SUB][:, 0:CW] = gated.astype(BF16)

    finish_part(*BACK, 1, entry_ref, saved_ref, spread_ref, within_ref, gate_ref, *shared, put, square)
    lane = lax.broadcasted_iota(jnp.int32, (SUB, 128), 1)
    for s in range(2):
        total = jnp.sum(square[s], axis=1, keepdims=True)
        hi = total.astype(BF16).astype(F32)
        sums = jnp.where(lane == 0, hi, jnp.where(lane == 1, total - hi, 0.0))
        msg_refs[s][:, CW : CW + 128] = sums.astype(BF16)


def finish_own_kernel(entry_ref, saved_ref, spread_ref, within_ref, gate_ref, *refs):
    shared, (square_in, after_ref, own_ref, square_ref) = refs[:3], refs[3:]
    square = [square_in[0, s * SUB : (s + 1) * SUB] for s in range(2)]

    def put(rows, gated):
        own_ref[rows] = gated

    finish_part(*BACK, 0, entry_ref, saved_ref, spread_ref, within_ref, gate_ref, *shared, put, square)
    for s in range(2):
        square_ref[s * SUB : (s + 1) * SUB] = square[s]


def norm_kernel(*refs):
    own_refs, other_refs, (square_ref, gain_ref, out_hbm, out_ref, sems) = refs[:4], refs[4:12], refs[12:]
    c, z, y = place()
    pieces = []
    for n, piece in enumerate((*NEAR, BACK)):
        pieces.append(((own_refs[n], own_refs[n].at[SUB:TOK]), c * HALF + start_of(*piece)))
        pieces.append((other_refs[2 * n : 2 * n + 2], (1 - c) * HALF + start_of(*piece)))
    step = 32
    copies = []
    for r in range(0, TOK, step):
        rows, inside = slice(r, r + step), slice(r % SUB, r % SUB + step)
        total = square_ref[rows] + other_refs[6 + r // SUB][inside, CW : CW + 128].astype(F32)
        scale = lax.rsqrt(jnp.sum(total, axis=1, keepdims=True) * (1.0 / INNER) + 1e-05)
        for refs, start in pieces:
            at = columns(start, CW)
            out_ref[rows, at] = (refs[r // SUB][inside, 0:CW].astype(F32) * scale * gain_ref[:, at]).astype(BF16)
        copies.append(pltpu.make_async_copy(out_ref.at[rows], out_hbm.at[rows], sems.at[len(copies)]))
        copies[-1].start()
    for copy in copies:
        copy.wait()


def per_device(mixer_input, gate_input, conv_forward, conv_reverse, step_size, decay_rate, skip_scale, norm_gain):
    n = lax.axis_size("seq")

    def send(v, perm):
        return lax.ppermute(v, "seq", perm)

    core = [(i, i ^ 1) for i in range(n)]
    zswap = [(i, i ^ 2) for i in range(n)]
    chips = [(i, i + 1) for i in range(1, n - 1, 2)] + [(i + 1, i) for i in range(1, n - 1, 2)]

    def along_y(msgs):
        return [send(m, [(i, (i + 4 * k) % n) for i in range(n)]) for k, m in enumerate(msgs, 1)]

    to_core, to_chip = call(
        edge_kernel,
        "edges",
        [vmem(BF16, TOK, WIDE + STEPS), vmem(BF16, HALO, E)],
        (),
        (mixer_input, step_size),
        [pltpu.VMEM((HEADS, TOK), F32), pltpu.SemaphoreType.DMA((4,))],
    )
    x, table, mcol, mrow, drow, taps, kq, u2a = call(
        front_kernel,
        "front",
        [
            vmem(BF16, 2, TOK, WIDE),
            vmem(BF16, 6, TOK, 2 * HEADS),
            vmem(F32, TOK, 2 * HEADS),
            vmem(F32, HEADS, TOK),
            vmem(BF16, 16, 2 * HEADS),
            vmem(F32, 8, WIDE),
            KEYS,
            U,
        ],
        (send(to_core, core),),
        (
            mixer_input,
            step_size,
            decay_rate.reshape(1, HEADS),
            skip_scale.reshape(1, HEADS),
            conv_forward,
            conv_reverse,
        ),
        [
            pltpu.VMEM((HEADS, TOK), F32),
            pltpu.VMEM((1, HEADS), F32),
            pltpu.VMEM((1, HEADS), F32),
            pltpu.VMEM((4, WIDE), F32),
            pltpu.VMEM((4, WIDE), F32),
            pltpu.SemaphoreType.DMA((10,)),
        ],
    )
    chip_halo, to_core = call(
        halo_kernel, "halo", [vmem(BF16, HALO, WIDE)] * 2, (send(to_chip, chips), kq)
    )
    halo = (x, taps, chip_halo, send(to_core, core))
    kq, u2a, kt, saved2a, spread2a, zsend0, gate_to_core = call(
        first_states_kernel,
        "states_first",
        [KEYS, U, vmem(BF16, 2, 2, STATE, TOK), SAVED, SPREAD, CHIP, vmem(BF16, TOK, HALF)],
        (kq, u2a, *halo, table, drow),
        (gate_input,),
        [pltpu.SemaphoreType.DMA(())],
        aliases={0: 0, 1: 1},
    )
    got0 = send(zsend0, zswap)

    def make_rest(name, todo, after):
        kernel = functools.partial(rest_kernel, todo)
        outs = [U, SAVED, SPREAD, CHIP] * len(todo)
        if len(todo) == 1:
            return call(kernel, name, outs, (*halo, table, drow, kt, after))
        outs += [vmem(BF16, TOK, HALF), vmem(F32, 1, INNER)]
        sems = [pltpu.SemaphoreType.DMA((2,))]
        params = (gate_input, norm_gain.reshape(1, INNER))
        return call(kernel, name, outs, (*halo, table, drow, kt, after), params, sems)

    u2b, saved2b, spread2b, zsend1, u3a, saved3a, spread3a, keep0, gate, gain = make_rest(
        "states_a", ((2, 1), (3, 0)), zsend0
    )
    got1 = send(zsend1, zswap)
    u3b, saved3b, spread3b, keep1 = make_rest("states_b", ((3, 1),), zsend1)
    gates = (gate, send(gate_to_core, core))
    tables = (kq, table, mcol, mrow, drow)
    yout = [vmem(BF16, YMSG, CW)] * 3
    entry = vmem(BF16, 2, STATE, CW)

    msgs = call(group_kernel, "group_a", yout, (keep0, got0, keep1, gates[1]))
    arrived0 = along_y(msgs)
    w2a, qk = make_within(2, 0, u2a, spread2a, *tables, msgs[0])
    msgs = call(group_kernel, "group_b", yout, (keep1, got1, w2a))
    arrived1 = along_y(msgs)
    mine0, back0 = call(entries_kernel, "entries_a", [entry, entry], (keep0, got0, *arrived0, msgs[0]))
    back0 = send(back0, zswap)
    w3a = make_within(3, 0, u3a, spread3a, *tables, mine0, qk)
    mine1, back1 = call(entries_kernel, "entries_b", [entry, entry], (keep1, got1, *arrived1, w3a))
    back1 = send(back1, zswap)
    w3b = make_within(3, 1, u3b, spread3b, *tables, mine1, qk)
    w2b = make_within(2, 1, u2b, spread2b, *tables, mine1, qk)
    shared = (kq, table, drow)
    square = kt
    own, other = [], []
    parts = (
        (mine0, saved3a, spread3a, w3a),
        (mine1, saved3b, spread3b, w3b),
        (back0, saved2a, spread2a, w2a),
    )
    for (k, p), part in zip(NEAR, parts):
        gated, *msg, square = call(
            functools.partial(finish_near_kernel, k, p),
            f"finish_{k}{p}",
            [vmem(F32, TOK, CW), vmem(BF16, SUB, CW), vmem(BF16, SUB, CW), vmem(F32, 2, TOK, 128)],
            (*part, *gates, *shared, square),
        )
        own.append(gated)
        other += [send(m, core) for m in msg]
    msg = call(
        finish_other_kernel,
        "finish_other",
        [vmem(BF16, SUB, CW + 128)] * 2,
        (back1, saved2b, spread2b, w2b, *gates[1:], *shared, square, *other[:4]),
    )
    other += [send(m, core) for m in msg]
    gated, square = call(
        finish_own_kernel,
        "finish_own",
        [vmem(F32, TOK, CW), vmem(F32, TOK, 128)],
        (back1, saved2b, spread2b, w2b, gates[0], *shared, square, msg[0]),
    )
    own.append(gated)
    (out,) = call(
        norm_kernel,
        "norm",
        [shape(BF16, TOK, INNER)],
        (*own, *other, square, gain),
        (),
        [pltpu.VMEM((TOK, INNER), BF16), pltpu.SemaphoreType.DMA((8,))],
    )
    return out


def solution(mesh):
    in_specs = (
        P(("row", "seq"), None),
        P(("row", "seq"), None),
        P(),
        P(),
        P(None, ("row", "seq")),
        P("row"),
        P(),
        P(),
    )
    out_specs = P(("row", "seq"), None)
    return jax.shard_map(per_device, mesh=mesh, in_specs=in_specs, out_specs=out_specs, check_vma=False)
```

```python
import functools

import jax
import jax.numpy as jnp
from jax import lax
from jax.experimental import pallas as pl
from jax.experimental.pallas import tpu as pltpu
from jax.sharding import PartitionSpec as P

HEADS = 64
HEAD_DIM = 64
STATE = 128
TOK = 256
SUB = 128
INNER = 4096
E = 4352
HALF = INNER // 2
QUART = INNER // 4
WIDE = HALF + 2 * STATE
STEPS = 256
CW = 512
HC = CW // HEAD_DIM
HALO = 16
MSG = 2 * STATE + 16
YMSG = STATE + 16
LOG2E = 1.4426950408889634
F32 = jnp.float32
BF16 = jnp.bfloat16
WF, WR, GF, GR, WV, GT = range(6)
MIB = 2**20


def dot(a, b, **kw):
    return jnp.dot(a, b, preferred_element_type=F32, **kw)


def shape(dtype, *dims):
    return jax.ShapeDtypeStruct(dims, dtype)


VMEM = pl.BlockSpec(memory_space=pltpu.VMEM)
HBM = pl.BlockSpec(memory_space=pltpu.HBM)


def vmem(dtype, *dims):
    return pltpu.VMEM(dims, dtype)


def call(kernel, name, outs, operands, params=(), scratch=(), limit=12, us=1.0, aliases=None):
    operands = [pltpu.with_memory_space_constraint(v, pltpu.VMEM) for v in operands]
    params = [pltpu.with_memory_space_constraint(v, pltpu.HBM) for v in params]
    return pl.pallas_call(
        kernel,
        name=name,
        in_specs=[VMEM] * len(operands) + [HBM] * len(params),
        out_specs=[HBM if isinstance(o, jax.ShapeDtypeStruct) else VMEM for o in outs],
        out_shape=outs,
        scratch_shapes=list(scratch),
        input_output_aliases=aliases or {},
        compiler_params=pltpu.CompilerParams(vmem_limit_bytes=limit * MIB),
        cost_estimate=pl.CostEstimate(flops=int(us * 1e8), bytes_accessed=int(us * 3e5), transcendentals=0),
    )(*operands, *params)


def place():
    at = lax.axis_index("seq")
    return at & 1, (at >> 1) & 1, at >> 2


def columns(start, width):
    return pl.ds(pl.multiple_of(start, 128), width)


def split2(x):
    hi = x.astype(BF16)
    lo = (x - hi.astype(F32)).astype(BF16)
    return hi, lo


def spread_matrix(start, width=CW):
    k = lax.broadcasted_iota(jnp.int32, (2 * HEADS, width), 0)
    col = lax.broadcasted_iota(jnp.int32, (2 * HEADS, width), 1)
    low = (k & (HEADS - 1)) * HEAD_DIM - start
    return jnp.where((col >= low) & (col < low + HEAD_DIM), 1.0, 0.0).astype(BF16)


def expand(table_ref, first, spread):
    both = dot(table_ref[first : first + 2].reshape(2 * TOK, 2 * HEADS), spread)
    return both[0:TOK], both[TOK:]


def read_decay(rows):
    rows = rows.astype(F32)
    return rows[0:1] + rows[1:2]


def decay_rows(d):
    hi, lo = split2(d)
    none = jnp.zeros((14, d.shape[1]), F32)
    return jnp.concatenate([hi.astype(F32), lo.astype(F32), none], axis=0).astype(BF16)


def make_tables(step, decay, skip, table_ref, mcol_ref, mrow_ref, drow_ref):
    a = -decay * step
    row = lax.broadcasted_iota(jnp.int32, (TOK, TOK), 0)
    col = lax.broadcasted_iota(jnp.int32, (TOK, TOK), 1)
    tri = jnp.where((row >= col) & ((row >= SUB) == (col >= SUB)), 1.0, 0.0).astype(BF16)
    p0 = a.astype(BF16)
    p1 = (a - p0.astype(F32)).astype(BF16)
    p2 = (a - p0.astype(F32) - p1.astype(F32)).astype(BF16)
    sums = dot(tri, jnp.concatenate([p0, p1, p2, jnp.zeros_like(p0)], axis=1))
    cum = sums[:, 0:HEADS] + sums[:, HEADS : 2 * HEADS] + sums[:, 2 * HEADS : 3 * HEADS]
    excl = cum - a
    e0 = cum[SUB - 1 : SUB]
    e1 = cum[TOK - 1 : TOK]
    ends = jnp.concatenate([jnp.broadcast_to(e0, (SUB, HEADS)), jnp.broadcast_to(e1, (SUB, HEADS))], axis=0)
    zero = jnp.zeros_like(cum)

    def put(at, value):
        hi, lo = split2(value)
        table_ref[at] = jnp.concatenate([hi, lo], axis=1)

    put(WF, step * jnp.exp(jnp.minimum(ends - cum, zero)))
    put(WR, step * jnp.exp(excl))
    put(GF, jnp.exp(cum))
    put(GR, jnp.exp(jnp.minimum(ends - excl, zero)))
    put(WV, step * jnp.exp(-0.5 * a))
    put(GT, jnp.exp(0.5 * a))
    m = (cum - 0.5 * a) * LOG2E
    mcol_ref[...] = jnp.concatenate([m, zero], axis=1)
    mrow_ref[...] = jnp.transpose(m)
    h0, l0 = split2(jnp.exp(e0))
    h1, l1 = split2(jnp.exp(e1))
    hd, ld = split2(jnp.exp(e0 + e1))
    hs, ls = split2(skip)
    no = jnp.zeros_like(h0)
    wide = [
        jnp.concatenate([hd, no], axis=1).astype(F32),
        jnp.concatenate([no, ld], axis=1).astype(F32),
        jnp.zeros((6, 2 * HEADS), F32),
        jnp.concatenate([h0, l0], axis=1).astype(F32),
        jnp.concatenate([h1, l1], axis=1).astype(F32),
        jnp.concatenate([hs, ls], axis=1).astype(F32),
        jnp.zeros((5, 2 * HEADS), F32),
    ]
    drow_ref[...] = jnp.concatenate(wide, axis=0).astype(BF16)


def conv(x, cf, cr):
    rows = x.shape[0]
    back = pltpu.roll(x, 1, 0)
    fore = pltpu.roll(x, rows - 1, 0)
    h = cf[3:4] * x + cf[2:3] * back + pltpu.roll(cf[1:2] * x + cf[0:1] * back, 2, 0)
    g = cr[3:4] * x + cr[2:3] * fore + pltpu.roll(cr[1:2] * x + cr[0:1] * fore, rows - 2, 0)
    return h, g


def silu_of_half(h):
    return (h + h * jnp.tanh(h)).astype(BF16)


def copy_all(pairs, sems):
    copies = [pltpu.make_async_copy(src, dst, sems.at[k]) for k, (src, dst) in enumerate(pairs)]
    for copy in copies:
        copy.start()
    return copies


def start_of(k, p):
    c, z, y = place()
    return (z if k == 3 else 1 - z) * QUART + p * CW


def edge_kernel(x_hbm, step_hbm, to_core_ref, to_chip_ref, step_ref, sems):
    c, z, y = place()
    far = columns((1 - c) * HALF, HALF)
    ends = pl.ds(pl.multiple_of(c * (TOK - HALO), HALO), HALO)
    copies = copy_all(
        [
            (step_hbm, step_ref),
            (x_hbm.at[ends], to_chip_ref),
            (x_hbm.at[:, far], to_core_ref.at[:, 0:HALF]),
            (x_hbm.at[:, INNER:E], to_core_ref.at[:, HALF:WIDE]),
        ],
        sems,
    )
    copies[0].wait()
    step = jnp.transpose(step_ref[...])
    p0 = step.astype(BF16).astype(F32)
    p1 = (step - p0).astype(BF16).astype(F32)
    p2 = step - p0 - p1
    to_core_ref[:, WIDE : WIDE + STEPS] = jnp.concatenate([p0, p1, p2, jnp.zeros_like(p0)], axis=1).astype(BF16)
    for copy in copies[1:]:
        copy.wait()


def halo_kernel(halo_ref, after_ref, mine_ref, to_core_ref):
    c, z, y = place()
    for ref, half in ((mine_ref, c), (to_core_ref, 1 - c)):
        ref[:, 0:HALF] = halo_ref[:, columns(half * HALF, HALF)]
        ref[:, HALF:WIDE] = halo_ref[:, INNER:E]


def conv_piece(x_ref, taps_ref, u_ref, start, halo=None):
    def body(i, _):
        at = columns(start + i * 128, 128)
        cols = columns(i * 128, 128)
        cf, cr = taps_ref[0:4, at], taps_ref[4:8, at]
        x0, x1 = x_ref[0, :, at].astype(F32), x_ref[1, :, at].astype(F32)
        before, after = halo(at) if halo else (x0[0:8], x1[TOK - 8 :])
        for b, rows in enumerate(((before, x0, x1[0:8]), (x0[TOK - 8 :], x1, after))):
            h, g = conv(jnp.concatenate(rows, axis=0), cf, cr)
            u_ref[b, 0, :, cols] = silu_of_half(h[8 : TOK + 8])
            u_ref[b, 1, :, cols] = silu_of_half(g[8 : TOK + 8])
        return _

    lax.fori_loop(0, u_ref.shape[3] // 128, body, 0)


def halo_of(chip_ref, core_ref):
    def rows(at):
        c, z, y = place()
        chip, core = chip_ref[:, at].astype(F32), core_ref[:, at].astype(F32)
        before, after = jnp.where(c == 0, chip, core), jnp.where(c == 0, core, chip)
        return before[HALO - 8 :], after[:8]

    return rows


def repair(x_ref, taps_ref, u_ref, start, halo):
    def body(i, _):
        at = columns(start + i * 256, 256)
        cols = columns(i * 256, 256)
        cf, cr = taps_ref[0:4, at], taps_ref[4:8, at]
        before, after = halo(at)
        h, _g = conv(jnp.concatenate([before, x_ref[0, 0:HALO, at].astype(F32)], axis=0), cf, cr)
        u_ref[0, 0, 0:HALO, cols] = silu_of_half(h[8:])
        _h, g = conv(jnp.concatenate([x_ref[1, TOK - HALO : TOK, at].astype(F32), after], axis=0), cf, cr)
        u_ref[1, 1, TOK - HALO : TOK, cols] = silu_of_half(g[:HALO])
        return _

    lax.fori_loop(0, u_ref.shape[3] // 256, body, 0)


def front_kernel(
    other_ref, x_hbm, step_hbm, decay_hbm, skip_hbm, cf_hbm, cr_hbm,
    x_ref, table_ref, mcol_ref, mrow_ref, drow_ref, taps_ref, kq_ref, u_ref,
    step_ref, decay_ref, skip_ref, cf_ref, cr_ref, sems,
):
    c, z, y = place()
    half = columns(c * HALF, HALF)
    copies = copy_all(
        [
            (step_hbm, step_ref),
            (decay_hbm, decay_ref),
            (skip_hbm, skip_ref),
            (x_hbm.at[:, half], x_ref.at[c, :, 0:HALF]),
            (x_hbm.at[:, INNER:E], x_ref.at[c, :, HALF:WIDE]),
            (cf_hbm.at[:, half], cf_ref.at[:, 0:HALF]),
            (cf_hbm.at[:, INNER:E], cf_ref.at[:, HALF:WIDE]),
            (cr_hbm.at[:, half], cr_ref.at[:, 0:HALF]),
            (cr_hbm.at[:, INNER:E], cr_ref.at[:, HALF:WIDE]),
            (other_ref.at[:, 0:WIDE], x_ref.at[1 - c]),
        ],
        sems,
    )
    for copy in copies[:3]:
        copy.wait()
    def half_of(values):
        return jnp.where(c == 0, values[:, 0 : HEADS // 2], values[:, HEADS // 2 : HEADS])

    parts = other_ref[:, WIDE : WIDE + STEPS].astype(F32)
    other = half_of(parts[:, 0:HEADS] + parts[:, HEADS : 2 * HEADS] + parts[:, 2 * HEADS : 3 * HEADS])
    mine = half_of(jnp.transpose(step_ref[...]))
    step = jnp.concatenate([jnp.where(c == 0, mine, other), jnp.where(c == 0, other, mine)], axis=1)
    decay, skip = half_of(decay_ref[...]), half_of(skip_ref[...])
    decay, skip = jnp.concatenate([decay, decay], axis=1), jnp.concatenate([skip, skip], axis=1)
    make_tables(step, decay, skip, table_ref, mcol_ref, mrow_ref, drow_ref)
    for copy in copies[3:]:
        copy.wait()
    taps_ref[0:4] = cf_ref[...] * 0.5
    taps_ref[4:8] = cr_ref[...] * 0.5
    conv_piece(x_ref, taps_ref, kq_ref, HALF)
    conv_piece(x_ref, taps_ref, u_ref, start_of(2, 0))


def piece_states(u_ref, kt_ref, table_ref, drow_ref, start, saved_ref, spread_ref, chip_ref):
    blocks = []
    for b in range(2):
        spread = spread_matrix(b * HALF + start)
        spread_ref[b] = spread
        drow = dot(drow_ref[...], spread)
        d0, d1 = drow[8:9], drow[9:10]

        weights = expand(table_ref, WF, spread)

        def weighted(d, r):
            return (u_ref[b, d, r : r + SUB].astype(F32) * weights[d][r : r + SUB]).astype(BF16)

        f0 = dot(kt_ref[b, 0, :, 0:SUB], weighted(0, 0))
        f1 = dot(kt_ref[b, 0, :, SUB:TOK], weighted(0, SUB))
        r0 = dot(kt_ref[b, 1, :, 0:SUB], weighted(1, 0))
        r1 = dot(kt_ref[b, 1, :, SUB:TOK], weighted(1, SUB))
        saved_ref[2 * b] = f0.astype(BF16)
        saved_ref[2 * b + 1] = r1.astype(BF16)
        blocks.append((d1 * f0 + f1, r0 + d0 * r1, drow[0:1] + drow[1:2]))
    (f0, r0, d0), (f1, r1, d1) = blocks
    saved_ref[4] = f0.astype(BF16)
    saved_ref[5] = r1.astype(BF16)
    chip_ref[0:STATE] = (d1 * f0 + f1).astype(BF16)
    chip_ref[STATE : 2 * STATE] = (r0 + d0 * r1).astype(BF16)
    chip_ref[2 * STATE : MSG] = decay_rows(d0 * d1)


def first_states_kernel(
    kq_in, u_in, x_ref, taps_ref, chip_halo_ref, core_halo_ref, table_ref, drow_ref, after_ref, gate_hbm,
    kq_ref, u_ref, kt_ref, saved_ref, spread_ref, chip_ref, gate_to_core_ref, sem,
):
    c, z, y = place()
    copy = pltpu.make_async_copy(gate_hbm.at[:, columns((1 - c) * HALF, HALF)], gate_to_core_ref, sem)
    copy.start()
    halo = halo_of(chip_halo_ref, core_halo_ref)
    repair(x_ref, taps_ref, kq_ref, HALF, halo)
    for b in range(2):
        for d in range(2):
            kt_ref[b, d] = jnp.transpose(kq_ref[b, d, :, 0:STATE].astype(F32)).astype(BF16)
    start = start_of(2, 0)
    repair(x_ref, taps_ref, u_ref, start, halo)
    piece_states(u_ref, kt_ref, table_ref, drow_ref, start, saved_ref, spread_ref, chip_ref)
    copy.wait()


def conv_kernel(x_ref, taps_ref, u_ref):
    conv_piece(x_ref, taps_ref, u_ref, start_of(2, 1))


def rest_kernel(todo, x_ref, taps_ref, chip_halo_ref, core_halo_ref, table_ref, drow_ref, kt_ref, after_ref, *outs):
    c, z, y = place()
    copies = []
    if len(todo) == 2:
        _u_in, gate_hbm, gain_hbm, *outs, gate_ref, gain_ref, sems = outs
        copies = copy_all([(gate_hbm.at[:, columns(c * HALF, HALF)], gate_ref), (gain_hbm, gain_ref)], sems)
    for n, piece in enumerate(todo):
        u_ref, saved_ref, spread_ref, chip_ref = outs[4 * n : 4 * n + 4]
        halo = halo_of(chip_halo_ref, core_halo_ref)
        if piece == (2, 1):
            repair(x_ref, taps_ref, u_ref, start_of(*piece), halo)
        else:
            conv_piece(x_ref, taps_ref, u_ref, start_of(*piece), halo)
        piece_states(u_ref, kt_ref, table_ref, drow_ref, start_of(*piece), saved_ref, spread_ref, chip_ref)
    for copy in copies:
        copy.wait()


KEYS = vmem(BF16, 2, 2, TOK, 2 * STATE)
U = vmem(BF16, 2, 2, TOK, CW)
SAVED = vmem(BF16, 6, STATE, CW)
SPREAD = vmem(BF16, 2, 2 * HEADS, CW)
CHIP = vmem(BF16, MSG, CW)


def group(keep_ref, got_ref, outs):
    c, z, y = place()
    z0 = z == 0
    dm, do = read_decay(keep_ref[2 * STATE : MSG]), read_decay(got_ref[2 * STATE : MSG])
    one = jnp.ones_like(dm)
    am, ao = jnp.where(z0, do, one), jnp.where(z0, one, dm)
    fwd = (am * keep_ref[0:STATE].astype(F32) + ao * got_ref[0:STATE].astype(F32)).astype(BF16)
    am, ao = jnp.where(z0, one, do), jnp.where(z0, dm, one)
    rows = slice(STATE, 2 * STATE)
    rev = (am * keep_ref[rows].astype(F32) + ao * got_ref[rows].astype(F32)).astype(BF16)
    decay = decay_rows(dm * do)
    for k in range(1, 4):
        outs[k - 1][0:STATE] = jnp.where(y + k < 4, fwd, rev)
        outs[k - 1][STATE:YMSG] = decay


def entries(keep_ref, got_ref, r1_ref, r2_ref, r3_ref, mine_ref, back_ref):
    c, z, y = place()
    z0 = z == 0
    r = [ref[0:STATE].astype(F32) for ref in (r1_ref, r2_ref, r3_ref)]
    d = [read_decay(ref[STATE:YMSG]) for ref in (r1_ref, r2_ref, r3_ref)]
    zero = jnp.zeros_like(r[0])
    ef = jnp.where(y >= 3, r[2], zero)
    ef = jnp.where(y >= 2, r[1] + d[1] * ef, zero)
    ef = jnp.where(y >= 1, r[0] + d[0] * ef, zero)
    er = jnp.where(y <= 0, r[0], zero)
    er = jnp.where(y <= 1, r[1] + d[1] * er, zero)
    er = jnp.where(y <= 2, r[2] + d[2] * er, zero)
    dm, do = read_decay(keep_ref[2 * STATE : MSG]), read_decay(got_ref[2 * STATE : MSG])
    df = jnp.where(z0, dm, do)
    tf = jnp.where(z0, keep_ref[0:STATE].astype(F32), got_ref[0:STATE].astype(F32))
    second_f = df * ef + tf
    dr = jnp.where(z0, do, dm)
    rows = slice(STATE, 2 * STATE)
    tr = jnp.where(z0, got_ref[rows].astype(F32), keep_ref[rows].astype(F32))
    first_r = dr * er + tr
    mine_ref[0] = jnp.where(z0, ef, second_f).astype(BF16)
    mine_ref[1] = jnp.where(z0, first_r, er).astype(BF16)
    back_ref[0] = jnp.where(z0, second_f, ef).astype(BF16)
    back_ref[1] = jnp.where(z0, er, first_r).astype(BF16)


def group_kernel(keep_ref, got_ref, *refs):
    group(keep_ref, got_ref, refs[-3:])


def entries_kernel(keep_ref, got_ref, r1_ref, r2_ref, r3_ref, *refs):
    entries(keep_ref, got_ref, r1_ref, r2_ref, r3_ref, *refs[-2:])


def within_kernel(k, p, u_ref, spread_ref, kq_ref, table_ref, mcol_ref, mrow_ref, drow_ref, after_ref, *refs):
    make_qk = len(refs) == 2 and refs[1].shape[0] == 2 and len(refs[1].shape) == 5
    qk_ref, out_ref = (refs[1], refs[0]) if make_qk else refs
    row = lax.broadcasted_iota(jnp.int32, (SUB, SUB), 0)
    col = lax.broadcasted_iota(jnp.int32, (SUB, SUB), 1)
    low = lax.broadcasted_iota(jnp.int32, (SUB, 2 * HEAD_DIM), 1) < HEAD_DIM

    def block(b, _):
        if make_qk:
            for s in range(2):
                rows = slice(s * SUB, (s + 1) * SUB)
                for d in range(2):
                    keys = kq_ref[b, d, rows, 0:STATE]
                    queries = kq_ref[b, d, rows, STATE : 2 * STATE]
                    prod = lax.dot_general(queries, keys, (((1,), (1,)), ((), ())), preferred_element_type=F32)
                    qk_ref[b, d, s] = jnp.where((row >= col) if d == 0 else (row <= col), prod, 0.0)
        start = b * HALF + start_of(k, p)
        first = start // HEAD_DIM
        spread = spread_ref[b]
        skip = dot(drow_ref[...], spread)[10:11]
        mcol = pltpu.roll(mcol_ref[...], 2 * HEADS - first, 1)
        mrow = mrow_ref[pl.ds(pl.multiple_of(first, HC), HC), :]
        wv, gt = expand(table_ref, WV, spread)
        for s in range(2):
            rows = slice(s * SUB, (s + 1) * SUB)
            for two in range(HC // 2):
                cols = slice(two * 128, (two + 1) * 128)
                up = u_ref[b, 0, rows, cols].astype(F32)
                xf = (up * wv[rows, cols]).astype(BF16)
                xb = (u_ref[b, 1, rows, cols].astype(F32) * wv[rows, cols]).astype(BF16)
                none = jnp.zeros_like(xf)
                left, right = [], []
                for h in range(2):
                    at = two * 2 + h
                    diff = mcol[rows, at : at + 1] - mrow[at : at + 1, rows]
                    decay = jnp.exp2(-jnp.abs(diff))
                    left += [(decay * qk_ref[b, 0, s]).astype(BF16), (decay * qk_ref[b, 1, s]).astype(BF16)]
                    keep = low if h == 0 else ~low
                    right += [jnp.where(keep, xf, none), jnp.where(keep, xb, none)]
                res = dot(jnp.concatenate(left, axis=1), jnp.concatenate(right, axis=0))
                out_ref[b, rows, cols] = (res * gt[rows, cols] + up * skip[:, cols]).astype(BF16)
        return _

    lax.fori_loop(0, 2, block, 0)


QK = vmem(F32, 2, 2, 2, SUB, SUB)


def make_within(k, p, u, spread, kq, table, mcol, mrow, drow, after, qk=None):
    outs = [vmem(BF16, 2, TOK, CW)]
    operands = (u, spread, kq, table, mcol, mrow, drow, after)
    kernel = functools.partial(within_kernel, k, p)
    if qk is None:
        return call(kernel, f"within_{k}{p}", [*outs, QK], operands)
    return call(kernel, f"within_{k}{p}", outs, (*operands, qk))[0]


def finish_part(k, p, other, entry_ref, saved_ref, spread_ref, within_ref, gate_ref, kq_ref, table_ref, drow_ref, put, square):
    c, z, y = place()
    b = 1 - c if other else c
    start = start_of(k, p)
    at = columns(start, CW)
    spread = spread_ref[b]
    drow = dot(drow_ref[...], spread)
    d0, d1 = drow[8:9], drow[9:10]
    far = dot(drow_ref[...], spread_ref[1 - b])
    far = far[0:1] + far[1:2]
    one = jnp.ones_like(far)
    none = jnp.zeros((STATE, CW), F32)
    first = b == 0
    ef = jnp.where(first, one, far) * entry_ref[0].astype(F32) + jnp.where(first, none, saved_ref[4].astype(F32))
    er = jnp.where(first, far, one) * entry_ref[1].astype(F32) + jnp.where(first, saved_ref[5].astype(F32), none)
    inside = [
        (ef.astype(BF16), (er * d1 + saved_ref[2 * b + 1].astype(F32)).astype(BF16)),
        ((ef * d0 + saved_ref[2 * b].astype(F32)).astype(BF16), er.astype(BF16)),
    ]
    gf, gr = expand(table_ref, GF, spread)
    for s in range(2):
        rows = slice(s * SUB, (s + 1) * SUB)
        cf = dot(kq_ref[b, 0, rows, STATE : 2 * STATE], inside[s][0])
        cr = dot(kq_ref[b, 1, rows, STATE : 2 * STATE], inside[s][1])
        mixed = within_ref[b, rows].astype(F32) + gf[rows] * cf + gr[rows] * cr
        half = gate_ref[rows, at].astype(F32) * 0.5
        gated = mixed * (half + half * jnp.tanh(half))
        put(rows, gated)
        sq = gated * gated
        for j in range(0, CW, 128):
            part = sq[:, j : j + 128]
            square[s] = part if square[s] is None else square[s] + part


def halves(refs):
    return refs if len(refs) == 2 else (refs[0].at[0:SUB], refs[0].at[SUB:TOK])


def finish_piece(k, p, entry_ref, saved_ref, spread_ref, within_ref, gates, shared, own_ref, msg_refs, squares):
    def put_own(rows, gated):
        own_ref[rows] = gated

    def put_other(rows, gated):
        msg_refs[rows.start // SUB][:, 0:CW] = gated.astype(BF16)

    for other, put in ((1, put_other), (0, put_own)):
        finish_part(k, p, other, entry_ref, saved_ref, spread_ref, within_ref, gates[other], *shared, put, squares[other])


NEAR = ((3, 0), (3, 1), (2, 0))
BACK = (2, 1)


def finish_near_kernel(k, p, entry_ref, saved_ref, spread_ref, within_ref, gate_ref, gate_other_ref, *refs):
    shared, (square_in, own_ref, *msg_refs, square_ref) = refs[:3], refs[3:]
    msg_refs = halves(msg_refs)
    squares = [[None, None], [None, None]]
    gates = (gate_ref, gate_other_ref)
    finish_piece(k, p, entry_ref, saved_ref, spread_ref, within_ref, gates, shared, own_ref, msg_refs, squares)
    for other in range(2):
        for s in range(2):
            rows = slice(s * SUB, (s + 1) * SUB)
            if (k, p) == NEAR[0]:
                square_ref[other, rows] = squares[other][s]
            else:
                square_ref[other, rows] = square_in[other, rows] + squares[other][s]


def finish_other_kernel(entry_ref, saved_ref, spread_ref, within_ref, gate_ref, *refs):
    shared, square_in, msg_refs = refs[:3], refs[3], halves(refs[-1:])
    square = [square_in[1, s * SUB : (s + 1) * SUB] for s in range(2)]

    def put(rows, gated):
        msg_refs[rows.start // SUB][:, 0:CW] = gated.astype(BF16)

    finish_part(*BACK, 1, entry_ref, saved_ref, spread_ref, within_ref, gate_ref, *shared, put, square)
    lane = lax.broadcasted_iota(jnp.int32, (SUB, 128), 1)
    for s in range(2):
        total = jnp.sum(square[s], axis=1, keepdims=True)
        hi = total.astype(BF16).astype(F32)
        sums = jnp.where(lane == 0, hi, jnp.where(lane == 1, total - hi, 0.0))
        msg_refs[s][:, CW : CW + 128] = sums.astype(BF16)


def finish_own_kernel(entry_ref, saved_ref, spread_ref, within_ref, gate_ref, *refs):
    shared, (square_in, after_ref, own_ref, square_ref) = refs[:3], refs[3:]
    square = [square_in[0, s * SUB : (s + 1) * SUB] for s in range(2)]

    def put(rows, gated):
        own_ref[rows] = gated

    finish_part(*BACK, 0, entry_ref, saved_ref, spread_ref, within_ref, gate_ref, *shared, put, square)
    for s in range(2):
        square_ref[s * SUB : (s + 1) * SUB] = square[s]


def norm_kernel(*refs):
    own_refs, other_refs, (square_ref, gain_ref, out_hbm, out_ref, sems) = refs[:4], refs[4:10], refs[10:]
    other_refs = (other_refs[0:2], other_refs[2:4], halves(other_refs[4:5]), halves(other_refs[5:6]))
    c, z, y = place()
    pieces = []
    for n, piece in enumerate((*NEAR, BACK)):
        pieces.append(((own_refs[n], own_refs[n].at[SUB:TOK]), c * HALF + start_of(*piece)))
        pieces.append((other_refs[n], (1 - c) * HALF + start_of(*piece)))
    step = 32
    copies = []
    for r in range(0, TOK, step):
        rows, inside = slice(r, r + step), slice(r % SUB, r % SUB + step)
        total = square_ref[rows] + other_refs[3][r // SUB][inside, CW : CW + 128].astype(F32)
        scale = lax.rsqrt(jnp.sum(total, axis=1, keepdims=True) * (1.0 / INNER) + 1e-05)
        for refs, start in pieces:
            at = columns(start, CW)
            out_ref[rows, at] = (refs[r // SUB][inside, 0:CW].astype(F32) * scale * gain_ref[:, at]).astype(BF16)
        copies.append(pltpu.make_async_copy(out_ref.at[rows], out_hbm.at[rows], sems.at[len(copies)]))
        copies[-1].start()
    for copy in copies:
        copy.wait()


def per_device(mixer_input, gate_input, conv_forward, conv_reverse, step_size, decay_rate, skip_scale, norm_gain):
    n = lax.axis_size("seq")

    def send(v, perm):
        return lax.ppermute(v, "seq", perm)

    core = [(i, i ^ 1) for i in range(n)]
    zswap = [(i, i ^ 2) for i in range(n)]
    chips = [(i, i + 1) for i in range(1, n - 1, 2)] + [(i + 1, i) for i in range(1, n - 1, 2)]

    def along_y(msgs):
        return [send(m, [(i, (i + 4 * k) % n) for i in range(n)]) for k, m in enumerate(msgs, 1)]

    to_core, to_chip = call(
        edge_kernel,
        "edges",
        [vmem(BF16, TOK, WIDE + STEPS), vmem(BF16, HALO, E)],
        (),
        (mixer_input, step_size),
        [pltpu.VMEM((HEADS, TOK), F32), pltpu.SemaphoreType.DMA((4,))],
    )
    x, table, mcol, mrow, drow, taps, kq, u2a = call(
        front_kernel,
        "front",
        [
            vmem(BF16, 2, TOK, WIDE),
            vmem(BF16, 6, TOK, 2 * HEADS),
            vmem(F32, TOK, 2 * HEADS),
            vmem(F32, HEADS, TOK),
            vmem(BF16, 16, 2 * HEADS),
            vmem(F32, 8, WIDE),
            KEYS,
            U,
        ],
        (send(to_core, core),),
        (
            mixer_input,
            step_size,
            decay_rate.reshape(1, HEADS),
            skip_scale.reshape(1, HEADS),
            conv_forward,
            conv_reverse,
        ),
        [
            pltpu.VMEM((HEADS, TOK), F32),
            pltpu.VMEM((1, HEADS), F32),
            pltpu.VMEM((1, HEADS), F32),
            pltpu.VMEM((4, WIDE), F32),
            pltpu.VMEM((4, WIDE), F32),
            pltpu.SemaphoreType.DMA((10,)),
        ],
    )
    chip_halo, to_core = call(
        halo_kernel, "halo", [vmem(BF16, HALO, WIDE)] * 2, (send(to_chip, chips), kq)
    )
    halo = (x, taps, chip_halo, send(to_core, core))
    (u2b,) = call(conv_kernel, "conv_21", [U], (x, taps))
    kq, u2a, kt, saved2a, spread2a, zsend0, gate_to_core = call(
        first_states_kernel,
        "states_first",
        [KEYS, U, vmem(BF16, 2, 2, STATE, TOK), SAVED, SPREAD, CHIP, vmem(BF16, TOK, HALF)],
        (kq, u2a, *halo, table, drow, u2b),
        (gate_input,),
        [pltpu.SemaphoreType.DMA(())],
        aliases={0: 0, 1: 1},
    )
    got0 = send(zsend0, zswap)

    def make_rest(name, todo, after):
        kernel = functools.partial(rest_kernel, todo)
        outs = [U, SAVED, SPREAD, CHIP] * len(todo)
        if len(todo) == 1:
            return call(kernel, name, outs, (*halo, table, drow, kt, after))
        outs += [vmem(BF16, TOK, HALF), vmem(F32, 1, INNER)]
        sems = [pltpu.SemaphoreType.DMA((2,))]
        params = (gate_input, norm_gain.reshape(1, INNER))
        return call(kernel, name, outs, (*halo, table, drow, kt, after, u2b), params, sems, aliases={8: 0})

    u3a, saved3a, spread3a, keep0 = make_rest("states_a", ((3, 0),), zsend0)
    u2b, saved2b, spread2b, zsend1, u3b, saved3b, spread3b, keep1, gate, gain = make_rest(
        "states_b", ((2, 1), (3, 1)), keep0
    )
    got1 = send(zsend1, zswap)
    gates = (gate, send(gate_to_core, core))
    tables = (kq, table, mcol, mrow, drow)
    yout = [vmem(BF16, YMSG, CW)] * 3
    entry = vmem(BF16, 2, STATE, CW)

    w2a, qk = make_within(2, 0, u2a, spread2a, *tables, keep1)
    msgs = call(group_kernel, "group_a", yout, (keep0, got0, w2a, gates[1]))
    arrived0 = along_y(msgs)
    w2b = make_within(2, 1, u2b, spread2b, *tables, msgs[0], qk)
    msgs = call(group_kernel, "group_b", yout, (keep1, got1, w2b))
    arrived1 = along_y(msgs)
    mine0, back0 = call(entries_kernel, "entries_a", [entry, entry], (keep0, got0, *arrived0, msgs[0]))
    back0 = send(back0, zswap)
    w3a = make_within(3, 0, u3a, spread3a, *tables, mine0, qk)
    mine1, back1 = call(entries_kernel, "entries_b", [entry, entry], (keep1, got1, *arrived1, w3a))
    back1 = send(back1, zswap)
    w3b = make_within(3, 1, u3b, spread3b, *tables, mine1, qk)
    shared = (kq, table, drow)
    square = kt
    own, other = [], []
    parts = (
        (mine0, saved3a, spread3a, w3a),
        (mine1, saved3b, spread3b, w3b),
        (back0, saved2a, spread2a, w2a),
    )
    two, one = [vmem(BF16, SUB, CW)] * 2, [vmem(BF16, TOK, CW)]
    for (k, p), part, message in zip(NEAR, parts, (two, two, one)):
        gated, *msg, square = call(
            functools.partial(finish_near_kernel, k, p),
            f"finish_{k}{p}",
            [vmem(F32, TOK, CW), *message, vmem(F32, 2, TOK, 128)],
            (*part, *gates, *shared, square),
        )
        own.append(gated)
        other += [send(m, core) for m in msg]
    msg = call(
        finish_other_kernel,
        "finish_other",
        [vmem(BF16, TOK, CW + 128)],
        (back1, saved2b, spread2b, w2b, *gates[1:], *shared, square, *other[:4]),
    )
    other += [send(m, core) for m in msg]
    gated, square = call(
        finish_own_kernel,
        "finish_own",
        [vmem(F32, TOK, CW), vmem(F32, TOK, 128)],
        (back1, saved2b, spread2b, w2b, gates[0], *shared, square, msg[0]),
    )
    own.append(gated)
    (out,) = call(
        norm_kernel,
        "norm",
        [shape(BF16, TOK, INNER)],
        (*own, *other, square, gain),
        (),
        [pltpu.VMEM((TOK, INNER), BF16), pltpu.SemaphoreType.DMA((8,))],
    )
    return out


def solution(mesh):
    in_specs = (
        P(("row", "seq"), None),
        P(("row", "seq"), None),
        P(),
        P(),
        P(None, ("row", "seq")),
        P("row"),
        P(),
        P(),
    )
    out_specs = P(("row", "seq"), None)
    return jax.shard_map(per_device, mesh=mesh, in_specs=in_specs, out_specs=out_specs, check_vma=False)
```

```python
import functools

import jax
import jax.numpy as jnp
from jax import lax
from jax.experimental import pallas as pl
from jax.experimental.pallas import tpu as pltpu
from jax.sharding import PartitionSpec as P

HEADS = 64
HEAD_DIM = 64
STATE = 128
TOK = 256
SUB = 128
INNER = 4096
E = 4352
HALF = INNER // 2
QUART = INNER // 4
WIDE = HALF + 2 * STATE
STEPS = 256
CW = 512
HC = CW // HEAD_DIM
HALO = 16
MSG = 2 * STATE + 16
YMSG = STATE + 16
LOG2E = 1.4426950408889634
F32 = jnp.float32
BF16 = jnp.bfloat16
WF, WR, GF, GR, WV, GT = range(6)
MIB = 2**20


def dot(a, b, **kw):
    return jnp.dot(a, b, preferred_element_type=F32, **kw)


def shape(dtype, *dims):
    return jax.ShapeDtypeStruct(dims, dtype)


VMEM = pl.BlockSpec(memory_space=pltpu.VMEM)
HBM = pl.BlockSpec(memory_space=pltpu.HBM)


def vmem(dtype, *dims):
    return pltpu.VMEM(dims, dtype)


def call(kernel, name, outs, operands, params=(), scratch=(), limit=12, us=1.0, aliases=None):
    operands = [pltpu.with_memory_space_constraint(v, pltpu.VMEM) for v in operands]
    params = [pltpu.with_memory_space_constraint(v, pltpu.HBM) for v in params]
    return pl.pallas_call(
        kernel,
        name=name,
        in_specs=[VMEM] * len(operands) + [HBM] * len(params),
        out_specs=[HBM if isinstance(o, jax.ShapeDtypeStruct) else VMEM for o in outs],
        out_shape=outs,
        scratch_shapes=list(scratch),
        input_output_aliases=aliases or {},
        compiler_params=pltpu.CompilerParams(vmem_limit_bytes=limit * MIB),
        cost_estimate=pl.CostEstimate(flops=int(us * 1e8), bytes_accessed=int(us * 3e5), transcendentals=0),
    )(*operands, *params)


def place():
    at = lax.axis_index("seq")
    return at & 1, (at >> 1) & 1, at >> 2


def columns(start, width):
    return pl.ds(pl.multiple_of(start, 128), width)


def split2(x):
    hi = x.astype(BF16)
    lo = (x - hi.astype(F32)).astype(BF16)
    return hi, lo


def spread_matrix(start, width=CW):
    k = lax.broadcasted_iota(jnp.int32, (2 * HEADS, width), 0)
    col = lax.broadcasted_iota(jnp.int32, (2 * HEADS, width), 1)
    low = (k & (HEADS - 1)) * HEAD_DIM - start
    return jnp.where((col >= low) & (col < low + HEAD_DIM), 1.0, 0.0).astype(BF16)


def expand(table_ref, first, spread):
    both = dot(table_ref[first : first + 2].reshape(2 * TOK, 2 * HEADS), spread)
    return both[0:TOK], both[TOK:]


def read_decay(rows):
    rows = rows.astype(F32)
    return rows[0:1] + rows[1:2]


def decay_rows(d):
    hi, lo = split2(d)
    none = jnp.zeros((14, d.shape[1]), F32)
    return jnp.concatenate([hi.astype(F32), lo.astype(F32), none], axis=0).astype(BF16)


def make_tables(step, decay, skip, table_ref, mcol_ref, mrow_ref, drow_ref):
    a = -decay * step
    row = lax.broadcasted_iota(jnp.int32, (TOK, TOK), 0)
    col = lax.broadcasted_iota(jnp.int32, (TOK, TOK), 1)
    tri = jnp.where((row >= col) & ((row >= SUB) == (col >= SUB)), 1.0, 0.0).astype(BF16)
    p0 = a.astype(BF16)
    p1 = (a - p0.astype(F32)).astype(BF16)
    p2 = (a - p0.astype(F32) - p1.astype(F32)).astype(BF16)
    sums = dot(tri, jnp.concatenate([p0, p1, p2, jnp.zeros_like(p0)], axis=1))
    cum = sums[:, 0:HEADS] + sums[:, HEADS : 2 * HEADS] + sums[:, 2 * HEADS : 3 * HEADS]
    excl = cum - a
    e0 = cum[SUB - 1 : SUB]
    e1 = cum[TOK - 1 : TOK]
    ends = jnp.concatenate([jnp.broadcast_to(e0, (SUB, HEADS)), jnp.broadcast_to(e1, (SUB, HEADS))], axis=0)
    zero = jnp.zeros_like(cum)

    def put(at, value):
        hi, lo = split2(value)
        table_ref[at] = jnp.concatenate([hi, lo], axis=1)

    put(WF, step * jnp.exp(jnp.minimum(ends - cum, zero)))
    put(WR, step * jnp.exp(excl))
    put(GF, jnp.exp(cum))
    put(GR, jnp.exp(jnp.minimum(ends - excl, zero)))
    put(WV, step * jnp.exp(-0.5 * a))
    put(GT, jnp.exp(0.5 * a))
    m = (cum - 0.5 * a) * LOG2E
    mcol_ref[...] = jnp.concatenate([m, zero], axis=1)
    mrow_ref[...] = jnp.transpose(m)
    h0, l0 = split2(jnp.exp(e0))
    h1, l1 = split2(jnp.exp(e1))
    hd, ld = split2(jnp.exp(e0 + e1))
    hs, ls = split2(skip)
    no = jnp.zeros_like(h0)
    wide = [
        jnp.concatenate([hd, no], axis=1).astype(F32),
        jnp.concatenate([no, ld], axis=1).astype(F32),
        jnp.zeros((6, 2 * HEADS), F32),
        jnp.concatenate([h0, l0], axis=1).astype(F32),
        jnp.concatenate([h1, l1], axis=1).astype(F32),
        jnp.concatenate([hs, ls], axis=1).astype(F32),
        jnp.zeros((5, 2 * HEADS), F32),
    ]
    drow_ref[...] = jnp.concatenate(wide, axis=0).astype(BF16)


def conv(x, cf, cr):
    rows = x.shape[0]
    back = pltpu.roll(x, 1, 0)
    fore = pltpu.roll(x, rows - 1, 0)
    h = cf[3:4] * x + cf[2:3] * back + pltpu.roll(cf[1:2] * x + cf[0:1] * back, 2, 0)
    g = cr[3:4] * x + cr[2:3] * fore + pltpu.roll(cr[1:2] * x + cr[0:1] * fore, rows - 2, 0)
    return h, g


def silu_of_half(h):
    return (h + h * jnp.tanh(h)).astype(BF16)


def copy_all(pairs, sems):
    copies = [pltpu.make_async_copy(src, dst, sems.at[k]) for k, (src, dst) in enumerate(pairs)]
    for copy in copies:
        copy.start()
    return copies


def start_of(k, p):
    c, z, y = place()
    return (z if k == 3 else 1 - z) * QUART + p * CW


def edge_kernel(x_hbm, step_hbm, to_core_ref, to_chip_ref, step_ref, sems):
    c, z, y = place()
    far = columns((1 - c) * HALF, HALF)
    ends = pl.ds(pl.multiple_of(c * (TOK - HALO), HALO), HALO)
    copies = copy_all(
        [
            (step_hbm, step_ref),
            (x_hbm.at[ends], to_chip_ref),
            (x_hbm.at[:, far], to_core_ref.at[:, 0:HALF]),
            (x_hbm.at[:, INNER:E], to_core_ref.at[:, HALF:WIDE]),
        ],
        sems,
    )
    copies[0].wait()
    step = jnp.transpose(step_ref[...])
    p0 = step.astype(BF16).astype(F32)
    p1 = (step - p0).astype(BF16).astype(F32)
    p2 = step - p0 - p1
    to_core_ref[:, WIDE : WIDE + STEPS] = jnp.concatenate([p0, p1, p2, jnp.zeros_like(p0)], axis=1).astype(BF16)
    for copy in copies[1:]:
        copy.wait()


def halo_kernel(halo_ref, after_ref, mine_ref, to_core_ref):
    c, z, y = place()
    for ref, half in ((mine_ref, c), (to_core_ref, 1 - c)):
        ref[:, 0:HALF] = halo_ref[:, columns(half * HALF, HALF)]
        ref[:, HALF:WIDE] = halo_ref[:, INNER:E]


def conv_piece(x_ref, taps_ref, u_ref, start, halo=None):
    def body(i, _):
        at = columns(start + i * 128, 128)
        cols = columns(i * 128, 128)
        cf, cr = taps_ref[0:4, at], taps_ref[4:8, at]
        x0, x1 = x_ref[0, :, at].astype(F32), x_ref[1, :, at].astype(F32)
        before, after = halo(at) if halo else (x0[0:8], x1[TOK - 8 :])
        for b, rows in enumerate(((before, x0, x1[0:8]), (x0[TOK - 8 :], x1, after))):
            h, g = conv(jnp.concatenate(rows, axis=0), cf, cr)
            u_ref[b, 0, :, cols] = silu_of_half(h[8 : TOK + 8])
            u_ref[b, 1, :, cols] = silu_of_half(g[8 : TOK + 8])
        return _

    lax.fori_loop(0, u_ref.shape[3] // 128, body, 0)


def halo_of(chip_ref, core_ref):
    def rows(at):
        c, z, y = place()
        chip, core = chip_ref[:, at].astype(F32), core_ref[:, at].astype(F32)
        before, after = jnp.where(c == 0, chip, core), jnp.where(c == 0, core, chip)
        return before[HALO - 8 :], after[:8]

    return rows


def repair(x_ref, taps_ref, u_ref, start, halo):
    def body(i, _):
        at = columns(start + i * 256, 256)
        cols = columns(i * 256, 256)
        cf, cr = taps_ref[0:4, at], taps_ref[4:8, at]
        before, after = halo(at)
        h, _g = conv(jnp.concatenate([before, x_ref[0, 0:HALO, at].astype(F32)], axis=0), cf, cr)
        u_ref[0, 0, 0:HALO, cols] = silu_of_half(h[8:])
        _h, g = conv(jnp.concatenate([x_ref[1, TOK - HALO : TOK, at].astype(F32), after], axis=0), cf, cr)
        u_ref[1, 1, TOK - HALO : TOK, cols] = silu_of_half(g[:HALO])
        return _

    lax.fori_loop(0, u_ref.shape[3] // 256, body, 0)


def front_kernel(
    other_ref, x_hbm, step_hbm, decay_hbm, skip_hbm, cf_hbm, cr_hbm,
    x_ref, table_ref, mcol_ref, mrow_ref, drow_ref, taps_ref, kq_ref, u_ref,
    step_ref, decay_ref, skip_ref, cf_ref, cr_ref, sems,
):
    c, z, y = place()
    half = columns(c * HALF, HALF)
    copies = copy_all(
        [
            (step_hbm, step_ref),
            (decay_hbm, decay_ref),
            (skip_hbm, skip_ref),
            (x_hbm.at[:, half], x_ref.at[c, :, 0:HALF]),
            (x_hbm.at[:, INNER:E], x_ref.at[c, :, HALF:WIDE]),
            (cf_hbm.at[:, half], cf_ref.at[:, 0:HALF]),
            (cf_hbm.at[:, INNER:E], cf_ref.at[:, HALF:WIDE]),
            (cr_hbm.at[:, half], cr_ref.at[:, 0:HALF]),
            (cr_hbm.at[:, INNER:E], cr_ref.at[:, HALF:WIDE]),
            (other_ref.at[:, 0:WIDE], x_ref.at[1 - c]),
        ],
        sems,
    )
    for copy in copies[:3]:
        copy.wait()
    def half_of(values):
        return jnp.where(c == 0, values[:, 0 : HEADS // 2], values[:, HEADS // 2 : HEADS])

    parts = other_ref[:, WIDE : WIDE + STEPS].astype(F32)
    other = half_of(parts[:, 0:HEADS] + parts[:, HEADS : 2 * HEADS] + parts[:, 2 * HEADS : 3 * HEADS])
    mine = half_of(jnp.transpose(step_ref[...]))
    step = jnp.concatenate([jnp.where(c == 0, mine, other), jnp.where(c == 0, other, mine)], axis=1)
    decay, skip = half_of(decay_ref[...]), half_of(skip_ref[...])
    decay, skip = jnp.concatenate([decay, decay], axis=1), jnp.concatenate([skip, skip], axis=1)
    make_tables(step, decay, skip, table_ref, mcol_ref, mrow_ref, drow_ref)
    for copy in copies[3:]:
        copy.wait()
    taps_ref[0:4] = cf_ref[...] * 0.5
    taps_ref[4:8] = cr_ref[...] * 0.5
    conv_piece(x_ref, taps_ref, kq_ref, HALF)
    conv_piece(x_ref, taps_ref, u_ref, start_of(2, 0))


def piece_states(u_ref, kt_ref, table_ref, drow_ref, start, saved_ref, spread_ref, chip_ref):
    blocks = []
    for b in range(2):
        spread = spread_matrix(b * HALF + start)
        spread_ref[b] = spread
        drow = dot(drow_ref[...], spread)
        d0, d1 = drow[8:9], drow[9:10]

        weights = expand(table_ref, WF, spread)

        def weighted(d, r):
            return (u_ref[b, d, r : r + SUB].astype(F32) * weights[d][r : r + SUB]).astype(BF16)

        f0 = dot(kt_ref[b, 0, :, 0:SUB], weighted(0, 0))
        f1 = dot(kt_ref[b, 0, :, SUB:TOK], weighted(0, SUB))
        r0 = dot(kt_ref[b, 1, :, 0:SUB], weighted(1, 0))
        r1 = dot(kt_ref[b, 1, :, SUB:TOK], weighted(1, SUB))
        saved_ref[2 * b] = f0.astype(BF16)
        saved_ref[2 * b + 1] = r1.astype(BF16)
        blocks.append((d1 * f0 + f1, r0 + d0 * r1, drow[0:1] + drow[1:2]))
    (f0, r0, d0), (f1, r1, d1) = blocks
    saved_ref[4] = f0.astype(BF16)
    saved_ref[5] = r1.astype(BF16)
    chip_ref[0:STATE] = (d1 * f0 + f1).astype(BF16)
    chip_ref[STATE : 2 * STATE] = (r0 + d0 * r1).astype(BF16)
    chip_ref[2 * STATE : MSG] = decay_rows(d0 * d1)


def first_states_kernel(
    kq_in, u_in, x_ref, taps_ref, chip_halo_ref, core_halo_ref, table_ref, drow_ref, after_ref, gate_hbm,
    kq_ref, u_ref, kt_ref, saved_ref, spread_ref, chip_ref, gate_to_core_ref, sem,
):
    c, z, y = place()
    copy = pltpu.make_async_copy(gate_hbm.at[:, columns((1 - c) * HALF, HALF)], gate_to_core_ref, sem)
    copy.start()
    halo = halo_of(chip_halo_ref, core_halo_ref)
    repair(x_ref, taps_ref, kq_ref, HALF, halo)
    for b in range(2):
        for d in range(2):
            kt_ref[b, d] = jnp.transpose(kq_ref[b, d, :, 0:STATE].astype(F32)).astype(BF16)
    start = start_of(2, 0)
    repair(x_ref, taps_ref, u_ref, start, halo)
    piece_states(u_ref, kt_ref, table_ref, drow_ref, start, saved_ref, spread_ref, chip_ref)
    copy.wait()


def conv_kernel(x_ref, taps_ref, u_ref):
    conv_piece(x_ref, taps_ref, u_ref, start_of(2, 1))


def rest_kernel(todo, x_ref, taps_ref, chip_halo_ref, core_halo_ref, table_ref, drow_ref, kt_ref, after_ref, *outs):
    c, z, y = place()
    copies = []
    if todo == ((2, 1),):
        _u_in, *outs = outs
    if todo == ((3, 1),):
        gate_hbm, gain_hbm, *outs, gate_ref, gain_ref, sems = outs
        copies = copy_all([(gate_hbm.at[:, columns(c * HALF, HALF)], gate_ref), (gain_hbm, gain_ref)], sems)
    for n, piece in enumerate(todo):
        u_ref, saved_ref, spread_ref, chip_ref = outs[4 * n : 4 * n + 4]
        halo = halo_of(chip_halo_ref, core_halo_ref)
        if piece == (2, 1):
            repair(x_ref, taps_ref, u_ref, start_of(*piece), halo)
        else:
            conv_piece(x_ref, taps_ref, u_ref, start_of(*piece), halo)
        piece_states(u_ref, kt_ref, table_ref, drow_ref, start_of(*piece), saved_ref, spread_ref, chip_ref)
    for copy in copies:
        copy.wait()


KEYS = vmem(BF16, 2, 2, TOK, 2 * STATE)
U = vmem(BF16, 2, 2, TOK, CW)
SAVED = vmem(BF16, 6, STATE, CW)
SPREAD = vmem(BF16, 2, 2 * HEADS, CW)
CHIP = vmem(BF16, MSG, CW)


def group(keep_ref, got_ref, outs):
    c, z, y = place()
    z0 = z == 0
    dm, do = read_decay(keep_ref[2 * STATE : MSG]), read_decay(got_ref[2 * STATE : MSG])
    one = jnp.ones_like(dm)
    am, ao = jnp.where(z0, do, one), jnp.where(z0, one, dm)
    fwd = (am * keep_ref[0:STATE].astype(F32) + ao * got_ref[0:STATE].astype(F32)).astype(BF16)
    am, ao = jnp.where(z0, one, do), jnp.where(z0, dm, one)
    rows = slice(STATE, 2 * STATE)
    rev = (am * keep_ref[rows].astype(F32) + ao * got_ref[rows].astype(F32)).astype(BF16)
    decay = decay_rows(dm * do)
    for k in range(1, 4):
        outs[k - 1][0:STATE] = jnp.where(y + k < 4, fwd, rev)
        outs[k - 1][STATE:YMSG] = decay


def entries(keep_ref, got_ref, r1_ref, r2_ref, r3_ref, mine_ref, back_ref):
    c, z, y = place()
    z0 = z == 0
    r = [ref[0:STATE].astype(F32) for ref in (r1_ref, r2_ref, r3_ref)]
    d = [read_decay(ref[STATE:YMSG]) for ref in (r1_ref, r2_ref, r3_ref)]
    zero = jnp.zeros_like(r[0])
    ef = jnp.where(y >= 3, r[2], zero)
    ef = jnp.where(y >= 2, r[1] + d[1] * ef, zero)
    ef = jnp.where(y >= 1, r[0] + d[0] * ef, zero)
    er = jnp.where(y <= 0, r[0], zero)
    er = jnp.where(y <= 1, r[1] + d[1] * er, zero)
    er = jnp.where(y <= 2, r[2] + d[2] * er, zero)
    dm, do = read_decay(keep_ref[2 * STATE : MSG]), read_decay(got_ref[2 * STATE : MSG])
    df = jnp.where(z0, dm, do)
    tf = jnp.where(z0, keep_ref[0:STATE].astype(F32), got_ref[0:STATE].astype(F32))
    second_f = df * ef + tf
    dr = jnp.where(z0, do, dm)
    rows = slice(STATE, 2 * STATE)
    tr = jnp.where(z0, got_ref[rows].astype(F32), keep_ref[rows].astype(F32))
    first_r = dr * er + tr
    mine_ref[0] = jnp.where(z0, ef, second_f).astype(BF16)
    mine_ref[1] = jnp.where(z0, first_r, er).astype(BF16)
    back_ref[0] = jnp.where(z0, second_f, ef).astype(BF16)
    back_ref[1] = jnp.where(z0, er, first_r).astype(BF16)


def group_kernel(keep_ref, got_ref, *refs):
    group(keep_ref, got_ref, refs[-3:])


def entries_kernel(keep_ref, got_ref, r1_ref, r2_ref, r3_ref, *refs):
    entries(keep_ref, got_ref, r1_ref, r2_ref, r3_ref, *refs[-2:])


def within_kernel(k, p, u_ref, spread_ref, kq_ref, table_ref, mcol_ref, mrow_ref, drow_ref, after_ref, *refs):
    make_qk = len(refs) == 2 and refs[1].shape[0] == 2 and len(refs[1].shape) == 5
    qk_ref, out_ref = (refs[1], refs[0]) if make_qk else refs
    row = lax.broadcasted_iota(jnp.int32, (SUB, SUB), 0)
    col = lax.broadcasted_iota(jnp.int32, (SUB, SUB), 1)
    low = lax.broadcasted_iota(jnp.int32, (SUB, 2 * HEAD_DIM), 1) < HEAD_DIM

    def block(b, _):
        if make_qk:
            for s in range(2):
                rows = slice(s * SUB, (s + 1) * SUB)
                for d in range(2):
                    keys = kq_ref[b, d, rows, 0:STATE]
                    queries = kq_ref[b, d, rows, STATE : 2 * STATE]
                    prod = lax.dot_general(queries, keys, (((1,), (1,)), ((), ())), preferred_element_type=F32)
                    qk_ref[b, d, s] = jnp.where((row >= col) if d == 0 else (row <= col), prod, 0.0)
        start = b * HALF + start_of(k, p)
        first = start // HEAD_DIM
        spread = spread_ref[b]
        skip = dot(drow_ref[...], spread)[10:11]
        mcol = pltpu.roll(mcol_ref[...], 2 * HEADS - first, 1)
        mrow = mrow_ref[pl.ds(pl.multiple_of(first, HC), HC), :]
        wv, gt = expand(table_ref, WV, spread)
        for s in range(2):
            rows = slice(s * SUB, (s + 1) * SUB)
            for two in range(HC // 2):
                cols = slice(two * 128, (two + 1) * 128)
                up = u_ref[b, 0, rows, cols].astype(F32)
                xf = (up * wv[rows, cols]).astype(BF16)
                xb = (u_ref[b, 1, rows, cols].astype(F32) * wv[rows, cols]).astype(BF16)
                none = jnp.zeros_like(xf)
                left, right = [], []
                for h in range(2):
                    at = two * 2 + h
                    diff = mcol[rows, at : at + 1] - mrow[at : at + 1, rows]
                    decay = jnp.exp2(-jnp.abs(diff))
                    left += [(decay * qk_ref[b, 0, s]).astype(BF16), (decay * qk_ref[b, 1, s]).astype(BF16)]
                    keep = low if h == 0 else ~low
                    right += [jnp.where(keep, xf, none), jnp.where(keep, xb, none)]
                res = dot(jnp.concatenate(left, axis=1), jnp.concatenate(right, axis=0))
                out_ref[b, rows, cols] = (res * gt[rows, cols] + up * skip[:, cols]).astype(BF16)
        return _

    lax.fori_loop(0, 2, block, 0)


QK = vmem(F32, 2, 2, 2, SUB, SUB)


def make_within(k, p, u, spread, kq, table, mcol, mrow, drow, after, qk=None):
    outs = [vmem(BF16, 2, TOK, CW)]
    operands = (u, spread, kq, table, mcol, mrow, drow, after)
    kernel = functools.partial(within_kernel, k, p)
    if qk is None:
        return call(kernel, f"within_{k}{p}", [*outs, QK], operands)
    return call(kernel, f"within_{k}{p}", outs, (*operands, qk))[0]


def finish_part(k, p, other, entry_ref, saved_ref, spread_ref, within_ref, gate_ref, kq_ref, table_ref, drow_ref, put, square):
    c, z, y = place()
    b = 1 - c if other else c
    start = start_of(k, p)
    at = columns(start, CW)
    spread = spread_ref[b]
    drow = dot(drow_ref[...], spread)
    d0, d1 = drow[8:9], drow[9:10]
    far = dot(drow_ref[...], spread_ref[1 - b])
    far = far[0:1] + far[1:2]
    one = jnp.ones_like(far)
    none = jnp.zeros((STATE, CW), F32)
    first = b == 0
    ef = jnp.where(first, one, far) * entry_ref[0].astype(F32) + jnp.where(first, none, saved_ref[4].astype(F32))
    er = jnp.where(first, far, one) * entry_ref[1].astype(F32) + jnp.where(first, saved_ref[5].astype(F32), none)
    inside = [
        (ef.astype(BF16), (er * d1 + saved_ref[2 * b + 1].astype(F32)).astype(BF16)),
        ((ef * d0 + saved_ref[2 * b].astype(F32)).astype(BF16), er.astype(BF16)),
    ]
    gf, gr = expand(table_ref, GF, spread)
    for s in range(2):
        rows = slice(s * SUB, (s + 1) * SUB)
        cf = dot(kq_ref[b, 0, rows, STATE : 2 * STATE], inside[s][0])
        cr = dot(kq_ref[b, 1, rows, STATE : 2 * STATE], inside[s][1])
        mixed = within_ref[b, rows].astype(F32) + gf[rows] * cf + gr[rows] * cr
        half = gate_ref[rows, at].astype(F32) * 0.5
        gated = mixed * (half + half * jnp.tanh(half))
        put(rows, gated)
        sq = gated * gated
        for j in range(0, CW, 128):
            part = sq[:, j : j + 128]
            square[s] = part if square[s] is None else square[s] + part


def halves(refs):
    return refs if len(refs) == 2 else (refs[0].at[0:SUB], refs[0].at[SUB:TOK])


def finish_piece(k, p, entry_ref, saved_ref, spread_ref, within_ref, gates, shared, own_ref, msg_refs, squares):
    def put_own(rows, gated):
        own_ref[rows] = gated

    def put_other(rows, gated):
        msg_refs[rows.start // SUB][:, 0:CW] = gated.astype(BF16)

    for other, put in ((1, put_other), (0, put_own)):
        finish_part(k, p, other, entry_ref, saved_ref, spread_ref, within_ref, gates[other], *shared, put, squares[other])


NEAR = ((3, 0), (3, 1), (2, 0))
BACK = (2, 1)


def finish_near_kernel(k, p, entry_ref, saved_ref, spread_ref, within_ref, gate_ref, gate_other_ref, *refs):
    shared, (square_in, own_ref, *msg_refs, square_ref) = refs[:3], refs[3:]
    msg_refs = halves(msg_refs)
    squares = [[None, None], [None, None]]
    gates = (gate_ref, gate_other_ref)
    finish_piece(k, p, entry_ref, saved_ref, spread_ref, within_ref, gates, shared, own_ref, msg_refs, squares)
    for other in range(2):
        for s in range(2):
            rows = slice(s * SUB, (s + 1) * SUB)
            if (k, p) == NEAR[0]:
                square_ref[other, rows] = squares[other][s]
            else:
                square_ref[other, rows] = square_in[other, rows] + squares[other][s]


def finish_other_kernel(entry_ref, saved_ref, spread_ref, within_ref, gate_ref, *refs):
    shared, square_in, msg_refs = refs[:3], refs[3], halves(refs[-1:])
    square = [square_in[1, s * SUB : (s + 1) * SUB] for s in range(2)]

    def put(rows, gated):
        msg_refs[rows.start // SUB][:, 0:CW] = gated.astype(BF16)

    finish_part(*BACK, 1, entry_ref, saved_ref, spread_ref, within_ref, gate_ref, *shared, put, square)
    lane = lax.broadcasted_iota(jnp.int32, (SUB, 128), 1)
    for s in range(2):
        total = jnp.sum(square[s], axis=1, keepdims=True)
        hi = total.astype(BF16).astype(F32)
        sums = jnp.where(lane == 0, hi, jnp.where(lane == 1, total - hi, 0.0))
        msg_refs[s][:, CW : CW + 128] = sums.astype(BF16)


def finish_own_kernel(entry_ref, saved_ref, spread_ref, within_ref, gate_ref, *refs):
    shared, (square_in, after_ref, own_ref, square_ref) = refs[:3], refs[3:]
    square = [square_in[0, s * SUB : (s + 1) * SUB] for s in range(2)]

    def put(rows, gated):
        own_ref[rows] = gated

    finish_part(*BACK, 0, entry_ref, saved_ref, spread_ref, within_ref, gate_ref, *shared, put, square)
    for s in range(2):
        square_ref[s * SUB : (s + 1) * SUB] = square[s]


def norm_kernel(*refs):
    own_refs, other_refs, (square_ref, gain_ref, out_hbm, out_ref, sems) = refs[:4], refs[4:10], refs[10:]
    other_refs = (other_refs[0:2], other_refs[2:4], halves(other_refs[4:5]), halves(other_refs[5:6]))
    c, z, y = place()
    pieces = []
    for n, piece in enumerate((*NEAR, BACK)):
        pieces.append(((own_refs[n], own_refs[n].at[SUB:TOK]), c * HALF + start_of(*piece)))
        pieces.append((other_refs[n], (1 - c) * HALF + start_of(*piece)))
    step = 32
    copies = []
    for r in range(0, TOK, step):
        rows, inside = slice(r, r + step), slice(r % SUB, r % SUB + step)
        total = square_ref[rows] + other_refs[3][r // SUB][inside, CW : CW + 128].astype(F32)
        scale = lax.rsqrt(jnp.sum(total, axis=1, keepdims=True) * (1.0 / INNER) + 1e-05)
        for refs, start in pieces:
            at = columns(start, CW)
            out_ref[rows, at] = (refs[r // SUB][inside, 0:CW].astype(F32) * scale * gain_ref[:, at]).astype(BF16)
        copies.append(pltpu.make_async_copy(out_ref.at[rows], out_hbm.at[rows], sems.at[len(copies)]))
        copies[-1].start()
    for copy in copies:
        copy.wait()


def per_device(mixer_input, gate_input, conv_forward, conv_reverse, step_size, decay_rate, skip_scale, norm_gain):
    n = lax.axis_size("seq")

    def send(v, perm):
        return lax.ppermute(v, "seq", perm)

    core = [(i, i ^ 1) for i in range(n)]
    zswap = [(i, i ^ 2) for i in range(n)]
    chips = [(i, i + 1) for i in range(1, n - 1, 2)] + [(i + 1, i) for i in range(1, n - 1, 2)]

    def along_y(msgs):
        return [send(m, [(i, (i + 4 * k) % n) for i in range(n)]) for k, m in enumerate(msgs, 1)]

    to_core, to_chip = call(
        edge_kernel,
        "edges",
        [vmem(BF16, TOK, WIDE + STEPS), vmem(BF16, HALO, E)],
        (),
        (mixer_input, step_size),
        [pltpu.VMEM((HEADS, TOK), F32), pltpu.SemaphoreType.DMA((4,))],
    )
    x, table, mcol, mrow, drow, taps, kq, u2a = call(
        front_kernel,
        "front",
        [
            vmem(BF16, 2, TOK, WIDE),
            vmem(BF16, 6, TOK, 2 * HEADS),
            vmem(F32, TOK, 2 * HEADS),
            vmem(F32, HEADS, TOK),
            vmem(BF16, 16, 2 * HEADS),
            vmem(F32, 8, WIDE),
            KEYS,
            U,
        ],
        (send(to_core, core),),
        (
            mixer_input,
            step_size,
            decay_rate.reshape(1, HEADS),
            skip_scale.reshape(1, HEADS),
            conv_forward,
            conv_reverse,
        ),
        [
            pltpu.VMEM((HEADS, TOK), F32),
            pltpu.VMEM((1, HEADS), F32),
            pltpu.VMEM((1, HEADS), F32),
            pltpu.VMEM((4, WIDE), F32),
            pltpu.VMEM((4, WIDE), F32),
            pltpu.SemaphoreType.DMA((10,)),
        ],
    )
    chip_halo, to_core = call(
        halo_kernel, "halo", [vmem(BF16, HALO, WIDE)] * 2, (send(to_chip, chips), kq)
    )
    halo = (x, taps, chip_halo, send(to_core, core))
    (u2b,) = call(conv_kernel, "conv_21", [U], (x, taps))
    kq, u2a, kt, saved2a, spread2a, zsend0, gate_to_core = call(
        first_states_kernel,
        "states_first",
        [KEYS, U, vmem(BF16, 2, 2, STATE, TOK), SAVED, SPREAD, CHIP, vmem(BF16, TOK, HALF)],
        (kq, u2a, *halo, table, drow, u2b),
        (gate_input,),
        [pltpu.SemaphoreType.DMA(())],
        aliases={0: 0, 1: 1},
    )
    got0 = send(zsend0, zswap)

    def make_rest(name, todo, after):
        kernel = functools.partial(rest_kernel, todo)
        outs = [U, SAVED, SPREAD, CHIP]
        operands = (*halo, table, drow, kt, after)
        if todo == ((2, 1),):
            return call(kernel, name, outs, (*operands, u2b), aliases={8: 0})
        if todo == ((3, 1),):
            outs += [vmem(BF16, TOK, HALF), vmem(F32, 1, INNER)]
            params = (gate_input, norm_gain.reshape(1, INNER))
            return call(kernel, name, outs, operands, params, [pltpu.SemaphoreType.DMA((2,))])
        return call(kernel, name, outs, operands)

    u3a, saved3a, spread3a, keep0 = make_rest("states_30", ((3, 0),), zsend0)
    u2b, saved2b, spread2b, zsend1 = make_rest("states_21", ((2, 1),), keep0)
    got1 = send(zsend1, zswap)
    u3b, saved3b, spread3b, keep1, gate, gain = make_rest("states_31", ((3, 1),), zsend1)
    gates = (gate, send(gate_to_core, core))
    tables = (kq, table, mcol, mrow, drow)
    yout = [vmem(BF16, YMSG, CW)] * 3
    entry = vmem(BF16, 2, STATE, CW)

    w2a, qk = make_within(2, 0, u2a, spread2a, *tables, keep1)
    msgs = call(group_kernel, "group_a", yout, (keep0, got0, w2a, gates[1]))
    arrived0 = along_y(msgs)
    w2b = make_within(2, 1, u2b, spread2b, *tables, msgs[0], qk)
    msgs = call(group_kernel, "group_b", yout, (keep1, got1, w2b))
    arrived1 = along_y(msgs)
    mine0, back0 = call(entries_kernel, "entries_a", [entry, entry], (keep0, got0, *arrived0, msgs[0]))
    back0 = send(back0, zswap)
    w3a = make_within(3, 0, u3a, spread3a, *tables, mine0, qk)
    mine1, back1 = call(entries_kernel, "entries_b", [entry, entry], (keep1, got1, *arrived1, w3a))
    back1 = send(back1, zswap)
    w3b = make_within(3, 1, u3b, spread3b, *tables, mine1, qk)
    shared = (kq, table, drow)
    square = kt
    own, other = [], []
    parts = (
        (mine0, saved3a, spread3a, w3a),
        (mine1, saved3b, spread3b, w3b),
        (back0, saved2a, spread2a, w2a),
    )
    two, one = [vmem(BF16, SUB, CW)] * 2, [vmem(BF16, TOK, CW)]
    for (k, p), part, message in zip(NEAR, parts, (two, two, one)):
        gated, *msg, square = call(
            functools.partial(finish_near_kernel, k, p),
            f"finish_{k}{p}",
            [vmem(F32, TOK, CW), *message, vmem(F32, 2, TOK, 128)],
            (*part, *gates, *shared, square),
        )
        own.append(gated)
        other += [send(m, core) for m in msg]
    msg = call(
        finish_other_kernel,
        "finish_other",
        [vmem(BF16, TOK, CW + 128)],
        (back1, saved2b, spread2b, w2b, *gates[1:], *shared, square, *other[:4]),
    )
    other += [send(m, core) for m in msg]
    gated, square = call(
        finish_own_kernel,
        "finish_own",
        [vmem(F32, TOK, CW), vmem(F32, TOK, 128)],
        (back1, saved2b, spread2b, w2b, gates[0], *shared, square, msg[0]),
    )
    own.append(gated)
    (out,) = call(
        norm_kernel,
        "norm",
        [shape(BF16, TOK, INNER)],
        (*own, *other, square, gain),
        (),
        [pltpu.VMEM((TOK, INNER), BF16), pltpu.SemaphoreType.DMA((8,))],
    )
    return out


def solution(mesh):
    in_specs = (
        P(("row", "seq"), None),
        P(("row", "seq"), None),
        P(),
        P(),
        P(None, ("row", "seq")),
        P("row"),
        P(),
        P(),
    )
    out_specs = P(("row", "seq"), None)
    return jax.shard_map(per_device, mesh=mesh, in_specs=in_specs, out_specs=out_specs, check_vma=False)
```

```python
import functools

import jax
import jax.numpy as jnp
from jax import lax
from jax.experimental import pallas as pl
from jax.experimental.pallas import tpu as pltpu
from jax.sharding import PartitionSpec as P

HEADS = 64
HEAD_DIM = 64
STATE = 128
TOK = 256
SUB = 128
INNER = 4096
E = 4352
HALF = INNER // 2
QUART = INNER // 4
WIDE = HALF + 2 * STATE
STEPS = 256
CW = 512
HC = CW // HEAD_DIM
HALO = 16
MSG = 2 * STATE + 16
YMSG = STATE + 16
LOG2E = 1.4426950408889634
F32 = jnp.float32
BF16 = jnp.bfloat16
WF, WR, GF, GR, WV, GT = range(6)
MIB = 2**20


def dot(a, b, **kw):
    return jnp.dot(a, b, preferred_element_type=F32, **kw)


def shape(dtype, *dims):
    return jax.ShapeDtypeStruct(dims, dtype)


VMEM = pl.BlockSpec(memory_space=pltpu.VMEM)
HBM = pl.BlockSpec(memory_space=pltpu.HBM)


def vmem(dtype, *dims):
    return pltpu.VMEM(dims, dtype)


def call(kernel, name, outs, operands, params=(), scratch=(), limit=12, us=1.0, aliases=None):
    operands = [pltpu.with_memory_space_constraint(v, pltpu.VMEM) for v in operands]
    params = [pltpu.with_memory_space_constraint(v, pltpu.HBM) for v in params]
    return pl.pallas_call(
        kernel,
        name=name,
        in_specs=[VMEM] * len(operands) + [HBM] * len(params),
        out_specs=[HBM if isinstance(o, jax.ShapeDtypeStruct) else VMEM for o in outs],
        out_shape=outs,
        scratch_shapes=list(scratch),
        input_output_aliases=aliases or {},
        compiler_params=pltpu.CompilerParams(vmem_limit_bytes=limit * MIB),
        cost_estimate=pl.CostEstimate(flops=int(us * 1e8), bytes_accessed=int(us * 3e5), transcendentals=0),
    )(*operands, *params)


def place():
    at = lax.axis_index("seq")
    return at & 1, (at >> 1) & 1, at >> 2


def columns(start, width):
    return pl.ds(pl.multiple_of(start, 128), width)


def split2(x):
    hi = x.astype(BF16)
    lo = (x - hi.astype(F32)).astype(BF16)
    return hi, lo


def spread_matrix(start, width=CW):
    k = lax.broadcasted_iota(jnp.int32, (2 * HEADS, width), 0)
    col = lax.broadcasted_iota(jnp.int32, (2 * HEADS, width), 1)
    low = (k & (HEADS - 1)) * HEAD_DIM - start
    return jnp.where((col >= low) & (col < low + HEAD_DIM), 1.0, 0.0).astype(BF16)


def expand(table_ref, first, spread):
    both = dot(table_ref[first : first + 2].reshape(2 * TOK, 2 * HEADS), spread)
    return both[0:TOK], both[TOK:]


def read_decay(rows):
    rows = rows.astype(F32)
    return rows[0:1] + rows[1:2]


def decay_rows(d):
    hi, lo = split2(d)
    none = jnp.zeros((14, d.shape[1]), F32)
    return jnp.concatenate([hi.astype(F32), lo.astype(F32), none], axis=0).astype(BF16)


def make_tables(step, decay, skip, table_ref, mcol_ref, mrow_ref, drow_ref):
    a = -decay * step
    row = lax.broadcasted_iota(jnp.int32, (TOK, TOK), 0)
    col = lax.broadcasted_iota(jnp.int32, (TOK, TOK), 1)
    tri = jnp.where((row >= col) & ((row >= SUB) == (col >= SUB)), 1.0, 0.0).astype(BF16)
    p0 = a.astype(BF16)
    p1 = (a - p0.astype(F32)).astype(BF16)
    p2 = (a - p0.astype(F32) - p1.astype(F32)).astype(BF16)
    sums = dot(tri, jnp.concatenate([p0, p1, p2, jnp.zeros_like(p0)], axis=1))
    cum = sums[:, 0:HEADS] + sums[:, HEADS : 2 * HEADS] + sums[:, 2 * HEADS : 3 * HEADS]
    excl = cum - a
    e0 = cum[SUB - 1 : SUB]
    e1 = cum[TOK - 1 : TOK]
    ends = jnp.concatenate([jnp.broadcast_to(e0, (SUB, HEADS)), jnp.broadcast_to(e1, (SUB, HEADS))], axis=0)
    zero = jnp.zeros_like(cum)

    def put(at, value):
        hi, lo = split2(value)
        table_ref[at] = jnp.concatenate([hi, lo], axis=1)

    put(WF, step * jnp.exp(jnp.minimum(ends - cum, zero)))
    put(WR, step * jnp.exp(excl))
    put(GF, jnp.exp(cum))
    put(GR, jnp.exp(jnp.minimum(ends - excl, zero)))
    put(WV, step * jnp.exp(-0.5 * a))
    put(GT, jnp.exp(0.5 * a))
    m = (cum - 0.5 * a) * LOG2E
    mcol_ref[...] = jnp.concatenate([m, zero], axis=1)
    mrow_ref[...] = jnp.transpose(m)
    h0, l0 = split2(jnp.exp(e0))
    h1, l1 = split2(jnp.exp(e1))
    hd, ld = split2(jnp.exp(e0 + e1))
    hs, ls = split2(skip)
    no = jnp.zeros_like(h0)
    wide = [
        jnp.concatenate([hd, no], axis=1).astype(F32),
        jnp.concatenate([no, ld], axis=1).astype(F32),
        jnp.zeros((6, 2 * HEADS), F32),
        jnp.concatenate([h0, l0], axis=1).astype(F32),
        jnp.concatenate([h1, l1], axis=1).astype(F32),
        jnp.concatenate([hs, ls], axis=1).astype(F32),
        jnp.zeros((5, 2 * HEADS), F32),
    ]
    drow_ref[...] = jnp.concatenate(wide, axis=0).astype(BF16)


def conv(x, cf, cr):
    rows = x.shape[0]
    back = pltpu.roll(x, 1, 0)
    fore = pltpu.roll(x, rows - 1, 0)
    h = cf[3:4] * x + cf[2:3] * back + pltpu.roll(cf[1:2] * x + cf[0:1] * back, 2, 0)
    g = cr[3:4] * x + cr[2:3] * fore + pltpu.roll(cr[1:2] * x + cr[0:1] * fore, rows - 2, 0)
    return h, g


def silu_of_half(h):
    return (h + h * jnp.tanh(h)).astype(BF16)


def copy_all(pairs, sems):
    copies = [pltpu.make_async_copy(src, dst, sems.at[k]) for k, (src, dst) in enumerate(pairs)]
    for copy in copies:
        copy.start()
    return copies


def start_of(k, p):
    c, z, y = place()
    return (z if k == 3 else 1 - z) * QUART + p * CW


def edge_kernel(x_hbm, step_hbm, to_core_ref, to_chip_ref, step_ref, sems):
    c, z, y = place()
    far = columns((1 - c) * HALF, HALF)
    ends = pl.ds(pl.multiple_of(c * (TOK - HALO), HALO), HALO)
    copies = copy_all(
        [
            (step_hbm, step_ref),
            (x_hbm.at[ends], to_chip_ref),
            (x_hbm.at[:, far], to_core_ref.at[:, 0:HALF]),
            (x_hbm.at[:, INNER:E], to_core_ref.at[:, HALF:WIDE]),
        ],
        sems,
    )
    copies[0].wait()
    step = jnp.transpose(step_ref[...])
    p0 = step.astype(BF16).astype(F32)
    p1 = (step - p0).astype(BF16).astype(F32)
    p2 = step - p0 - p1
    to_core_ref[:, WIDE : WIDE + STEPS] = jnp.concatenate([p0, p1, p2, jnp.zeros_like(p0)], axis=1).astype(BF16)
    for copy in copies[1:]:
        copy.wait()


def halo_kernel(halo_ref, after_ref, mine_ref, to_core_ref):
    c, z, y = place()
    for ref, half in ((mine_ref, c), (to_core_ref, 1 - c)):
        ref[:, 0:HALF] = halo_ref[:, columns(half * HALF, HALF)]
        ref[:, HALF:WIDE] = halo_ref[:, INNER:E]


def conv_piece(x_ref, taps_ref, u_ref, start, halo=None):
    def body(i, _):
        at = columns(start + i * 128, 128)
        cols = columns(i * 128, 128)
        cf, cr = taps_ref[0:4, at], taps_ref[4:8, at]
        x0, x1 = x_ref[0, :, at].astype(F32), x_ref[1, :, at].astype(F32)
        before, after = halo(at) if halo else (x0[0:8], x1[TOK - 8 :])
        for b, rows in enumerate(((before, x0, x1[0:8]), (x0[TOK - 8 :], x1, after))):
            h, g = conv(jnp.concatenate(rows, axis=0), cf, cr)
            u_ref[b, 0, :, cols] = silu_of_half(h[8 : TOK + 8])
            u_ref[b, 1, :, cols] = silu_of_half(g[8 : TOK + 8])
        return _

    lax.fori_loop(0, u_ref.shape[3] // 128, body, 0)


def halo_of(chip_ref, core_ref):
    def rows(at):
        c, z, y = place()
        chip, core = chip_ref[:, at].astype(F32), core_ref[:, at].astype(F32)
        before, after = jnp.where(c == 0, chip, core), jnp.where(c == 0, core, chip)
        return before[HALO - 8 :], after[:8]

    return rows


def repair(x_ref, taps_ref, u_ref, start, halo):
    def body(i, _):
        at = columns(start + i * 256, 256)
        cols = columns(i * 256, 256)
        cf, cr = taps_ref[0:4, at], taps_ref[4:8, at]
        before, after = halo(at)
        h, _g = conv(jnp.concatenate([before, x_ref[0, 0:HALO, at].astype(F32)], axis=0), cf, cr)
        u_ref[0, 0, 0:HALO, cols] = silu_of_half(h[8:])
        _h, g = conv(jnp.concatenate([x_ref[1, TOK - HALO : TOK, at].astype(F32), after], axis=0), cf, cr)
        u_ref[1, 1, TOK - HALO : TOK, cols] = silu_of_half(g[:HALO])
        return _

    lax.fori_loop(0, u_ref.shape[3] // 256, body, 0)


def front_kernel(
    other_ref, x_hbm, step_hbm, decay_hbm, skip_hbm, cf_hbm, cr_hbm,
    x_ref, table_ref, mcol_ref, mrow_ref, drow_ref, taps_ref, kq_ref, u_ref,
    step_ref, decay_ref, skip_ref, cf_ref, cr_ref, sems,
):
    c, z, y = place()
    half = columns(c * HALF, HALF)
    copies = copy_all(
        [
            (step_hbm, step_ref),
            (decay_hbm, decay_ref),
            (skip_hbm, skip_ref),
            (x_hbm.at[:, half], x_ref.at[c, :, 0:HALF]),
            (x_hbm.at[:, INNER:E], x_ref.at[c, :, HALF:WIDE]),
            (cf_hbm.at[:, half], cf_ref.at[:, 0:HALF]),
            (cf_hbm.at[:, INNER:E], cf_ref.at[:, HALF:WIDE]),
            (cr_hbm.at[:, half], cr_ref.at[:, 0:HALF]),
            (cr_hbm.at[:, INNER:E], cr_ref.at[:, HALF:WIDE]),
            (other_ref.at[:, 0:WIDE], x_ref.at[1 - c]),
        ],
        sems,
    )
    for copy in copies[:3]:
        copy.wait()
    def half_of(values):
        return jnp.where(c == 0, values[:, 0 : HEADS // 2], values[:, HEADS // 2 : HEADS])

    parts = other_ref[:, WIDE : WIDE + STEPS].astype(F32)
    other = half_of(parts[:, 0:HEADS] + parts[:, HEADS : 2 * HEADS] + parts[:, 2 * HEADS : 3 * HEADS])
    mine = half_of(jnp.transpose(step_ref[...]))
    step = jnp.concatenate([jnp.where(c == 0, mine, other), jnp.where(c == 0, other, mine)], axis=1)
    decay, skip = half_of(decay_ref[...]), half_of(skip_ref[...])
    decay, skip = jnp.concatenate([decay, decay], axis=1), jnp.concatenate([skip, skip], axis=1)
    make_tables(step, decay, skip, table_ref, mcol_ref, mrow_ref, drow_ref)
    for copy in copies[3:]:
        copy.wait()
    taps_ref[0:4] = cf_ref[...] * 0.5
    taps_ref[4:8] = cr_ref[...] * 0.5
    conv_piece(x_ref, taps_ref, kq_ref, HALF)
    conv_piece(x_ref, taps_ref, u_ref, start_of(2, 0))


def piece_states(u_ref, kt_ref, table_ref, drow_ref, start, saved_ref, spread_ref, chip_ref):
    blocks = []
    for b in range(2):
        spread = spread_matrix(b * HALF + start)
        spread_ref[b] = spread
        drow = dot(drow_ref[...], spread)
        d0, d1 = drow[8:9], drow[9:10]

        weights = expand(table_ref, WF, spread)

        def weighted(d, r):
            return (u_ref[b, d, r : r + SUB].astype(F32) * weights[d][r : r + SUB]).astype(BF16)

        f0 = dot(kt_ref[b, 0, :, 0:SUB], weighted(0, 0))
        f1 = dot(kt_ref[b, 0, :, SUB:TOK], weighted(0, SUB))
        r0 = dot(kt_ref[b, 1, :, 0:SUB], weighted(1, 0))
        r1 = dot(kt_ref[b, 1, :, SUB:TOK], weighted(1, SUB))
        saved_ref[2 * b] = f0.astype(BF16)
        saved_ref[2 * b + 1] = r1.astype(BF16)
        blocks.append((d1 * f0 + f1, r0 + d0 * r1, drow[0:1] + drow[1:2]))
    (f0, r0, d0), (f1, r1, d1) = blocks
    saved_ref[4] = f0.astype(BF16)
    saved_ref[5] = r1.astype(BF16)
    chip_ref[0:STATE] = (d1 * f0 + f1).astype(BF16)
    chip_ref[STATE : 2 * STATE] = (r0 + d0 * r1).astype(BF16)
    chip_ref[2 * STATE : MSG] = decay_rows(d0 * d1)


def first_states_kernel(
    kq_in, u_in, x_ref, taps_ref, chip_halo_ref, core_halo_ref, table_ref, drow_ref, after_ref, gate_hbm,
    kq_ref, u_ref, kt_ref, saved_ref, spread_ref, chip_ref, gate_to_core_ref, sem,
):
    c, z, y = place()
    copy = pltpu.make_async_copy(gate_hbm.at[:, columns((1 - c) * HALF, HALF)], gate_to_core_ref, sem)
    copy.start()
    halo = halo_of(chip_halo_ref, core_halo_ref)
    repair(x_ref, taps_ref, kq_ref, HALF, halo)
    for b in range(2):
        for d in range(2):
            kt_ref[b, d] = jnp.transpose(kq_ref[b, d, :, 0:STATE].astype(F32)).astype(BF16)
    start = start_of(2, 0)
    repair(x_ref, taps_ref, u_ref, start, halo)
    piece_states(u_ref, kt_ref, table_ref, drow_ref, start, saved_ref, spread_ref, chip_ref)
    copy.wait()


def conv_kernel(x_ref, taps_ref, u_ref):
    conv_piece(x_ref, taps_ref, u_ref, start_of(2, 1))


def rest_kernel(todo, x_ref, taps_ref, chip_halo_ref, core_halo_ref, table_ref, drow_ref, kt_ref, after_ref, *outs):
    c, z, y = place()
    copies = []
    if todo == ((2, 1),):
        _u_in, *outs = outs
    if todo == ((3, 1),):
        gate_hbm, gain_hbm, *outs, gate_ref, gain_ref, sems = outs
        copies = copy_all([(gate_hbm.at[:, columns(c * HALF, HALF)], gate_ref), (gain_hbm, gain_ref)], sems)
    for n, piece in enumerate(todo):
        u_ref, saved_ref, spread_ref, chip_ref = outs[4 * n : 4 * n + 4]
        halo = halo_of(chip_halo_ref, core_halo_ref)
        if piece == (2, 1):
            repair(x_ref, taps_ref, u_ref, start_of(*piece), halo)
        else:
            conv_piece(x_ref, taps_ref, u_ref, start_of(*piece), halo)
        piece_states(u_ref, kt_ref, table_ref, drow_ref, start_of(*piece), saved_ref, spread_ref, chip_ref)
    for copy in copies:
        copy.wait()


KEYS = vmem(BF16, 2, 2, TOK, 2 * STATE)
U = vmem(BF16, 2, 2, TOK, CW)
SAVED = vmem(BF16, 6, STATE, CW)
SPREAD = vmem(BF16, 2, 2 * HEADS, CW)
CHIP = vmem(BF16, MSG, CW)


def group(keep_ref, got_ref, outs):
    c, z, y = place()
    z0 = z == 0
    dm, do = read_decay(keep_ref[2 * STATE : MSG]), read_decay(got_ref[2 * STATE : MSG])
    one = jnp.ones_like(dm)
    am, ao = jnp.where(z0, do, one), jnp.where(z0, one, dm)
    fwd = (am * keep_ref[0:STATE].astype(F32) + ao * got_ref[0:STATE].astype(F32)).astype(BF16)
    am, ao = jnp.where(z0, one, do), jnp.where(z0, dm, one)
    rows = slice(STATE, 2 * STATE)
    rev = (am * keep_ref[rows].astype(F32) + ao * got_ref[rows].astype(F32)).astype(BF16)
    decay = decay_rows(dm * do)
    for k in range(1, 4):
        outs[k - 1][0:STATE] = jnp.where(y + k < 4, fwd, rev)
        outs[k - 1][STATE:YMSG] = decay


def entries(keep_ref, got_ref, r1_ref, r2_ref, r3_ref, mine_ref, back_ref):
    c, z, y = place()
    z0 = z == 0
    r = [ref[0:STATE].astype(F32) for ref in (r1_ref, r2_ref, r3_ref)]
    d = [read_decay(ref[STATE:YMSG]) for ref in (r1_ref, r2_ref, r3_ref)]
    zero = jnp.zeros_like(r[0])
    ef = jnp.where(y >= 3, r[2], zero)
    ef = jnp.where(y >= 2, r[1] + d[1] * ef, zero)
    ef = jnp.where(y >= 1, r[0] + d[0] * ef, zero)
    er = jnp.where(y <= 0, r[0], zero)
    er = jnp.where(y <= 1, r[1] + d[1] * er, zero)
    er = jnp.where(y <= 2, r[2] + d[2] * er, zero)
    dm, do = read_decay(keep_ref[2 * STATE : MSG]), read_decay(got_ref[2 * STATE : MSG])
    df = jnp.where(z0, dm, do)
    tf = jnp.where(z0, keep_ref[0:STATE].astype(F32), got_ref[0:STATE].astype(F32))
    second_f = df * ef + tf
    dr = jnp.where(z0, do, dm)
    rows = slice(STATE, 2 * STATE)
    tr = jnp.where(z0, got_ref[rows].astype(F32), keep_ref[rows].astype(F32))
    first_r = dr * er + tr
    mine_ref[0] = jnp.where(z0, ef, second_f).astype(BF16)
    mine_ref[1] = jnp.where(z0, first_r, er).astype(BF16)
    back_ref[0] = jnp.where(z0, second_f, ef).astype(BF16)
    back_ref[1] = jnp.where(z0, er, first_r).astype(BF16)


def group_kernel(keep_ref, got_ref, *refs):
    group(keep_ref, got_ref, refs[-3:])


def entries_kernel(keep_ref, got_ref, r1_ref, r2_ref, r3_ref, *refs):
    entries(keep_ref, got_ref, r1_ref, r2_ref, r3_ref, *refs[-2:])


def within_kernel(k, p, u_ref, spread_ref, kq_ref, table_ref, mcol_ref, mrow_ref, drow_ref, after_ref, *refs):
    make_qk = len(refs) == 2 and refs[1].shape[0] == 2 and len(refs[1].shape) == 5
    qk_ref, out_ref = (refs[1], refs[0]) if make_qk else refs
    row = lax.broadcasted_iota(jnp.int32, (SUB, SUB), 0)
    col = lax.broadcasted_iota(jnp.int32, (SUB, SUB), 1)
    low = lax.broadcasted_iota(jnp.int32, (SUB, 2 * HEAD_DIM), 1) < HEAD_DIM

    def block(b, _):
        if make_qk:
            for s in range(2):
                rows = slice(s * SUB, (s + 1) * SUB)
                for d in range(2):
                    keys = kq_ref[b, d, rows, 0:STATE]
                    queries = kq_ref[b, d, rows, STATE : 2 * STATE]
                    prod = lax.dot_general(queries, keys, (((1,), (1,)), ((), ())), preferred_element_type=F32)
                    qk_ref[b, d, s] = jnp.where((row >= col) if d == 0 else (row <= col), prod, 0.0)
        start = b * HALF + start_of(k, p)
        first = start // HEAD_DIM
        spread = spread_ref[b]
        skip = dot(drow_ref[...], spread)[10:11]
        mcol = pltpu.roll(mcol_ref[...], 2 * HEADS - first, 1)
        mrow = mrow_ref[pl.ds(pl.multiple_of(first, HC), HC), :]
        wv, gt = expand(table_ref, WV, spread)
        for s in range(2):
            rows = slice(s * SUB, (s + 1) * SUB)
            for two in range(HC // 2):
                cols = slice(two * 128, (two + 1) * 128)
                up = u_ref[b, 0, rows, cols].astype(F32)
                xf = (up * wv[rows, cols]).astype(BF16)
                xb = (u_ref[b, 1, rows, cols].astype(F32) * wv[rows, cols]).astype(BF16)
                none = jnp.zeros_like(xf)
                left, right = [], []
                for h in range(2):
                    at = two * 2 + h
                    diff = mcol[rows, at : at + 1] - mrow[at : at + 1, rows]
                    decay = jnp.exp2(-jnp.abs(diff))
                    left += [(decay * qk_ref[b, 0, s]).astype(BF16), (decay * qk_ref[b, 1, s]).astype(BF16)]
                    keep = low if h == 0 else ~low
                    right += [jnp.where(keep, xf, none), jnp.where(keep, xb, none)]
                res = dot(jnp.concatenate(left, axis=1), jnp.concatenate(right, axis=0))
                out_ref[b, rows, cols] = (res * gt[rows, cols] + up * skip[:, cols]).astype(BF16)
        return _

    lax.fori_loop(0, 2, block, 0)


QK = vmem(F32, 2, 2, 2, SUB, SUB)


def make_within(k, p, u, spread, kq, table, mcol, mrow, drow, after, qk=None):
    outs = [vmem(BF16, 2, TOK, CW)]
    operands = (u, spread, kq, table, mcol, mrow, drow, after)
    kernel = functools.partial(within_kernel, k, p)
    if qk is None:
        return call(kernel, f"within_{k}{p}", [*outs, QK], operands)
    return call(kernel, f"within_{k}{p}", outs, (*operands, qk))[0]


def finish_part(k, p, other, entry_ref, saved_ref, spread_ref, within_ref, gate_ref, kq_ref, table_ref, drow_ref, put, square):
    c, z, y = place()
    b = 1 - c if other else c
    start = start_of(k, p)
    at = columns(start, CW)
    spread = spread_ref[b]
    drow = dot(drow_ref[...], spread)
    d0, d1 = drow[8:9], drow[9:10]
    far = dot(drow_ref[...], spread_ref[1 - b])
    far = far[0:1] + far[1:2]
    one = jnp.ones_like(far)
    none = jnp.zeros((STATE, CW), F32)
    first = b == 0
    ef = jnp.where(first, one, far) * entry_ref[0].astype(F32) + jnp.where(first, none, saved_ref[4].astype(F32))
    er = jnp.where(first, far, one) * entry_ref[1].astype(F32) + jnp.where(first, saved_ref[5].astype(F32), none)
    inside = [
        (ef.astype(BF16), (er * d1 + saved_ref[2 * b + 1].astype(F32)).astype(BF16)),
        ((ef * d0 + saved_ref[2 * b].astype(F32)).astype(BF16), er.astype(BF16)),
    ]
    gf, gr = expand(table_ref, GF, spread)
    for s in range(2):
        rows = slice(s * SUB, (s + 1) * SUB)
        cf = dot(kq_ref[b, 0, rows, STATE : 2 * STATE], inside[s][0])
        cr = dot(kq_ref[b, 1, rows, STATE : 2 * STATE], inside[s][1])
        mixed = within_ref[b, rows].astype(F32) + gf[rows] * cf + gr[rows] * cr
        half = gate_ref[rows, at].astype(F32) * 0.5
        gated = mixed * (half + half * jnp.tanh(half))
        put(rows, gated)
        sq = gated * gated
        for j in range(0, CW, 128):
            part = sq[:, j : j + 128]
            square[s] = part if square[s] is None else square[s] + part


def halves(refs):
    return refs if len(refs) == 2 else (refs[0].at[0:SUB], refs[0].at[SUB:TOK])


def finish_piece(k, p, entry_ref, saved_ref, spread_ref, within_ref, gates, shared, own_ref, msg_refs, squares):
    def put_own(rows, gated):
        own_ref[rows] = gated

    def put_other(rows, gated):
        msg_refs[rows.start // SUB][:, 0:CW] = gated.astype(BF16)

    for other, put in ((1, put_other), (0, put_own)):
        finish_part(k, p, other, entry_ref, saved_ref, spread_ref, within_ref, gates[other], *shared, put, squares[other])


NEAR = ((3, 0), (3, 1), (2, 0))
BACK = (2, 1)


def finish_near_kernel(k, p, entry_ref, saved_ref, spread_ref, within_ref, gate_ref, gate_other_ref, *refs):
    shared, (square_in, own_ref, *msg_refs, square_ref) = refs[:3], refs[3:]
    msg_refs = halves(msg_refs)
    squares = [[None, None], [None, None]]
    gates = (gate_ref, gate_other_ref)
    finish_piece(k, p, entry_ref, saved_ref, spread_ref, within_ref, gates, shared, own_ref, msg_refs, squares)
    for other in range(2):
        for s in range(2):
            rows = slice(s * SUB, (s + 1) * SUB)
            if (k, p) == NEAR[0]:
                square_ref[other, rows] = squares[other][s]
            else:
                square_ref[other, rows] = square_in[other, rows] + squares[other][s]


def finish_other_kernel(entry_ref, saved_ref, spread_ref, within_ref, gate_ref, *refs):
    shared, square_in, msg_refs = refs[:3], refs[3], halves(refs[-1:])
    square = [square_in[1, s * SUB : (s + 1) * SUB] for s in range(2)]

    def put(rows, gated):
        msg_refs[rows.start // SUB][:, 0:CW] = gated.astype(BF16)

    finish_part(*BACK, 1, entry_ref, saved_ref, spread_ref, within_ref, gate_ref, *shared, put, square)
    lane = lax.broadcasted_iota(jnp.int32, (SUB, 128), 1)
    for s in range(2):
        total = jnp.sum(square[s], axis=1, keepdims=True)
        hi = total.astype(BF16).astype(F32)
        sums = jnp.where(lane == 0, hi, jnp.where(lane == 1, total - hi, 0.0))
        msg_refs[s][:, CW : CW + 128] = sums.astype(BF16)


def finish_own_kernel(entry_ref, saved_ref, spread_ref, within_ref, gate_ref, *refs):
    shared, (square_in, after_ref, own_ref, square_ref) = refs[:3], refs[3:]
    square = [square_in[0, s * SUB : (s + 1) * SUB] for s in range(2)]

    def put(rows, gated):
        own_ref[rows] = gated

    finish_part(*BACK, 0, entry_ref, saved_ref, spread_ref, within_ref, gate_ref, *shared, put, square)
    for s in range(2):
        square_ref[s * SUB : (s + 1) * SUB] = square[s]


def norm_kernel(*refs):
    own_refs, other_refs, (square_ref, gain_ref, out_hbm, out_ref, sems) = refs[:4], refs[4:8], refs[8:]
    other_refs = [halves([ref]) for ref in other_refs]
    c, z, y = place()
    pieces = []
    for n, piece in enumerate((*NEAR, BACK)):
        pieces.append(((own_refs[n], own_refs[n].at[SUB:TOK]), c * HALF + start_of(*piece)))
        pieces.append((other_refs[n], (1 - c) * HALF + start_of(*piece)))
    step = 32
    copies = []
    for r in range(0, TOK, step):
        rows, inside = slice(r, r + step), slice(r % SUB, r % SUB + step)
        total = square_ref[rows] + other_refs[3][r // SUB][inside, CW : CW + 128].astype(F32)
        scale = lax.rsqrt(jnp.sum(total, axis=1, keepdims=True) * (1.0 / INNER) + 1e-05)
        for refs, start in pieces:
            at = columns(start, CW)
            out_ref[rows, at] = (refs[r // SUB][inside, 0:CW].astype(F32) * scale * gain_ref[:, at]).astype(BF16)
        copies.append(pltpu.make_async_copy(out_ref.at[rows], out_hbm.at[rows], sems.at[len(copies)]))
        copies[-1].start()
    for copy in copies:
        copy.wait()


def per_device(mixer_input, gate_input, conv_forward, conv_reverse, step_size, decay_rate, skip_scale, norm_gain):
    n = lax.axis_size("seq")

    def send(v, perm):
        return lax.ppermute(v, "seq", perm)

    core = [(i, i ^ 1) for i in range(n)]
    zswap = [(i, i ^ 2) for i in range(n)]
    chips = [(i, i + 1) for i in range(1, n - 1, 2)] + [(i + 1, i) for i in range(1, n - 1, 2)]

    def along_y(msgs):
        return [send(m, [(i, (i + 4 * k) % n) for i in range(n)]) for k, m in enumerate(msgs, 1)]

    to_core, to_chip = call(
        edge_kernel,
        "edges",
        [vmem(BF16, TOK, WIDE + STEPS), vmem(BF16, HALO, E)],
        (),
        (mixer_input, step_size),
        [pltpu.VMEM((HEADS, TOK), F32), pltpu.SemaphoreType.DMA((4,))],
    )
    x, table, mcol, mrow, drow, taps, kq, u2a = call(
        front_kernel,
        "front",
        [
            vmem(BF16, 2, TOK, WIDE),
            vmem(BF16, 6, TOK, 2 * HEADS),
            vmem(F32, TOK, 2 * HEADS),
            vmem(F32, HEADS, TOK),
            vmem(BF16, 16, 2 * HEADS),
            vmem(F32, 8, WIDE),
            KEYS,
            U,
        ],
        (send(to_core, core),),
        (
            mixer_input,
            step_size,
            decay_rate.reshape(1, HEADS),
            skip_scale.reshape(1, HEADS),
            conv_forward,
            conv_reverse,
        ),
        [
            pltpu.VMEM((HEADS, TOK), F32),
            pltpu.VMEM((1, HEADS), F32),
            pltpu.VMEM((1, HEADS), F32),
            pltpu.VMEM((4, WIDE), F32),
            pltpu.VMEM((4, WIDE), F32),
            pltpu.SemaphoreType.DMA((10,)),
        ],
    )
    chip_halo, to_core = call(
        halo_kernel, "halo", [vmem(BF16, HALO, WIDE)] * 2, (send(to_chip, chips), kq)
    )
    halo = (x, taps, chip_halo, send(to_core, core))
    (u2b,) = call(conv_kernel, "conv_21", [U], (x, taps))
    kq, u2a, kt, saved2a, spread2a, zsend0, gate_to_core = call(
        first_states_kernel,
        "states_first",
        [KEYS, U, vmem(BF16, 2, 2, STATE, TOK), SAVED, SPREAD, CHIP, vmem(BF16, TOK, HALF)],
        (kq, u2a, *halo, table, drow, u2b),
        (gate_input,),
        [pltpu.SemaphoreType.DMA(())],
        aliases={0: 0, 1: 1},
    )
    got0 = send(zsend0, zswap)

    def make_rest(name, todo, after):
        kernel = functools.partial(rest_kernel, todo)
        outs = [U, SAVED, SPREAD, CHIP]
        operands = (*halo, table, drow, kt, after)
        if todo == ((2, 1),):
            return call(kernel, name, outs, (*operands, u2b), aliases={8: 0})
        if todo == ((3, 1),):
            outs += [vmem(BF16, TOK, HALF), vmem(F32, 1, INNER)]
            params = (gate_input, norm_gain.reshape(1, INNER))
            return call(kernel, name, outs, operands, params, [pltpu.SemaphoreType.DMA((2,))])
        return call(kernel, name, outs, operands)

    u3a, saved3a, spread3a, keep0 = make_rest("states_30", ((3, 0),), zsend0)
    u2b, saved2b, spread2b, zsend1 = make_rest("states_21", ((2, 1),), keep0)
    got1 = send(zsend1, zswap)
    u3b, saved3b, spread3b, keep1, gate, gain = make_rest("states_31", ((3, 1),), zsend1)
    gates = (gate, send(gate_to_core, core))
    tables = (kq, table, mcol, mrow, drow)
    yout = [vmem(BF16, YMSG, CW)] * 3
    entry = vmem(BF16, 2, STATE, CW)

    w2a, qk = make_within(2, 0, u2a, spread2a, *tables, keep1)
    msgs = call(group_kernel, "group_a", yout, (keep0, got0, w2a, gates[1]))
    arrived0 = along_y(msgs)
    w2b = make_within(2, 1, u2b, spread2b, *tables, msgs[0], qk)
    msgs = call(group_kernel, "group_b", yout, (keep1, got1, w2b))
    arrived1 = along_y(msgs)
    mine0, back0 = call(entries_kernel, "entries_a", [entry, entry], (keep0, got0, *arrived0, msgs[0]))
    back0 = send(back0, zswap)
    w3a = make_within(3, 0, u3a, spread3a, *tables, mine0, qk)
    mine1, back1 = call(entries_kernel, "entries_b", [entry, entry], (keep1, got1, *arrived1, w3a))
    back1 = send(back1, zswap)
    w3b = make_within(3, 1, u3b, spread3b, *tables, mine1, qk)
    shared = (kq, table, drow)
    square = kt
    own, other = [], []
    parts = (
        (mine0, saved3a, spread3a, w3a),
        (mine1, saved3b, spread3b, w3b),
        (back0, saved2a, spread2a, w2a),
    )
    message = [vmem(BF16, TOK, CW)]
    for (k, p), part in zip(NEAR, parts):
        gated, *msg, square = call(
            functools.partial(finish_near_kernel, k, p),
            f"finish_{k}{p}",
            [vmem(F32, TOK, CW), *message, vmem(F32, 2, TOK, 128)],
            (*part, *gates, *shared, square),
        )
        own.append(gated)
        other += [send(m, core) for m in msg]
    msg = call(
        finish_other_kernel,
        "finish_other",
        [vmem(BF16, TOK, CW + 128)],
        (back1, saved2b, spread2b, w2b, *gates[1:], *shared, square, *other[:2]),
    )
    other += [send(m, core) for m in msg]
    gated, square = call(
        finish_own_kernel,
        "finish_own",
        [vmem(F32, TOK, CW), vmem(F32, TOK, 128)],
        (back1, saved2b, spread2b, w2b, gates[0], *shared, square, msg[0]),
    )
    own.append(gated)
    (out,) = call(
        norm_kernel,
        "norm",
        [shape(BF16, TOK, INNER)],
        (*own, *other, square, gain),
        (),
        [pltpu.VMEM((TOK, INNER), BF16), pltpu.SemaphoreType.DMA((8,))],
    )
    return out


def solution(mesh):
    in_specs = (
        P(("row", "seq"), None),
        P(("row", "seq"), None),
        P(),
        P(),
        P(None, ("row", "seq")),
        P("row"),
        P(),
        P(),
    )
    out_specs = P(("row", "seq"), None)
    return jax.shard_map(per_device, mesh=mesh, in_specs=in_specs, out_specs=out_specs, check_vma=False)
```

```python
import functools

import jax
import jax.numpy as jnp
from jax import lax
from jax.experimental import pallas as pl
from jax.experimental.pallas import tpu as pltpu
from jax.sharding import PartitionSpec as P

HEADS = 64
HEAD_DIM = 64
STATE = 128
TOK = 256
SUB = 128
INNER = 4096
E = 4352
HALF = INNER // 2
QUART = INNER // 4
WIDE = HALF + 2 * STATE
STEPS = 256
CW = 512
HC = CW // HEAD_DIM
HALO = 16
MSG = 2 * STATE + 16
YMSG = STATE + 16
LOG2E = 1.4426950408889634
F32 = jnp.float32
BF16 = jnp.bfloat16
WF, WR, GF, GR, WV, GT = range(6)
MIB = 2**20


def dot(a, b, **kw):
    return jnp.dot(a, b, preferred_element_type=F32, **kw)


def shape(dtype, *dims):
    return jax.ShapeDtypeStruct(dims, dtype)


VMEM = pl.BlockSpec(memory_space=pltpu.VMEM)
HBM = pl.BlockSpec(memory_space=pltpu.HBM)


def vmem(dtype, *dims):
    return pltpu.VMEM(dims, dtype)


def call(kernel, name, outs, operands, params=(), scratch=(), limit=12, us=1.0, aliases=None):
    operands = [pltpu.with_memory_space_constraint(v, pltpu.VMEM) for v in operands]
    params = [pltpu.with_memory_space_constraint(v, pltpu.HBM) for v in params]
    return pl.pallas_call(
        kernel,
        name=name,
        in_specs=[VMEM] * len(operands) + [HBM] * len(params),
        out_specs=[HBM if isinstance(o, jax.ShapeDtypeStruct) else VMEM for o in outs],
        out_shape=outs,
        scratch_shapes=list(scratch),
        input_output_aliases=aliases or {},
        compiler_params=pltpu.CompilerParams(vmem_limit_bytes=limit * MIB),
        cost_estimate=pl.CostEstimate(flops=int(us * 1e8), bytes_accessed=int(us * 3e5), transcendentals=0),
    )(*operands, *params)


def place():
    at = lax.axis_index("seq")
    return at & 1, (at >> 1) & 1, at >> 2


def columns(start, width):
    return pl.ds(pl.multiple_of(start, 128), width)


def split2(x):
    hi = x.astype(BF16)
    lo = (x - hi.astype(F32)).astype(BF16)
    return hi, lo


def spread_matrix(start, width=CW):
    k = lax.broadcasted_iota(jnp.int32, (2 * HEADS, width), 0)
    col = lax.broadcasted_iota(jnp.int32, (2 * HEADS, width), 1)
    low = (k & (HEADS - 1)) * HEAD_DIM - start
    return jnp.where((col >= low) & (col < low + HEAD_DIM), 1.0, 0.0).astype(BF16)


def expand(table_ref, drow_ref, first, spread):
    rows = jnp.concatenate([table_ref[first : first + 2].reshape(2 * TOK, 2 * HEADS), drow_ref[...]], axis=0)
    wide = dot(rows, spread)
    return wide[0:TOK], wide[TOK : 2 * TOK], wide[2 * TOK :]


def read_decay(rows):
    rows = rows.astype(F32)
    return rows[0:1] + rows[1:2]


def decay_rows(d):
    hi, lo = split2(d)
    none = jnp.zeros((14, d.shape[1]), F32)
    return jnp.concatenate([hi.astype(F32), lo.astype(F32), none], axis=0).astype(BF16)


def make_tables(step, decay, skip, table_ref, mcol_ref, mrow_ref, drow_ref):
    a = -decay * step
    row = lax.broadcasted_iota(jnp.int32, (TOK, TOK), 0)
    col = lax.broadcasted_iota(jnp.int32, (TOK, TOK), 1)
    tri = jnp.where((row >= col) & ((row >= SUB) == (col >= SUB)), 1.0, 0.0).astype(BF16)
    p0 = a.astype(BF16)
    p1 = (a - p0.astype(F32)).astype(BF16)
    p2 = (a - p0.astype(F32) - p1.astype(F32)).astype(BF16)
    sums = dot(tri, jnp.concatenate([p0, p1, p2, jnp.zeros_like(p0)], axis=1))
    cum = sums[:, 0:HEADS] + sums[:, HEADS : 2 * HEADS] + sums[:, 2 * HEADS : 3 * HEADS]
    excl = cum - a
    e0 = cum[SUB - 1 : SUB]
    e1 = cum[TOK - 1 : TOK]
    ends = jnp.concatenate([jnp.broadcast_to(e0, (SUB, HEADS)), jnp.broadcast_to(e1, (SUB, HEADS))], axis=0)
    zero = jnp.zeros_like(cum)

    def put(at, value):
        hi, lo = split2(value)
        table_ref[at] = jnp.concatenate([hi, lo], axis=1)

    put(WF, step * jnp.exp(jnp.minimum(ends - cum, zero)))
    put(WR, step * jnp.exp(excl))
    put(GF, jnp.exp(cum))
    put(GR, jnp.exp(jnp.minimum(ends - excl, zero)))
    put(WV, step * jnp.exp(-0.5 * a))
    put(GT, jnp.exp(0.5 * a))
    m = (cum - 0.5 * a) * LOG2E
    mcol_ref[...] = jnp.concatenate([m, zero], axis=1)
    mrow_ref[...] = jnp.transpose(m)
    h0, l0 = split2(jnp.exp(e0))
    h1, l1 = split2(jnp.exp(e1))
    hd, ld = split2(jnp.exp(e0 + e1))
    hs, ls = split2(skip)
    no = jnp.zeros_like(h0)
    wide = [
        jnp.concatenate([hd, no], axis=1).astype(F32),
        jnp.concatenate([no, ld], axis=1).astype(F32),
        jnp.zeros((6, 2 * HEADS), F32),
        jnp.concatenate([h0, l0], axis=1).astype(F32),
        jnp.concatenate([h1, l1], axis=1).astype(F32),
        jnp.concatenate([hs, ls], axis=1).astype(F32),
        jnp.zeros((5, 2 * HEADS), F32),
    ]
    drow_ref[...] = jnp.concatenate(wide, axis=0).astype(BF16)


def conv(x, cf, cr):
    rows = x.shape[0]
    back = pltpu.roll(x, 1, 0)
    fore = pltpu.roll(x, rows - 1, 0)
    h = cf[3:4] * x + cf[2:3] * back + pltpu.roll(cf[1:2] * x + cf[0:1] * back, 2, 0)
    g = cr[3:4] * x + cr[2:3] * fore + pltpu.roll(cr[1:2] * x + cr[0:1] * fore, rows - 2, 0)
    return h, g


def silu_of_half(h):
    return (h + h * jnp.tanh(h)).astype(BF16)


def copy_all(pairs, sems):
    copies = [pltpu.make_async_copy(src, dst, sems.at[k]) for k, (src, dst) in enumerate(pairs)]
    for copy in copies:
        copy.start()
    return copies


def start_of(k, p):
    c, z, y = place()
    return (z if k == 3 else 1 - z) * QUART + p * CW


def edge_kernel(x_hbm, step_hbm, to_core_ref, to_chip_ref, step_ref, sems):
    c, z, y = place()
    far = columns((1 - c) * HALF, HALF)
    ends = pl.ds(pl.multiple_of(c * (TOK - HALO), HALO), HALO)
    copies = copy_all(
        [
            (step_hbm, step_ref),
            (x_hbm.at[ends], to_chip_ref),
            (x_hbm.at[:, far], to_core_ref.at[:, 0:HALF]),
            (x_hbm.at[:, INNER:E], to_core_ref.at[:, HALF:WIDE]),
        ],
        sems,
    )
    copies[0].wait()
    step = jnp.transpose(step_ref[...])
    p0 = step.astype(BF16).astype(F32)
    p1 = (step - p0).astype(BF16).astype(F32)
    p2 = step - p0 - p1
    to_core_ref[:, WIDE : WIDE + STEPS] = jnp.concatenate([p0, p1, p2, jnp.zeros_like(p0)], axis=1).astype(BF16)
    for copy in copies[1:]:
        copy.wait()


def halo_kernel(halo_ref, after_ref, mine_ref, to_core_ref):
    c, z, y = place()
    for ref, half in ((mine_ref, c), (to_core_ref, 1 - c)):
        ref[:, 0:HALF] = halo_ref[:, columns(half * HALF, HALF)]
        ref[:, HALF:WIDE] = halo_ref[:, INNER:E]


def conv_piece(x_ref, taps_ref, u_ref, start, halo=None):
    def body(i, _):
        at = columns(start + i * 128, 128)
        cols = columns(i * 128, 128)
        cf, cr = taps_ref[0:4, at], taps_ref[4:8, at]
        x0, x1 = x_ref[0, :, at].astype(F32), x_ref[1, :, at].astype(F32)
        before, after = halo(at) if halo else (x0[0:8], x1[TOK - 8 :])
        for b, rows in enumerate(((before, x0, x1[0:8]), (x0[TOK - 8 :], x1, after))):
            h, g = conv(jnp.concatenate(rows, axis=0), cf, cr)
            u_ref[b, 0, :, cols] = silu_of_half(h[8 : TOK + 8])
            u_ref[b, 1, :, cols] = silu_of_half(g[8 : TOK + 8])
        return _

    lax.fori_loop(0, u_ref.shape[3] // 128, body, 0)


def halo_of(chip_ref, core_ref):
    def rows(at):
        c, z, y = place()
        chip, core = chip_ref[:, at].astype(F32), core_ref[:, at].astype(F32)
        before, after = jnp.where(c == 0, chip, core), jnp.where(c == 0, core, chip)
        return before[HALO - 8 :], after[:8]

    return rows


def repair(x_ref, taps_ref, u_ref, start, halo):
    def body(i, _):
        at = columns(start + i * 256, 256)
        cols = columns(i * 256, 256)
        cf, cr = taps_ref[0:4, at], taps_ref[4:8, at]
        before, after = halo(at)
        h, _g = conv(jnp.concatenate([before, x_ref[0, 0:HALO, at].astype(F32)], axis=0), cf, cr)
        u_ref[0, 0, 0:HALO, cols] = silu_of_half(h[8:])
        _h, g = conv(jnp.concatenate([x_ref[1, TOK - HALO : TOK, at].astype(F32), after], axis=0), cf, cr)
        u_ref[1, 1, TOK - HALO : TOK, cols] = silu_of_half(g[:HALO])
        return _

    lax.fori_loop(0, u_ref.shape[3] // 256, body, 0)


def front_kernel(
    other_ref, x_hbm, step_hbm, decay_hbm, skip_hbm, cf_hbm, cr_hbm,
    x_ref, table_ref, mcol_ref, mrow_ref, drow_ref, taps_ref, kq_ref, u_ref,
    step_ref, decay_ref, skip_ref, cf_ref, cr_ref, sems,
):
    c, z, y = place()
    half = columns(c * HALF, HALF)
    copies = copy_all(
        [
            (step_hbm, step_ref),
            (decay_hbm, decay_ref),
            (skip_hbm, skip_ref),
            (x_hbm.at[:, half], x_ref.at[c, :, 0:HALF]),
            (x_hbm.at[:, INNER:E], x_ref.at[c, :, HALF:WIDE]),
            (cf_hbm.at[:, half], cf_ref.at[:, 0:HALF]),
            (cf_hbm.at[:, INNER:E], cf_ref.at[:, HALF:WIDE]),
            (cr_hbm.at[:, half], cr_ref.at[:, 0:HALF]),
            (cr_hbm.at[:, INNER:E], cr_ref.at[:, HALF:WIDE]),
            (other_ref.at[:, 0:WIDE], x_ref.at[1 - c]),
        ],
        sems,
    )
    for copy in copies[:3]:
        copy.wait()
    def half_of(values):
        return jnp.where(c == 0, values[:, 0 : HEADS // 2], values[:, HEADS // 2 : HEADS])

    parts = other_ref[:, WIDE : WIDE + STEPS].astype(F32)
    other = half_of(parts[:, 0:HEADS] + parts[:, HEADS : 2 * HEADS] + parts[:, 2 * HEADS : 3 * HEADS])
    mine = half_of(jnp.transpose(step_ref[...]))
    step = jnp.concatenate([jnp.where(c == 0, mine, other), jnp.where(c == 0, other, mine)], axis=1)
    decay, skip = half_of(decay_ref[...]), half_of(skip_ref[...])
    decay, skip = jnp.concatenate([decay, decay], axis=1), jnp.concatenate([skip, skip], axis=1)
    make_tables(step, decay, skip, table_ref, mcol_ref, mrow_ref, drow_ref)
    for copy in copies[3:]:
        copy.wait()
    taps_ref[0:4] = cf_ref[...] * 0.5
    taps_ref[4:8] = cr_ref[...] * 0.5
    conv_piece(x_ref, taps_ref, kq_ref, HALF)
    conv_piece(x_ref, taps_ref, u_ref, start_of(2, 0))


def piece_states(u_ref, kt_ref, table_ref, drow_ref, start, saved_ref, spread_ref, chip_ref):
    blocks = []
    for b in range(2):
        spread = spread_matrix(b * HALF + start)
        spread_ref[b] = spread
        *weights, drow = expand(table_ref, drow_ref, WF, spread)
        d0, d1 = drow[8:9], drow[9:10]

        def weighted(d, r):
            return (u_ref[b, d, r : r + SUB].astype(F32) * weights[d][r : r + SUB]).astype(BF16)

        f0 = dot(kt_ref[b, 0, :, 0:SUB], weighted(0, 0))
        f1 = dot(kt_ref[b, 0, :, SUB:TOK], weighted(0, SUB))
        r0 = dot(kt_ref[b, 1, :, 0:SUB], weighted(1, 0))
        r1 = dot(kt_ref[b, 1, :, SUB:TOK], weighted(1, SUB))
        saved_ref[2 * b] = f0.astype(BF16)
        saved_ref[2 * b + 1] = r1.astype(BF16)
        blocks.append((d1 * f0 + f1, r0 + d0 * r1, drow[0:1] + drow[1:2]))
    (f0, r0, d0), (f1, r1, d1) = blocks
    saved_ref[4] = f0.astype(BF16)
    saved_ref[5] = r1.astype(BF16)
    chip_ref[0:STATE] = (d1 * f0 + f1).astype(BF16)
    chip_ref[STATE : 2 * STATE] = (r0 + d0 * r1).astype(BF16)
    chip_ref[2 * STATE : MSG] = decay_rows(d0 * d1)


def first_states_kernel(
    kq_in, u_in, x_ref, taps_ref, chip_halo_ref, core_halo_ref, table_ref, drow_ref, after_ref, gate_hbm,
    kq_ref, u_ref, kt_ref, saved_ref, spread_ref, chip_ref, gate_to_core_ref, sem,
):
    c, z, y = place()
    copy = pltpu.make_async_copy(gate_hbm.at[:, columns((1 - c) * HALF, HALF)], gate_to_core_ref, sem)
    copy.start()
    halo = halo_of(chip_halo_ref, core_halo_ref)
    repair(x_ref, taps_ref, kq_ref, HALF, halo)
    for b in range(2):
        for d in range(2):
            kt_ref[b, d] = jnp.transpose(kq_ref[b, d, :, 0:STATE].astype(F32)).astype(BF16)
    start = start_of(2, 0)
    repair(x_ref, taps_ref, u_ref, start, halo)
    piece_states(u_ref, kt_ref, table_ref, drow_ref, start, saved_ref, spread_ref, chip_ref)
    copy.wait()


def conv_kernel(x_ref, taps_ref, u_ref):
    conv_piece(x_ref, taps_ref, u_ref, start_of(2, 1))


def rest_kernel(todo, x_ref, taps_ref, chip_halo_ref, core_halo_ref, table_ref, drow_ref, kt_ref, after_ref, *outs):
    c, z, y = place()
    copies = []
    if todo == ((2, 1),):
        _u_in, *outs = outs
    if todo == ((3, 1),):
        gate_hbm, gain_hbm, *outs, gate_ref, gain_ref, sems = outs
        copies = copy_all([(gate_hbm.at[:, columns(c * HALF, HALF)], gate_ref), (gain_hbm, gain_ref)], sems)
    for n, piece in enumerate(todo):
        u_ref, saved_ref, spread_ref, chip_ref = outs[4 * n : 4 * n + 4]
        halo = halo_of(chip_halo_ref, core_halo_ref)
        if piece == (2, 1):
            repair(x_ref, taps_ref, u_ref, start_of(*piece), halo)
        else:
            conv_piece(x_ref, taps_ref, u_ref, start_of(*piece), halo)
        piece_states(u_ref, kt_ref, table_ref, drow_ref, start_of(*piece), saved_ref, spread_ref, chip_ref)
    for copy in copies:
        copy.wait()


KEYS = vmem(BF16, 2, 2, TOK, 2 * STATE)
U = vmem(BF16, 2, 2, TOK, CW)
SAVED = vmem(BF16, 6, STATE, CW)
SPREAD = vmem(BF16, 2, 2 * HEADS, CW)
CHIP = vmem(BF16, MSG, CW)


def group(keep_ref, got_ref, outs):
    c, z, y = place()
    z0 = z == 0
    dm, do = read_decay(keep_ref[2 * STATE : MSG]), read_decay(got_ref[2 * STATE : MSG])
    one = jnp.ones_like(dm)
    am, ao = jnp.where(z0, do, one), jnp.where(z0, one, dm)
    fwd = (am * keep_ref[0:STATE].astype(F32) + ao * got_ref[0:STATE].astype(F32)).astype(BF16)
    am, ao = jnp.where(z0, one, do), jnp.where(z0, dm, one)
    rows = slice(STATE, 2 * STATE)
    rev = (am * keep_ref[rows].astype(F32) + ao * got_ref[rows].astype(F32)).astype(BF16)
    decay = decay_rows(dm * do)
    for k in range(1, 4):
        outs[k - 1][0:STATE] = jnp.where(y + k < 4, fwd, rev)
        outs[k - 1][STATE:YMSG] = decay


def entries(keep_ref, got_ref, r1_ref, r2_ref, r3_ref, mine_ref, back_ref):
    c, z, y = place()
    z0 = z == 0
    r = [ref[0:STATE].astype(F32) for ref in (r1_ref, r2_ref, r3_ref)]
    d = [read_decay(ref[STATE:YMSG]) for ref in (r1_ref, r2_ref, r3_ref)]
    zero = jnp.zeros_like(r[0])
    ef = jnp.where(y >= 3, r[2], zero)
    ef = jnp.where(y >= 2, r[1] + d[1] * ef, zero)
    ef = jnp.where(y >= 1, r[0] + d[0] * ef, zero)
    er = jnp.where(y <= 0, r[0], zero)
    er = jnp.where(y <= 1, r[1] + d[1] * er, zero)
    er = jnp.where(y <= 2, r[2] + d[2] * er, zero)
    dm, do = read_decay(keep_ref[2 * STATE : MSG]), read_decay(got_ref[2 * STATE : MSG])
    df = jnp.where(z0, dm, do)
    tf = jnp.where(z0, keep_ref[0:STATE].astype(F32), got_ref[0:STATE].astype(F32))
    second_f = df * ef + tf
    dr = jnp.where(z0, do, dm)
    rows = slice(STATE, 2 * STATE)
    tr = jnp.where(z0, got_ref[rows].astype(F32), keep_ref[rows].astype(F32))
    first_r = dr * er + tr
    mine_ref[0] = jnp.where(z0, ef, second_f).astype(BF16)
    mine_ref[1] = jnp.where(z0, first_r, er).astype(BF16)
    back_ref[0] = jnp.where(z0, second_f, ef).astype(BF16)
    back_ref[1] = jnp.where(z0, er, first_r).astype(BF16)


def group_kernel(keep_ref, got_ref, *refs):
    group(keep_ref, got_ref, refs[-3:])


def entries_kernel(keep_ref, got_ref, r1_ref, r2_ref, r3_ref, *refs):
    entries(keep_ref, got_ref, r1_ref, r2_ref, r3_ref, *refs[-2:])


def within_kernel(k, p, u_ref, spread_ref, kq_ref, table_ref, mcol_ref, mrow_ref, drow_ref, after_ref, *refs):
    make_qk = len(refs) == 2 and refs[1].shape[0] == 2 and len(refs[1].shape) == 5
    qk_ref, out_ref = (refs[1], refs[0]) if make_qk else refs
    row = lax.broadcasted_iota(jnp.int32, (SUB, SUB), 0)
    col = lax.broadcasted_iota(jnp.int32, (SUB, SUB), 1)
    low = lax.broadcasted_iota(jnp.int32, (SUB, 2 * HEAD_DIM), 1) < HEAD_DIM

    def block(b, _):
        if make_qk:
            for s in range(2):
                rows = slice(s * SUB, (s + 1) * SUB)
                for d in range(2):
                    keys = kq_ref[b, d, rows, 0:STATE]
                    queries = kq_ref[b, d, rows, STATE : 2 * STATE]
                    prod = lax.dot_general(queries, keys, (((1,), (1,)), ((), ())), preferred_element_type=F32)
                    qk_ref[b, d, s] = jnp.where((row >= col) if d == 0 else (row <= col), prod, 0.0)
        start = b * HALF + start_of(k, p)
        first = start // HEAD_DIM
        spread = spread_ref[b]
        mcol = pltpu.roll(mcol_ref[...], 2 * HEADS - first, 1)
        mrow = mrow_ref[pl.ds(pl.multiple_of(first, HC), HC), :]
        wv, gt, drow = expand(table_ref, drow_ref, WV, spread)
        skip = drow[10:11]
        for s in range(2):
            rows = slice(s * SUB, (s + 1) * SUB)
            for two in range(HC // 2):
                cols = slice(two * 128, (two + 1) * 128)
                up = u_ref[b, 0, rows, cols].astype(F32)
                xf = (up * wv[rows, cols]).astype(BF16)
                xb = (u_ref[b, 1, rows, cols].astype(F32) * wv[rows, cols]).astype(BF16)
                none = jnp.zeros_like(xf)
                left, right = [], []
                for h in range(2):
                    at = two * 2 + h
                    diff = mcol[rows, at : at + 1] - mrow[at : at + 1, rows]
                    decay = jnp.exp2(-jnp.abs(diff))
                    left += [(decay * qk_ref[b, 0, s]).astype(BF16), (decay * qk_ref[b, 1, s]).astype(BF16)]
                    keep = low if h == 0 else ~low
                    right += [jnp.where(keep, xf, none), jnp.where(keep, xb, none)]
                res = dot(jnp.concatenate(left, axis=1), jnp.concatenate(right, axis=0))
                out_ref[b, rows, cols] = (res * gt[rows, cols] + up * skip[:, cols]).astype(BF16)
        return _

    lax.fori_loop(0, 2, block, 0)


QK = vmem(F32, 2, 2, 2, SUB, SUB)


def make_within(k, p, u, spread, kq, table, mcol, mrow, drow, after, qk=None):
    outs = [vmem(BF16, 2, TOK, CW)]
    operands = (u, spread, kq, table, mcol, mrow, drow, after)
    kernel = functools.partial(within_kernel, k, p)
    if qk is None:
        return call(kernel, f"within_{k}{p}", [*outs, QK], operands)
    return call(kernel, f"within_{k}{p}", outs, (*operands, qk))[0]


def finish_part(k, p, other, entry_ref, saved_ref, spread_ref, within_ref, gate_ref, kq_ref, table_ref, drow_ref, put, square):
    c, z, y = place()
    b = 1 - c if other else c
    start = start_of(k, p)
    at = columns(start, CW)
    spread = spread_ref[b]
    gf, gr, drow = expand(table_ref, drow_ref, GF, spread)
    d0, d1 = drow[8:9], drow[9:10]
    far = dot(drow_ref[...], spread_ref[1 - b])
    far = far[0:1] + far[1:2]
    one = jnp.ones_like(far)
    none = jnp.zeros((STATE, CW), F32)
    first = b == 0
    ef = jnp.where(first, one, far) * entry_ref[0].astype(F32) + jnp.where(first, none, saved_ref[4].astype(F32))
    er = jnp.where(first, far, one) * entry_ref[1].astype(F32) + jnp.where(first, saved_ref[5].astype(F32), none)
    inside = [
        (ef.astype(BF16), (er * d1 + saved_ref[2 * b + 1].astype(F32)).astype(BF16)),
        ((ef * d0 + saved_ref[2 * b].astype(F32)).astype(BF16), er.astype(BF16)),
    ]
    for s in range(2):
        rows = slice(s * SUB, (s + 1) * SUB)
        cf = dot(kq_ref[b, 0, rows, STATE : 2 * STATE], inside[s][0])
        cr = dot(kq_ref[b, 1, rows, STATE : 2 * STATE], inside[s][1])
        mixed = within_ref[b, rows].astype(F32) + gf[rows] * cf + gr[rows] * cr
        half = gate_ref[rows, at].astype(F32) * 0.5
        gated = mixed * (half + half * jnp.tanh(half))
        put(rows, gated)
        sq = gated * gated
        for j in range(0, CW, 128):
            part = sq[:, j : j + 128]
            square[s] = part if square[s] is None else square[s] + part


def halves(refs):
    return refs if len(refs) == 2 else (refs[0].at[0:SUB], refs[0].at[SUB:TOK])


def finish_piece(k, p, entry_ref, saved_ref, spread_ref, within_ref, gates, shared, own_ref, msg_refs, squares):
    def put_own(rows, gated):
        own_ref[rows] = gated

    def put_other(rows, gated):
        msg_refs[rows.start // SUB][:, 0:CW] = gated.astype(BF16)

    for other, put in ((1, put_other), (0, put_own)):
        finish_part(k, p, other, entry_ref, saved_ref, spread_ref, within_ref, gates[other], *shared, put, squares[other])


NEAR = ((3, 0), (3, 1), (2, 0))
BACK = (2, 1)


def finish_near_kernel(k, p, entry_ref, saved_ref, spread_ref, within_ref, gate_ref, gate_other_ref, *refs):
    shared, (square_in, own_ref, *msg_refs, square_ref) = refs[:3], refs[3:]
    msg_refs = halves(msg_refs)
    squares = [[None, None], [None, None]]
    gates = (gate_ref, gate_other_ref)
    finish_piece(k, p, entry_ref, saved_ref, spread_ref, within_ref, gates, shared, own_ref, msg_refs, squares)
    for other in range(2):
        for s in range(2):
            rows = slice(s * SUB, (s + 1) * SUB)
            if (k, p) == NEAR[0]:
                square_ref[other, rows] = squares[other][s]
            else:
                square_ref[other, rows] = square_in[other, rows] + squares[other][s]


def finish_other_kernel(entry_ref, saved_ref, spread_ref, within_ref, gate_ref, *refs):
    shared, square_in, msg_refs = refs[:3], refs[3], halves(refs[-1:])
    square = [square_in[1, s * SUB : (s + 1) * SUB] for s in range(2)]

    def put(rows, gated):
        msg_refs[rows.start // SUB][:, 0:CW] = gated.astype(BF16)

    finish_part(*BACK, 1, entry_ref, saved_ref, spread_ref, within_ref, gate_ref, *shared, put, square)
    lane = lax.broadcasted_iota(jnp.int32, (SUB, 128), 1)
    for s in range(2):
        total = jnp.sum(square[s], axis=1, keepdims=True)
        hi = total.astype(BF16).astype(F32)
        sums = jnp.where(lane == 0, hi, jnp.where(lane == 1, total - hi, 0.0))
        msg_refs[s][:, CW : CW + 128] = sums.astype(BF16)


def finish_own_kernel(entry_ref, saved_ref, spread_ref, within_ref, gate_ref, *refs):
    shared, (square_in, after_ref, own_ref, square_ref) = refs[:3], refs[3:]
    square = [square_in[0, s * SUB : (s + 1) * SUB] for s in range(2)]

    def put(rows, gated):
        own_ref[rows] = gated

    finish_part(*BACK, 0, entry_ref, saved_ref, spread_ref, within_ref, gate_ref, *shared, put, square)
    for s in range(2):
        square_ref[s * SUB : (s + 1) * SUB] = square[s]


def norm_kernel(*refs):
    own_refs, other_refs, (square_ref, gain_ref, out_hbm, out_ref, sems) = refs[:4], refs[4:8], refs[8:]
    other_refs = [halves([ref]) for ref in other_refs]
    c, z, y = place()
    pieces = []
    for n, piece in enumerate((*NEAR, BACK)):
        pieces.append(((own_refs[n], own_refs[n].at[SUB:TOK]), c * HALF + start_of(*piece)))
        pieces.append((other_refs[n], (1 - c) * HALF + start_of(*piece)))
    step = 32
    copies = []
    for r in range(0, TOK, step):
        rows, inside = slice(r, r + step), slice(r % SUB, r % SUB + step)
        total = square_ref[rows] + other_refs[3][r // SUB][inside, CW : CW + 128].astype(F32)
        scale = lax.rsqrt(jnp.sum(total, axis=1, keepdims=True) * (1.0 / INNER) + 1e-05)
        for refs, start in pieces:
            at = columns(start, CW)
            out_ref[rows, at] = (refs[r // SUB][inside, 0:CW].astype(F32) * scale * gain_ref[:, at]).astype(BF16)
        copies.append(pltpu.make_async_copy(out_ref.at[rows], out_hbm.at[rows], sems.at[len(copies)]))
        copies[-1].start()
    for copy in copies:
        copy.wait()


def per_device(mixer_input, gate_input, conv_forward, conv_reverse, step_size, decay_rate, skip_scale, norm_gain):
    n = lax.axis_size("seq")

    def send(v, perm):
        return lax.ppermute(v, "seq", perm)

    core = [(i, i ^ 1) for i in range(n)]
    zswap = [(i, i ^ 2) for i in range(n)]
    chips = [(i, i + 1) for i in range(1, n - 1, 2)] + [(i + 1, i) for i in range(1, n - 1, 2)]

    def along_y(msgs):
        return [send(m, [(i, (i + 4 * k) % n) for i in range(n)]) for k, m in enumerate(msgs, 1)]

    to_core, to_chip = call(
        edge_kernel,
        "edges",
        [vmem(BF16, TOK, WIDE + STEPS), vmem(BF16, HALO, E)],
        (),
        (mixer_input, step_size),
        [pltpu.VMEM((HEADS, TOK), F32), pltpu.SemaphoreType.DMA((4,))],
    )
    x, table, mcol, mrow, drow, taps, kq, u2a = call(
        front_kernel,
        "front",
        [
            vmem(BF16, 2, TOK, WIDE),
            vmem(BF16, 6, TOK, 2 * HEADS),
            vmem(F32, TOK, 2 * HEADS),
            vmem(F32, HEADS, TOK),
            vmem(BF16, 16, 2 * HEADS),
            vmem(F32, 8, WIDE),
            KEYS,
            U,
        ],
        (send(to_core, core),),
        (
            mixer_input,
            step_size,
            decay_rate.reshape(1, HEADS),
            skip_scale.reshape(1, HEADS),
            conv_forward,
            conv_reverse,
        ),
        [
            pltpu.VMEM((HEADS, TOK), F32),
            pltpu.VMEM((1, HEADS), F32),
            pltpu.VMEM((1, HEADS), F32),
            pltpu.VMEM((4, WIDE), F32),
            pltpu.VMEM((4, WIDE), F32),
            pltpu.SemaphoreType.DMA((10,)),
        ],
    )
    chip_halo, to_core = call(
        halo_kernel, "halo", [vmem(BF16, HALO, WIDE)] * 2, (send(to_chip, chips), kq)
    )
    halo = (x, taps, chip_halo, send(to_core, core))
    (u2b,) = call(conv_kernel, "conv_21", [U], (x, taps))
    kq, u2a, kt, saved2a, spread2a, zsend0, gate_to_core = call(
        first_states_kernel,
        "states_first",
        [KEYS, U, vmem(BF16, 2, 2, STATE, TOK), SAVED, SPREAD, CHIP, vmem(BF16, TOK, HALF)],
        (kq, u2a, *halo, table, drow, u2b),
        (gate_input,),
        [pltpu.SemaphoreType.DMA(())],
        aliases={0: 0, 1: 1},
    )
    got0 = send(zsend0, zswap)

    def make_rest(name, todo, after):
        kernel = functools.partial(rest_kernel, todo)
        outs = [U, SAVED, SPREAD, CHIP]
        operands = (*halo, table, drow, kt, after)
        if todo == ((2, 1),):
            return call(kernel, name, outs, (*operands, u2b), aliases={8: 0})
        if todo == ((3, 1),):
            outs += [vmem(BF16, TOK, HALF), vmem(F32, 1, INNER)]
            params = (gate_input, norm_gain.reshape(1, INNER))
            return call(kernel, name, outs, operands, params, [pltpu.SemaphoreType.DMA((2,))])
        return call(kernel, name, outs, operands)

    u3a, saved3a, spread3a, keep0 = make_rest("states_30", ((3, 0),), zsend0)
    u2b, saved2b, spread2b, zsend1 = make_rest("states_21", ((2, 1),), keep0)
    got1 = send(zsend1, zswap)
    u3b, saved3b, spread3b, keep1, gate, gain = make_rest("states_31", ((3, 1),), zsend1)
    gates = (gate, send(gate_to_core, core))
    tables = (kq, table, mcol, mrow, drow)
    yout = [vmem(BF16, YMSG, CW)] * 3
    entry = vmem(BF16, 2, STATE, CW)

    w2a, qk = make_within(2, 0, u2a, spread2a, *tables, keep1)
    msgs = call(group_kernel, "group_a", yout, (keep0, got0, w2a, gates[1]))
    arrived0 = along_y(msgs)
    w2b = make_within(2, 1, u2b, spread2b, *tables, msgs[0], qk)
    msgs = call(group_kernel, "group_b", yout, (keep1, got1, w2b))
    arrived1 = along_y(msgs)
    mine0, back0 = call(entries_kernel, "entries_a", [entry, entry], (keep0, got0, *arrived0, msgs[0]))
    back0 = send(back0, zswap)
    w3a = make_within(3, 0, u3a, spread3a, *tables, mine0, qk)
    mine1, back1 = call(entries_kernel, "entries_b", [entry, entry], (keep1, got1, *arrived1, w3a))
    back1 = send(back1, zswap)
    w3b = make_within(3, 1, u3b, spread3b, *tables, mine1, qk)
    shared = (kq, table, drow)
    square = kt
    own, other = [], []
    parts = (
        (mine0, saved3a, spread3a, w3a),
        (mine1, saved3b, spread3b, w3b),
        (back0, saved2a, spread2a, w2a),
    )
    message = [vmem(BF16, TOK, CW)]
    for (k, p), part in zip(NEAR, parts):
        gated, *msg, square = call(
            functools.partial(finish_near_kernel, k, p),
            f"finish_{k}{p}",
            [vmem(F32, TOK, CW), *message, vmem(F32, 2, TOK, 128)],
            (*part, *gates, *shared, square),
        )
        own.append(gated)
        other += [send(m, core) for m in msg]
    msg = call(
        finish_other_kernel,
        "finish_other",
        [vmem(BF16, TOK, CW + 128)],
        (back1, saved2b, spread2b, w2b, *gates[1:], *shared, square, *other[:2]),
    )
    other += [send(m, core) for m in msg]
    gated, square = call(
        finish_own_kernel,
        "finish_own",
        [vmem(F32, TOK, CW), vmem(F32, TOK, 128)],
        (back1, saved2b, spread2b, w2b, gates[0], *shared, square, msg[0]),
    )
    own.append(gated)
    (out,) = call(
        norm_kernel,
        "norm",
        [shape(BF16, TOK, INNER)],
        (*own, *other, square, gain),
        (),
        [pltpu.VMEM((TOK, INNER), BF16), pltpu.SemaphoreType.DMA((8,))],
    )
    return out


def solution(mesh):
    in_specs = (
        P(("row", "seq"), None),
        P(("row", "seq"), None),
        P(),
        P(),
        P(None, ("row", "seq")),
        P("row"),
        P(),
        P(),
    )
    out_specs = P(("row", "seq"), None)
    return jax.shard_map(per_device, mesh=mesh, in_specs=in_specs, out_specs=out_specs, check_vma=False)
```
